32 devices in a mesh: parts: 2 (over y), set: 4 (over x, core), seq: 4 (over z).
Axes of the slice: x: 2, y: 2, z: 4, core: 2. Of those that a mesh axis runs over, the one named last changes fastest.
Arguments:
- span_hidden: bfloat16 [512, 8192], P('parts', 'seq'), parts along dimension 0, may hold values from -500 to 500
- norm_gain: bfloat16 [8192], P('seq'), may hold values from 0.099609375 to 1.8984375
- key_value_weight: bfloat16 [8192, 2048], P('seq', 'set'), may hold values from -0.0625 to 0.0625
- prompt_key_value: bfloat16 [256, 2048], P(('parts', 'seq')), parts along dimension 0, may hold values from -6 to 6
- span_offset: int32 [2], P('parts'), parts along dimension 0, may hold values from 64 to 128
- cont_query: bfloat16 [32, 64, 8192], P(('parts', 'set', 'seq')), parts along dimension 0, may hold values from -24 to 24
- continuation_key_value: bfloat16 [32, 64, 2048], P(('parts', 'set', 'seq')), parts along dimension 0, may hold values from -6 to 6
- cont_lengths: int32 [32], P(('parts', 'set', 'seq')), parts along dimension 0, may hold values from 1 to 64
Outputs:
- span_key_value: bfloat16 [512, 2048], P(('parts', 'seq'), 'set'), parts along dimension 0
- attended: bfloat16 [32, 64, 8192], P(('parts', 'set', 'seq')), parts along dimension 0
The draws below stay inside these ranges and needn't reach their ends.
There are 2 independent parts, one for each index of `parts`. The reference program is written for one: setup_inputs(seed, part) draws one part's arguments, and reference() takes and returns one part's arrays. A program takes and returns all parts, laid end to end along the dimension named above; an argument that names none is the same for every part. Nothing has to cross between parts.
All inputs are finite; a program needn't handle non-finite values.
Results may differ from the reference program's by a relative error of at most 0.02.
Values may be sent and summed in bfloat16 or wider, within the bound.
No kernel may reach another device: no remote copies, remote signals or barrier semaphores. Data moves between devices by JAX's collectives and lax.ppermute only.
A program may use at most 64 MiB of HBM per device.

```python
import math
import jax
import jax.numpy as jnp
from jax import lax

MODEL_WIDTH = 8192
QUERY_HEADS = 64
KEY_HEADS = 8
HEAD_SIZE = 128
SPAN_LENGTH = 256
CONTINUE_LENGTH = 64
PROMPT_LENGTH = 128
CONTINUATION_SET = 16


def draw_span_hidden(key, part):
    first, second = jax.random.split(jax.random.fold_in(key, 11), 2)
    columns = jnp.arange(MODEL_WIDTH).astype(jnp.float32) / MODEL_WIDTH
    ramp = 0.6 * 3.0 ** columns
    rough = jax.random.uniform(second, (MODEL_WIDTH,), jnp.float32, 0.5, 1.5)
    base = jnp.clip(jax.random.normal(first, (SPAN_LENGTH, MODEL_WIDTH), jnp.float32), -6.0, 6.0)
    result = base * (ramp * rough)[None, :]
    return result.astype(jnp.bfloat16)


def continuation_pair(key):
    query_key, kv_key = jax.random.split(jax.random.fold_in(key, 23), 2)
    key_value_shape = (CONTINUATION_SET, CONTINUE_LENGTH, 2 * KEY_HEADS * HEAD_SIZE)
    query_shape = (CONTINUATION_SET, CONTINUE_LENGTH, QUERY_HEADS * HEAD_SIZE)
    key_value_sample = jnp.clip(jax.random.normal(kv_key, key_value_shape, jnp.float32), -6.0, 6.0)
    query_draw = jnp.clip(jax.random.normal(query_key, query_shape, jnp.float32), -6.0, 6.0)
    return (query_draw, key_value_sample)


def draw_cont_query(key, part):
    return continuation_pair(key)[0].astype(jnp.bfloat16)


def draw_continuation_key_value(key, part):
    return continuation_pair(key)[1].astype(jnp.bfloat16)


def place_ends(drawn, stream_key, least, high):
    spot = [jax.random.randint(jax.random.fold_in(stream_key, axis), (), 0, length) for axis, length in enumerate(drawn.shape)]
    main_axis = drawn.shape.index(max(drawn.shape))
    next_to = spot[:main_axis] + [(spot[main_axis] + 1) % drawn.shape[main_axis]] + spot[main_axis + 1:]
    return drawn.at[tuple(spot)].set(least).at[tuple(next_to)].set(high)


def block_scale(stream_key, dims, cuts, least, largest):
    def one(position, blocks):
        draws = jax.random.uniform(jax.random.fold_in(jax.random.fold_in(stream_key, 6), position), (blocks,), jnp.float32, least / len(cuts), largest / len(cuts))
        return jnp.repeat(jnp.exp(draws), dims[position] // blocks).reshape((-1,) + (1,) * (len(dims) - position - 1))

    loudness = one(*cuts[0])
    for cut in cuts[1:]:
        loudness = loudness * one(*cut)
    return loudness


def bell_draw(stream_key, shape, spread, most, pieces=(), kind=jnp.bfloat16):
    loudness = block_scale(stream_key, shape, pieces, -0.22, 0.18) if pieces else 1.0
    entries = jax.random.normal(stream_key, shape, jnp.float32) * spread * loudness
    return jnp.minimum(jnp.maximum(entries, -most), most).astype(kind)


def setup_inputs(seed: int = 0, part: int = 0) -> dict:
    streams_of = jax.random.split(jax.random.key(seed), 9)
    own_keys = jax.random.split(jax.random.fold_in(streams_of[8], part), 9)
    span_hidden = draw_span_hidden(jax.random.fold_in(jax.random.fold_in(streams_of[8], part), 71), part)
    norm_gain = jnp.clip(1.0 + 0.18 * jax.random.normal(streams_of[1], (MODEL_WIDTH,), jnp.float32), 0.099609375, 1.8984375).astype(jnp.bfloat16)
    key_value_weight = bell_draw(streams_of[2], (MODEL_WIDTH, 2 * KEY_HEADS * HEAD_SIZE), MODEL_WIDTH ** -0.5, 0.0625, ((0, 4), (1, 4)))
    prompt_key_value = bell_draw(own_keys[3], (PROMPT_LENGTH, 2 * KEY_HEADS * HEAD_SIZE), 1.0, 6.0, ((0, 4),))
    span_offset = jax.random.randint(own_keys[4], (1,), PROMPT_LENGTH // 2, PROMPT_LENGTH + 1).astype(jnp.int32)
    cont_query = draw_cont_query(jax.random.fold_in(jax.random.fold_in(streams_of[8], part), 71), part)
    continuation_key_value = draw_continuation_key_value(jax.random.fold_in(jax.random.fold_in(streams_of[8], part), 71), part)
    cont_lengths = place_ends(jax.random.randint(own_keys[7], (CONTINUATION_SET,), 1, CONTINUE_LENGTH + 1), jax.random.fold_in(own_keys[7], 1), 1, CONTINUE_LENGTH).astype(jnp.int32)
    return dict(span_hidden=span_hidden, norm_gain=norm_gain, key_value_weight=key_value_weight, prompt_key_value=prompt_key_value, span_offset=span_offset, cont_query=cont_query, continuation_key_value=continuation_key_value, cont_lengths=cont_lengths)


EPS = 1e-05
NEGATIVE_LARGE = -1e+30

def frequencies(count, width, dtype):
    base = 500000.0 ** (-(jnp.arange(count).astype(dtype) * 2.0) / width)
    wave = 2.0 * math.pi / base
    smooth = (8192.0 / wave - 1.0) / 3.0
    blended = (1.0 - smooth) * base / 8.0 + smooth * base
    return jnp.where(wave < 2048.0, base, jnp.where(wave > 8192.0, base / 8.0, blended))

def apply_rotary(value_matrix, positions):
    mid_point = value_matrix.shape[-1] // 2
    frequency = frequencies(mid_point, value_matrix.shape[-1], value_matrix.dtype)
    angles = positions.astype(value_matrix.dtype)[:, None] * frequency[None, :]
    cosine = jnp.concatenate([jnp.cos(angles), jnp.cos(angles)], -1)[:, None, :]
    sine_part = jnp.concatenate([jnp.sin(angles), jnp.sin(angles)], -1)[:, None, :]
    turned = jnp.concatenate([-value_matrix[..., mid_point:], value_matrix[..., :mid_point]], -1)
    return value_matrix * cosine + turned * sine_part

def reference(span_hidden, norm_gain, key_value_weight, prompt_key_value, span_offset, cont_query, continuation_key_value, cont_lengths):
    key_columns_width = KEY_HEADS * HEAD_SIZE
    group_factor = QUERY_HEADS // KEY_HEADS
    hidden = span_hidden.astype(jnp.float32)
    mean_square = lax.optimization_barrier(jnp.sum(hidden * hidden, axis=1)) / MODEL_WIDTH
    normed = (hidden * lax.rsqrt(mean_square + EPS)[:, None] * norm_gain.astype(jnp.float32)[None, :]).astype(jnp.bfloat16)
    projected_rows = jnp.dot(normed, key_value_weight, preferred_element_type=jnp.float32)
    offset = span_offset[0]
    span_positions = offset + jnp.arange(SPAN_LENGTH, dtype=jnp.int32)
    rotary_applied = apply_rotary(projected_rows[:, :key_columns_width].reshape(SPAN_LENGTH, KEY_HEADS, HEAD_SIZE), span_positions).reshape(SPAN_LENGTH, key_columns_width)
    span_key_value = jnp.concatenate([rotary_applied, projected_rows[:, key_columns_width:]], 1).astype(jnp.bfloat16)
    prior_key_rows = jnp.concatenate([prompt_key_value[:, :key_columns_width], span_key_value[:, :key_columns_width]], 0).reshape(PROMPT_LENGTH + SPAN_LENGTH, KEY_HEADS, HEAD_SIZE)
    prior_value_rows = jnp.concatenate([prompt_key_value[:, key_columns_width:], span_key_value[:, key_columns_width:]], 0).reshape(PROMPT_LENGTH + SPAN_LENGTH, KEY_HEADS, HEAD_SIZE)
    past_valid = jnp.concatenate([jnp.arange(PROMPT_LENGTH, dtype=jnp.int32) < offset, jnp.ones((SPAN_LENGTH,), bool)])
    self_positions = offset + SPAN_LENGTH + jnp.arange(CONTINUE_LENGTH, dtype=jnp.int32)
    token_index = jnp.arange(CONTINUE_LENGTH, dtype=jnp.int32)
    causal = token_index[:, None] >= token_index[None, :]
    valid = jnp.concatenate([jnp.broadcast_to(past_valid[None, :], (CONTINUE_LENGTH, PROMPT_LENGTH + SPAN_LENGTH)), causal], 1)
    valid_four = valid[:, None, None, :]

    def score_one(item):
        query_raw, key_value_plain, sequence_length = item
        query_rows = apply_rotary(query_raw.astype(jnp.float32).reshape(CONTINUE_LENGTH, QUERY_HEADS, HEAD_SIZE), self_positions).astype(jnp.bfloat16)
        query_rows = query_rows.reshape(CONTINUE_LENGTH, KEY_HEADS, group_factor, HEAD_SIZE)
        self_key_rows = apply_rotary(key_value_plain[:, :key_columns_width].astype(jnp.float32).reshape(CONTINUE_LENGTH, KEY_HEADS, HEAD_SIZE), self_positions).astype(jnp.bfloat16)
        self_value_rows = key_value_plain[:, key_columns_width:].reshape(CONTINUE_LENGTH, KEY_HEADS, HEAD_SIZE)
        key_matrix = jnp.concatenate([prior_key_rows, self_key_rows], 0).astype(jnp.float32)
        vals = jnp.concatenate([prior_value_rows, self_value_rows], 0).astype(jnp.float32)
        scores = jnp.einsum('tgkd,ngd->tgkn', query_rows.astype(jnp.float32), key_matrix) * HEAD_SIZE ** (-0.5)
        masked = jnp.where(valid_four, scores, NEGATIVE_LARGE)
        top = lax.optimization_barrier(jnp.max(masked, axis=-1))
        weights = jnp.where(valid_four, jnp.exp(masked - top[..., None]), 0.0)
        total = lax.optimization_barrier(jnp.sum(weights, axis=-1))
        rounded = weights.astype(jnp.bfloat16).astype(jnp.float32)
        mixed = jnp.einsum('tgkn,ngd->tgkd', rounded, vals) / total[..., None]
        mixed = mixed.reshape(CONTINUE_LENGTH, QUERY_HEADS * HEAD_SIZE)
        live = token_index < sequence_length
        return jnp.where(live[:, None], mixed, 0.0).astype(jnp.bfloat16)
    attended = lax.map(score_one, (cont_query, continuation_key_value, cont_lengths))
    return (span_key_value, attended)
```

```python
import functools
import math

import jax
import jax.numpy as jnp
from jax import lax
from jax.experimental import pallas as pl
from jax.experimental.pallas import tpu as pltpu
from jax.sharding import PartitionSpec as P

MODEL_WIDTH = 8192
QUERY_HEADS = 64
KEY_HEADS = 8
HEAD_SIZE = 128
SPAN_LENGTH = 256
EPS = 1e-05
NEGATIVE_LARGE = -1e30
GROUP = QUERY_HEADS // KEY_HEADS
KEY_COLUMNS = KEY_HEADS * HEAD_SIZE
BF16 = jnp.bfloat16
F32 = jnp.float32
VMEM = pl.BlockSpec(memory_space=pltpu.VMEM)
SMEM = pl.BlockSpec(memory_space=pltpu.SMEM)


def peer(index, step, count):
    if count & (count - 1) == 0:
        return index ^ step
    return (index + step) % count


def source(index, step, count):
    if count & (count - 1) == 0:
        return index ^ step
    return (index + count - step) % count


def exchange(value, axis, step):
    count = lax.axis_size(axis)
    return lax.ppermute(value, axis, [(i, peer(i, step, count)) for i in range(count)])


def frequencies():
    base = 500000.0 ** (-(jnp.arange(HEAD_SIZE // 2).astype(F32) * 2.0) / HEAD_SIZE)
    wave = 2.0 * math.pi / base
    smooth = (8192.0 / wave - 1.0) / 3.0
    blended = (1.0 - smooth) * base / 8.0 + smooth * base
    return jnp.where(wave < 2048.0, base, jnp.where(wave > 8192.0, base / 8.0, blended))


def tables(positions):
    angles = positions.astype(F32)[:, None] * frequencies()[None, :]
    cosine, sine = jnp.cos(angles), jnp.sin(angles)
    return jnp.concatenate([cosine, cosine], -1), jnp.concatenate([-sine, sine], -1)


def turn(value, cosine, sine):
    return value * cosine + pltpu.roll(value, HEAD_SIZE // 2, 1) * sine


def diagonal(rows):
    shape = (rows, HEAD_SIZE)
    return lax.broadcasted_iota(jnp.int32, shape, 0) == lax.broadcasted_iota(jnp.int32, shape, 1)


def project_kernel(count, rows, heads, at_ref, hidden_ref, gain_ref, weight_ref, *rest):
    own_ref, square_ref = rest[:2]
    sends, (total, squares) = rest[2 : 1 + count], rest[1 + count :]
    step = pl.program_id(0)
    hidden = hidden_ref[...].astype(F32)
    scaled = (hidden * gain_ref[...].astype(F32)).astype(BF16)
    part = jnp.dot(scaled, weight_ref[...], preferred_element_type=F32)
    square = hidden * hidden
    folded = square[:, :HEAD_SIZE]
    for lane in range(1, square.shape[1] // HEAD_SIZE):
        folded = folded + square[:, lane * HEAD_SIZE : (lane + 1) * HEAD_SIZE]

    @pl.when(step == 0)
    def _():
        total[...] = part
        squares[...] = folded

    @pl.when(step > 0)
    def _():
        total[...] += part
        squares[...] += folded

    @pl.when(step == pl.num_programs(0) - 1)
    def _():
        me = at_ref[0]
        for k in range(count):
            to = pl.ds(pl.multiple_of(peer(me, k, count) * rows, rows), rows)
            column = jnp.sum(squares[to, :], axis=1, keepdims=True)
            if k == 0:
                square_ref[...] = jnp.broadcast_to(column, (rows, HEAD_SIZE))
                out = own_ref
            else:
                out = sends[k - 1]
                line = jnp.sum(jnp.where(diagonal(rows), column, 0.0), axis=0, keepdims=True)
                high = line.astype(BF16).astype(F32)
                low = line - high
                which = lax.broadcasted_iota(jnp.int32, (16, HEAD_SIZE), 0)
                tail = jnp.where(which == 0, high, jnp.where(which == 1, low, 0.0))
                out[heads * rows :, :] = tail.astype(BF16)
            for h in range(heads):
                piece = total[to, h * HEAD_SIZE : (h + 1) * HEAD_SIZE]
                out[h * rows : (h + 1) * rows, :] = piece.astype(out.dtype)


def project(at, span_hidden, norm_gain, key_value_weight, count):
    length, depth = span_hidden.shape
    width = key_value_weight.shape[1]
    rows, heads = length // count, width // HEAD_SIZE
    steps = 4 if depth % 512 == 0 else 1
    chunk = depth // steps
    whole = lambda i: (0, 0)
    outs = [
        jax.ShapeDtypeStruct((heads * rows, HEAD_SIZE), F32),
        jax.ShapeDtypeStruct((rows, HEAD_SIZE), F32),
    ] + [jax.ShapeDtypeStruct((heads * rows + 16, HEAD_SIZE), BF16)] * (count - 1)
    return pl.pallas_call(
        functools.partial(project_kernel, count, rows, heads),
        grid=(steps,),
        in_specs=[
            SMEM,
            pl.BlockSpec((length, chunk), lambda i: (0, i)),
            pl.BlockSpec((1, chunk), lambda i: (0, i)),
            pl.BlockSpec((chunk, width), lambda i: (i, 0)),
        ],
        out_shape=outs,
        out_specs=[pl.BlockSpec(o.shape, whole) for o in outs],
        scratch_shapes=[pltpu.VMEM((length, width), F32), pltpu.VMEM((length, HEAD_SIZE), F32)],
        compiler_params=pltpu.CompilerParams(vmem_limit_bytes=24 << 20),
        cost_estimate=pl.CostEstimate(
            flops=2 * length * depth * width, bytes_accessed=2 * depth * (length + width), transcendentals=0
        ),
        name="project",
    )(at, span_hidden, norm_gain[None, :], key_value_weight)


def combine_kernel(rows, heads, first_ref, own_ref, square_ref, cosine_ref, sine_ref, *rest):
    got, out_ref = rest[:-1], rest[-1]
    line = jnp.zeros((1, HEAD_SIZE), F32)
    for ref in got:
        tail = ref[heads * rows :, :].astype(F32)
        line = line + tail[0:1, :] + tail[1:2, :]
    column = jnp.sum(jnp.where(diagonal(rows), line, 0.0), axis=1, keepdims=True)
    scale = lax.rsqrt((square_ref[...] + column) / MODEL_WIDTH + EPS)
    cosine, sine = cosine_ref[...], sine_ref[...]
    for h in range(heads):
        span = slice(h * rows, (h + 1) * rows)
        value = own_ref[span, :]
        for ref in got:
            value = value + ref[span, :].astype(F32)
        value = value * scale
        is_key = first_ref[0] + h < KEY_HEADS
        out = jnp.where(is_key, turn(value, cosine, sine), value)
        out_ref[:, h * HEAD_SIZE : (h + 1) * HEAD_SIZE] = out.astype(BF16)


def combine(first, own, square, cosine, sine, got):
    rows = square.shape[0]
    heads = own.shape[0] // rows
    return pl.pallas_call(
        functools.partial(combine_kernel, rows, heads),
        in_specs=[SMEM] + [VMEM] * (4 + len(got)),
        out_shape=jax.ShapeDtypeStruct((rows, heads * HEAD_SIZE), BF16),
        out_specs=VMEM,
        name="combine",
    )(first, own, square, cosine, sine, *got)


def queries_kernel(query_ref, own_ref, cosine_ref, sine_ref, query_out, key_out):
    tokens = cosine_ref.shape[0]
    cosine, sine = cosine_ref[...], sine_ref[...]
    for h in range(KEY_HEADS):
        span = slice(h * HEAD_SIZE, (h + 1) * HEAD_SIZE)
        key_out[:, span] = turn(own_ref[:, span].astype(F32), cosine, sine).astype(BF16)
    factor = HEAD_SIZE**-0.5 * math.log2(math.e)
    cosine, sine = cosine * factor, sine * factor
    for h in range(QUERY_HEADS):
        span = slice(h * HEAD_SIZE, (h + 1) * HEAD_SIZE)
        turned = turn(query_ref[:, span].astype(F32), cosine, sine)
        query_out[h * tokens : (h + 1) * tokens, :] = turned.astype(BF16)


def queries(cont_query, own_rows, cosine, sine):
    tokens = cosine.shape[0]
    return pl.pallas_call(
        queries_kernel,
        in_specs=[VMEM] * 4,
        out_shape=[
            jax.ShapeDtypeStruct((QUERY_HEADS * tokens, HEAD_SIZE), BF16),
            jax.ShapeDtypeStruct((tokens, KEY_COLUMNS), BF16),
        ],
        out_specs=[VMEM, VMEM],
        compiler_params=pltpu.CompilerParams(vmem_limit_bytes=24 << 20),
        cost_estimate=pl.CostEstimate(flops=8 * cont_query.size, bytes_accessed=4 * cont_query.size, transcendentals=0),
        name="queries",
    )(cont_query, own_rows, cosine, sine)


def attend_kernel(sets, blocks, spots_ref, query_ref, key_ref, own_ref, prompt_refs, span_refs, out_ref, cache):
    me, offset, length = spots_ref[0], spots_ref[1], spots_ref[2]
    tokens = key_ref.shape[0]
    width = cache.shape[2]
    heads = width // HEAD_SIZE
    prompt_rows = prompt_refs[0].shape[0]
    span_rows = cache.shape[1] - prompt_rows - tokens
    for ref, (step, first) in zip(list(span_refs) + list(prompt_refs), blocks):
        cache[source(me, step, sets), first : first + ref.shape[0], :] = ref[...]
    for s in range(sets):
        columns = slice(s * width, (s + 1) * width)
        mine = key_ref if s * width < KEY_COLUMNS else own_ref
        cache[s, span_rows + prompt_rows :, :] = mine[:, columns]
    token = lax.broadcasted_iota(jnp.int32, (tokens, prompt_rows + tokens), 0)
    place = lax.broadcasted_iota(jnp.int32, (tokens, prompt_rows + tokens), 1)
    live = (place < offset) & (place < prompt_rows) | (place >= prompt_rows) & (place - prompt_rows <= token)
    bias = jnp.concatenate([jnp.where(live, 0.0, NEGATIVE_LARGE)] * GROUP, axis=0)
    keep = lax.broadcasted_iota(jnp.int32, (tokens, HEAD_SIZE), 0) < length
    for g in range(KEY_HEADS):
        lane = (g % heads) * HEAD_SIZE
        key = cache[g // heads, :, lane : lane + HEAD_SIZE]
        value = cache[sets // 2 + g // heads, :, lane : lane + HEAD_SIZE]
        query = query_ref[g * GROUP * tokens : (g + 1) * GROUP * tokens, :]
        scores = lax.dot_general(query, key, (((1,), (1,)), ((), ())), preferred_element_type=F32)
        scores = jnp.concatenate([scores[:, :span_rows], scores[:, span_rows:] + bias], axis=1)
        top = jnp.max(scores, axis=1, keepdims=True)
        weights = jnp.exp2(scores - top)
        total = jnp.sum(weights, axis=1, keepdims=True)
        mixed = jnp.dot(weights.astype(BF16), value, preferred_element_type=F32) / total
        for j in range(GROUP):
            column = (g * GROUP + j) * HEAD_SIZE
            piece = jnp.where(keep, mixed[j * tokens : (j + 1) * tokens, :], 0.0)
            out_ref[:, column : column + HEAD_SIZE] = piece.astype(BF16)


def attend(spots, query, key, own_rows, prompts, spans, sets, blocks, total_rows):
    tokens = key.shape[0]
    width = spans[0].shape[1]
    n_prompt = len(prompts)

    def kernel(spots_ref, query_ref, key_ref, own_ref, *rest):
        prompt_refs, span_refs = rest[:n_prompt], rest[n_prompt:-2]
        attend_kernel(
            sets, blocks, spots_ref, query_ref, key_ref, own_ref, prompt_refs, span_refs, rest[-2], rest[-1]
        )

    return pl.pallas_call(
        kernel,
        in_specs=[SMEM] + [VMEM] * (3 + len(prompts) + len(spans)),
        out_shape=jax.ShapeDtypeStruct((tokens, QUERY_HEADS * HEAD_SIZE), BF16),
        out_specs=VMEM,
        scratch_shapes=[pltpu.VMEM((sets, total_rows, width), BF16)],
        compiler_params=pltpu.CompilerParams(vmem_limit_bytes=40 << 20),
        cost_estimate=pl.CostEstimate(
            flops=4 * query.size * total_rows, bytes_accessed=4 * query.size, transcendentals=query.size
        ),
        name="attend",
    )(spots, query, key, own_rows, *prompts, *spans)


def on_device(
    span_hidden,
    norm_gain,
    key_value_weight,
    prompt_key_value,
    span_offset,
    cont_query,
    continuation_key_value,
    cont_lengths,
):
    offset = span_offset[0]
    sets, count = lax.axis_size("set"), lax.axis_size("seq")
    my_set, my_seq = lax.axis_index("set"), lax.axis_index("seq")
    width = key_value_weight.shape[1]
    rows = span_hidden.shape[0] // count
    tokens = cont_query.shape[1]
    low = 2 if sets % 2 == 0 else 1

    own, square, *sends = project(my_seq[None].astype(jnp.int32), span_hidden, norm_gain, key_value_weight, count)
    order = list(range(count - 1, 0, -1))
    got = [exchange(sends[k - 1], "seq", k) for k in order]

    span_cosine, span_sine = tables(offset + my_seq * rows + jnp.arange(rows, dtype=jnp.int32))
    self_cosine, self_sine = tables(offset + SPAN_LENGTH + jnp.arange(tokens, dtype=jnp.int32))
    query, key = queries(cont_query[0], continuation_key_value[0], self_cosine, self_sine)

    mine = lax.dynamic_slice_in_dim(prompt_key_value, my_set * width, width, 1)
    mine, *_ = lax.optimization_barrier((mine, own))
    parts = [mine] + [exchange(mine, "seq", k) for k in order]
    places = jnp.stack([my_seq] + [source(my_seq, k, count) for k in order])
    prompt = jnp.zeros((count,) + mine.shape, BF16)
    for part, place in zip(parts, [my_seq] + [source(my_seq, k, count) for k in order]):
        prompt = lax.dynamic_update_slice(prompt, part[None], (place, 0, 0))
    prompt = prompt.reshape(-1, width)
    prompts = [(0, prompt)]
    for step in range(low, sets, low):
        prompts.append((step, exchange(prompt, "set", step)))
    if low == 2:
        prompts += [(step ^ 1, exchange(value, "set", 1)) for step, value in prompts]

    first = (my_set * (width // HEAD_SIZE))[None].astype(jnp.int32)
    block = combine(first, own, square, span_cosine, span_sine, got)

    spans = [(0, 0, block)]
    for step in range(low, sets, low):
        spans.append((step, 0, exchange(block, "set", step)))
    across = [(k, exchange(block, "seq", k)) for k in order]
    for k, value in across:
        spans.append((0, k * rows, value))
        for step in range(low, sets, low):
            spans.append((step, k * rows, exchange(value, "set", step)))
    if low == 2:
        spans += [(step ^ 1, row, exchange(value, "set", 1)) for step, row, value in spans]

    span_total = count * rows
    blocks = [(step, row) for step, row, _ in spans] + [(step, span_total) for step, _ in prompts]
    spots = jnp.stack([my_set.astype(jnp.int32), offset, cont_lengths[0]])
    attended = attend(
        spots,
        query,
        key,
        continuation_key_value[0],
        [value for _, value in prompts],
        [value for _, _, value in spans],
        sets,
        blocks,
        span_total + prompt.shape[0] + tokens,
    )
    return block, attended[None]


def solution(mesh):
    placed = (
        P("parts", "seq"),
        P("seq"),
        P("seq", "set"),
        P(("parts", "seq"), None),
        P("parts"),
        P(("parts", "set", "seq"), None, None),
        P(("parts", "set", "seq"), None, None),
        P(("parts", "set", "seq")),
    )
    return jax.shard_map(
        on_device,
        mesh=mesh,
        in_specs=placed,
        out_specs=(P(("parts", "seq"), "set"), P(("parts", "set", "seq"), None, None)),
        check_vma=False,
    )
```

```python
import functools
import math

import jax
import jax.numpy as jnp
from jax import lax
from jax.experimental import pallas as pl
from jax.experimental.pallas import tpu as pltpu
from jax.sharding import PartitionSpec as P

MODEL_WIDTH = 8192
QUERY_HEADS = 64
KEY_HEADS = 8
HEAD_SIZE = 128
SPAN_LENGTH = 256
EPS = 1e-05
NEGATIVE_LARGE = -1e30
GROUP = QUERY_HEADS // KEY_HEADS
KEY_COLUMNS = KEY_HEADS * HEAD_SIZE
BF16 = jnp.bfloat16
F32 = jnp.float32
VMEM = pl.BlockSpec(memory_space=pltpu.VMEM)
HBM = pl.BlockSpec(memory_space=pltpu.HBM)
SMEM = pl.BlockSpec(memory_space=pltpu.SMEM)


def peer(index, step, count):
    if count & (count - 1) == 0:
        return index ^ step
    return (index + step) % count


def source(index, step, count):
    if count & (count - 1) == 0:
        return index ^ step
    return (index + count - step) % count


def exchange(value, axis, step):
    count = lax.axis_size(axis)
    return lax.ppermute(value, axis, [(i, peer(i, step, count)) for i in range(count)])


def frequencies():
    base = 500000.0 ** (-(jnp.arange(HEAD_SIZE // 2).astype(F32) * 2.0) / HEAD_SIZE)
    wave = 2.0 * math.pi / base
    smooth = (8192.0 / wave - 1.0) / 3.0
    blended = (1.0 - smooth) * base / 8.0 + smooth * base
    return jnp.where(wave < 2048.0, base, jnp.where(wave > 8192.0, base / 8.0, blended))


def tables(positions):
    angles = positions.astype(F32)[:, None] * frequencies()[None, :]
    cosine, sine = jnp.cos(angles), jnp.sin(angles)
    return jnp.concatenate([cosine, cosine], -1), jnp.concatenate([-sine, sine], -1)


def turn(value, cosine, sine):
    return value * cosine + pltpu.roll(value, HEAD_SIZE // 2, 1) * sine


def diagonal(rows):
    shape = (rows, HEAD_SIZE)
    return lax.broadcasted_iota(jnp.int32, shape, 0) == lax.broadcasted_iota(jnp.int32, shape, 1)


def project_kernel(count, rows, heads, chunks, at_ref, hidden_ref, gain_ref, weight_ref, *rest):
    own_ref, square_ref = rest[:2]
    sends = rest[2 : 1 + count]
    hidden_buf, gain_buf, weight_buf, total, squares, sems = rest[1 + count :]
    depth = hidden_ref.shape[1]
    size = depth // chunks
    gain_copy = pltpu.make_async_copy(gain_ref, gain_buf, sems.at[2 * chunks])
    gain_copy.start()
    copies = []
    for c in range(chunks):
        part = pl.ds(c * size, size)
        copies.append(
            (
                pltpu.make_async_copy(hidden_ref.at[:, part], hidden_buf.at[:, part], sems.at[2 * c]),
                pltpu.make_async_copy(weight_ref.at[part, :], weight_buf.at[part, :], sems.at[2 * c + 1]),
            )
        )
        copies[-1][0].start()
        copies[-1][1].start()
    gain_copy.wait()
    for c in range(chunks):
        copies[c][0].wait()
        folded, scaled = None, []
        for lane in range(c * size, (c + 1) * size, HEAD_SIZE):
            hidden = hidden_buf[:, lane : lane + HEAD_SIZE].astype(F32)
            tile = lane // HEAD_SIZE
            scaled.append((hidden * gain_buf[tile : tile + 1, :].astype(F32)).astype(BF16))
            square = hidden * hidden
            folded = square if folded is None else folded + square
        copies[c][1].wait()
        part = jnp.dot(
            jnp.concatenate(scaled, axis=1),
            weight_buf[c * size : (c + 1) * size, :],
            preferred_element_type=F32,
        )
        if c == 0:
            total[...] = part
            squares[...] = folded
        else:
            total[...] += part
            squares[...] += folded
    me = at_ref[0]
    for k in range(count):
        to = pl.ds(pl.multiple_of(peer(me, k, count) * rows, rows), rows)
        column = jnp.sum(squares[to, :], axis=1, keepdims=True)
        if k == 0:
            square_ref[...] = jnp.broadcast_to(column, (rows, HEAD_SIZE))
            out = own_ref
        else:
            out = sends[k - 1]
            line = jnp.sum(jnp.where(diagonal(rows), column, 0.0), axis=0, keepdims=True)
            high = line.astype(BF16).astype(F32)
            low = line - high
            which = lax.broadcasted_iota(jnp.int32, (16, HEAD_SIZE), 0)
            tail = jnp.where(which == 0, high, jnp.where(which == 1, low, 0.0))
            out[heads * rows :, :] = tail.astype(BF16)
        for h in range(heads):
            piece = total[to, h * HEAD_SIZE : (h + 1) * HEAD_SIZE]
            out[h * rows : (h + 1) * rows, :] = piece.astype(out.dtype)


def project(at, span_hidden, norm_gain, key_value_weight, count):
    length, depth = span_hidden.shape
    width = key_value_weight.shape[1]
    rows, heads = length // count, width // HEAD_SIZE
    chunks = 4 if depth % (4 * HEAD_SIZE) == 0 else 1
    gain = norm_gain.reshape(-1, HEAD_SIZE)
    outs = [
        jax.ShapeDtypeStruct((heads * rows, HEAD_SIZE), F32),
        jax.ShapeDtypeStruct((rows, HEAD_SIZE), F32),
    ] + [jax.ShapeDtypeStruct((heads * rows + 16, HEAD_SIZE), BF16)] * (count - 1)
    return pl.pallas_call(
        functools.partial(project_kernel, count, rows, heads, chunks),
        in_specs=[SMEM, HBM, HBM, HBM],
        out_shape=outs,
        out_specs=[VMEM] * len(outs),
        scratch_shapes=[
            pltpu.VMEM((length, depth), BF16),
            pltpu.VMEM(gain.shape, BF16),
            pltpu.VMEM((depth, width), BF16),
            pltpu.VMEM((length, width), F32),
            pltpu.VMEM((length, HEAD_SIZE), F32),
            pltpu.SemaphoreType.DMA((2 * chunks + 1,)),
        ],
        compiler_params=pltpu.CompilerParams(vmem_limit_bytes=16 << 20),
        cost_estimate=pl.CostEstimate(
            flops=2 * length * depth * width, bytes_accessed=2 * depth * (length + width), transcendentals=0
        ),
        name="project",
    )(at, span_hidden, gain, key_value_weight)


def combine_kernel(rows, heads, first_ref, own_ref, square_ref, cosine_ref, sine_ref, *rest):
    got, out_ref = rest[:-1], rest[-1]
    line = jnp.zeros((1, HEAD_SIZE), F32)
    for ref in got:
        tail = ref[heads * rows :, :].astype(F32)
        line = line + tail[0:1, :] + tail[1:2, :]
    column = jnp.sum(jnp.where(diagonal(rows), line, 0.0), axis=1, keepdims=True)
    scale = lax.rsqrt((square_ref[...] + column) / MODEL_WIDTH + EPS)
    cosine, sine = cosine_ref[...], sine_ref[...]
    for h in range(heads):
        span = slice(h * rows, (h + 1) * rows)
        value = own_ref[span, :]
        for ref in got:
            value = value + ref[span, :].astype(F32)
        value = value * scale
        is_key = first_ref[0] + h < KEY_HEADS
        out = jnp.where(is_key, turn(value, cosine, sine), value)
        out_ref[:, h * HEAD_SIZE : (h + 1) * HEAD_SIZE] = out.astype(BF16)


def combine(first, own, square, cosine, sine, got):
    rows = square.shape[0]
    heads = own.shape[0] // rows
    return pl.pallas_call(
        functools.partial(combine_kernel, rows, heads),
        in_specs=[SMEM] + [VMEM] * (4 + len(got)),
        out_shape=jax.ShapeDtypeStruct((rows, heads * HEAD_SIZE), BF16),
        out_specs=VMEM,
        compiler_params=pltpu.CompilerParams(vmem_limit_bytes=4 << 20),
        name="combine",
    )(first, own, square, cosine, sine, *got)


def queries_kernel(query_ref, own_ref, cosine_ref, sine_ref, query_out, key_out):
    tokens = cosine_ref.shape[0]
    cosine, sine = cosine_ref[...], sine_ref[...]
    for h in range(KEY_HEADS):
        span = slice(h * HEAD_SIZE, (h + 1) * HEAD_SIZE)
        key_out[:, span] = turn(own_ref[:, span].astype(F32), cosine, sine).astype(BF16)
    factor = HEAD_SIZE**-0.5 * math.log2(math.e)
    cosine, sine = cosine * factor, sine * factor
    for h in range(QUERY_HEADS):
        span = slice(h * HEAD_SIZE, (h + 1) * HEAD_SIZE)
        turned = turn(query_ref[:, span].astype(F32), cosine, sine)
        query_out[h * tokens : (h + 1) * tokens, :] = turned.astype(BF16)


def queries(cont_query, own_rows, cosine, sine):
    tokens = cosine.shape[0]
    return pl.pallas_call(
        queries_kernel,
        in_specs=[VMEM] * 4,
        out_shape=[
            jax.ShapeDtypeStruct((QUERY_HEADS * tokens, HEAD_SIZE), BF16),
            jax.ShapeDtypeStruct((tokens, KEY_COLUMNS), BF16),
        ],
        out_specs=[VMEM, VMEM],
        compiler_params=pltpu.CompilerParams(vmem_limit_bytes=8 << 20),
        cost_estimate=pl.CostEstimate(flops=8 * cont_query.size, bytes_accessed=4 * cont_query.size, transcendentals=0),
        name="queries",
    )(cont_query, own_rows, cosine, sine)


def attend_kernel(sets, plan, first, last, spots_ref, query_ref, *rest):
    pieces, rest = rest[: len(plan)], rest[len(plan) :]
    if first:
        key_ref, own_ref = rest[:2]
        top_out, mixed_out, cache = rest[2:]
    elif last:
        top_ref, mixed_ref, out_ref, cache, staged, sems = rest
    else:
        top_ref, mixed_ref, top_out, mixed_out, cache = rest
    me, offset, length = spots_ref[0], spots_ref[1], spots_ref[2]
    width = cache.shape[2]
    heads = width // HEAD_SIZE
    block = query_ref.shape[0] // KEY_HEADS
    tokens = block // GROUP
    total_rows = cache.shape[1]
    for ref, (step, row) in zip(pieces, plan):
        cache[source(me, step, sets), row : row + ref.shape[0], :] = ref[...]
    if first:
        prompt_rows = total_rows - tokens
        for s in range(sets):
            mine = key_ref if s * width < KEY_COLUMNS else own_ref
            cache[s, prompt_rows:, :] = mine[:, s * width : (s + 1) * width]
        token = lax.broadcasted_iota(jnp.int32, (tokens, total_rows), 0)
        place = lax.broadcasted_iota(jnp.int32, (tokens, total_rows), 1)
        live = (place < offset) & (place < prompt_rows) | (place >= prompt_rows) & (place - prompt_rows <= token)
        bias = jnp.concatenate([jnp.where(live, 0.0, NEGATIVE_LARGE)] * GROUP, axis=0)
    if last:
        keep = lax.broadcasted_iota(jnp.int32, (tokens, HEAD_SIZE), 0) < length
    ones = jnp.ones((total_rows, HEAD_SIZE), BF16)
    copies = []
    for g in range(KEY_HEADS):
        lane = (g % heads) * HEAD_SIZE
        span = slice(g * block, (g + 1) * block)
        key = cache[g // heads, :, lane : lane + HEAD_SIZE]
        value = cache[sets // 2 + g // heads, :, lane : lane + HEAD_SIZE]
        scores = lax.dot_general(
            query_ref[span, :], key, (((1,), (1,)), ((), ())), preferred_element_type=F32
        )
        if first:
            scores = scores + bias
        top = jnp.max(scores, axis=1, keepdims=True)
        if not first:
            old = top_ref[span, :]
            top = jnp.maximum(old, top)
        weights = jnp.exp2(scores - top[:, :1]).astype(BF16)
        mixed = jnp.dot(weights, jnp.concatenate([value, ones], axis=1), preferred_element_type=F32)
        if not first:
            shrink = jnp.exp2(old - top)
            mixed = mixed + mixed_ref[span, :] * jnp.concatenate([shrink, shrink], axis=1)
        if last:
            mixed = mixed[:, :HEAD_SIZE] / mixed[:, HEAD_SIZE:]
            for j in range(GROUP):
                column = (g * GROUP + j) * HEAD_SIZE
                piece = jnp.where(keep, mixed[j * tokens : (j + 1) * tokens, :], 0.0)
                staged[:, column : column + HEAD_SIZE] = piece.astype(BF16)
            part = pl.ds(g * GROUP * HEAD_SIZE, GROUP * HEAD_SIZE)
            copies.append(pltpu.make_async_copy(staged.at[:, part], out_ref.at[:, part], sems.at[g]))
            copies[-1].start()
        else:
            top_out[span, :] = jnp.broadcast_to(top, (block, HEAD_SIZE))
            mixed_out[span, :] = mixed
    for copy in copies:
        copy.wait()


def attend(spots, query, sets, pieces, own=(), state=(), last=False):
    first = not state
    width = pieces[0][2].shape[1]
    block = query.shape[0] // KEY_HEADS
    tokens = block // GROUP
    total_rows = max(row + value.shape[0] for _, row, value in pieces) + (tokens if first else 0)
    plan = [(step, row) for step, row, _ in pieces]
    operands = [spots, query] + [value for _, _, value in pieces] + list(own) + list(state)
    scratch = [pltpu.VMEM((sets, total_rows, width), BF16)]
    if last:
        out_shape = jax.ShapeDtypeStruct((tokens, QUERY_HEADS * HEAD_SIZE), BF16)
        out_specs = HBM
        scratch += [pltpu.VMEM(out_shape.shape, BF16), pltpu.SemaphoreType.DMA((KEY_HEADS,))]
    else:
        out_shape = [
            jax.ShapeDtypeStruct((query.shape[0], HEAD_SIZE), F32),
            jax.ShapeDtypeStruct((query.shape[0], 2 * HEAD_SIZE), F32),
        ]
        out_specs = [VMEM, VMEM]
    name = "attend_own" if first else "attend_last" if last else "attend_more"
    return pl.pallas_call(
        functools.partial(attend_kernel, sets, plan, first, last),
        in_specs=[SMEM] + [VMEM] * (len(operands) - 1),
        out_shape=out_shape,
        out_specs=out_specs,
        scratch_shapes=scratch,
        input_output_aliases={} if first or last else {len(operands) - 2: 0, len(operands) - 1: 1},
        compiler_params=pltpu.CompilerParams(vmem_limit_bytes=16 << 20),
        cost_estimate=pl.CostEstimate(
            flops=4 * query.size * total_rows, bytes_accessed=4 * query.size, transcendentals=query.size
        ),
        name=name,
    )(*operands)


def on_device(
    span_hidden,
    norm_gain,
    key_value_weight,
    prompt_key_value,
    span_offset,
    cont_query,
    continuation_key_value,
    cont_lengths,
):
    offset = span_offset[0]
    sets, count = lax.axis_size("set"), lax.axis_size("seq")
    my_set, my_seq = lax.axis_index("set"), lax.axis_index("seq")
    width = key_value_weight.shape[1]
    rows = span_hidden.shape[0] // count
    tokens = cont_query.shape[1]
    low = 2 if sets % 2 == 0 else 1

    own, square, *sends = project(my_seq[None].astype(jnp.int32), span_hidden, norm_gain, key_value_weight, count)
    order = list(range(count - 1, 0, -1))
    got = [exchange(sends[k - 1], "seq", k) for k in order]

    span_cosine, span_sine = tables(offset + my_seq * rows + jnp.arange(rows, dtype=jnp.int32))
    self_cosine, self_sine = tables(offset + SPAN_LENGTH + jnp.arange(tokens, dtype=jnp.int32))
    query, key = queries(cont_query[0], continuation_key_value[0], self_cosine, self_sine)

    mine = lax.dynamic_slice_in_dim(prompt_key_value, my_set * width, width, 1)
    mine, _ = lax.optimization_barrier((mine, got[0]))
    parts = [mine] + [exchange(mine, "seq", k) for k in order]
    prompt = jnp.zeros((count,) + mine.shape, BF16)
    for part, place in zip(parts, [my_seq] + [source(my_seq, k, count) for k in order]):
        prompt = lax.dynamic_update_slice(prompt, part[None], (place, 0, 0))
    prompt = prompt.reshape(-1, width)

    first = (my_set * (width // HEAD_SIZE))[None].astype(jnp.int32)
    block = combine(first, own, square, span_cosine, span_sine, got)

    far = list(range(low, sets, low))
    beside = [exchange(block, "set", step) for step in far]
    across = [exchange(block, "seq", k) for k in order[:-1]]
    nearest = exchange(jnp.concatenate([block] + beside, axis=0), "seq", order[-1])
    prompt, _ = lax.optimization_barrier((prompt, beside))
    prompts = [prompt] + [exchange(prompt, "set", step) for step in far]
    columns = [(0, [block] + beside)]
    for k, value in zip(order[:-1], across):
        columns.append((k * rows, [value] + [exchange(value, "set", step) for step in far]))
    columns.append((order[-1] * rows, [nearest[i * rows : (i + 1) * rows] for i in range(1 + len(far))]))

    def with_core(first_row, values):
        steps = [0] + far
        pieces = [(step, first_row, value) for step, value in zip(steps, values)]
        if low == 2:
            length = values[0].shape[0]
            others = exchange(jnp.concatenate(values, axis=0), "set", 1)
            pieces += [
                (step ^ 1, first_row, others[i * length : (i + 1) * length]) for i, step in enumerate(steps)
            ]
        return pieces

    spots = jnp.stack([my_set.astype(jnp.int32), offset, cont_lengths[0]])
    state = attend(spots, query, sets, with_core(0, prompts), own=(key, continuation_key_value[0]))
    split = max(1, len(columns) // 2)
    shares = [columns[:split], columns[split:]]
    for share in shares:
        pieces, row = [], 0
        for _, values in share:
            pieces += with_core(row, values)
            row += rows
        state = attend(spots, query, sets, pieces, state=state, last=share is shares[-1])
    return block, state[None]


def solution(mesh):
    placed = (
        P("parts", "seq"),
        P("seq"),
        P("seq", "set"),
        P(("parts", "seq"), None),
        P("parts"),
        P(("parts", "set", "seq"), None, None),
        P(("parts", "set", "seq"), None, None),
        P(("parts", "set", "seq")),
    )
    return jax.shard_map(
        on_device,
        mesh=mesh,
        in_specs=placed,
        out_specs=(P(("parts", "seq"), "set"), P(("parts", "set", "seq"), None, None)),
        check_vma=False,
    )
```

```python
import functools
import math

import jax
import jax.numpy as jnp
from jax import lax
from jax.experimental import pallas as pl
from jax.experimental.pallas import tpu as pltpu
from jax.sharding import PartitionSpec as P

MODEL_WIDTH = 8192
QUERY_HEADS = 64
KEY_HEADS = 8
HEAD_SIZE = 128
SPAN_LENGTH = 256
EPS = 1e-05
NEGATIVE_LARGE = -1e30
GROUP = QUERY_HEADS // KEY_HEADS
KEY_COLUMNS = KEY_HEADS * HEAD_SIZE
BF16 = jnp.bfloat16
F32 = jnp.float32
VMEM = pl.BlockSpec(memory_space=pltpu.VMEM)
HBM = pl.BlockSpec(memory_space=pltpu.HBM)
SMEM = pl.BlockSpec(memory_space=pltpu.SMEM)


def peer(index, step, count):
    if count & (count - 1) == 0:
        return index ^ step
    return (index + step) % count


def source(index, step, count):
    if count & (count - 1) == 0:
        return index ^ step
    return (index + count - step) % count


def exchange(value, axis, step):
    count = lax.axis_size(axis)
    return lax.ppermute(value, axis, [(i, peer(i, step, count)) for i in range(count)])


def frequencies():
    base = 500000.0 ** (-(jnp.arange(HEAD_SIZE // 2).astype(F32) * 2.0) / HEAD_SIZE)
    wave = 2.0 * math.pi / base
    smooth = (8192.0 / wave - 1.0) / 3.0
    blended = (1.0 - smooth) * base / 8.0 + smooth * base
    return jnp.where(wave < 2048.0, base, jnp.where(wave > 8192.0, base / 8.0, blended))


def tables(positions):
    angles = positions.astype(F32)[:, None] * frequencies()[None, :]
    cosine, sine = jnp.cos(angles), jnp.sin(angles)
    return jnp.concatenate([cosine, cosine], -1), jnp.concatenate([-sine, sine], -1)


def turn(value, cosine, sine):
    return value * cosine + pltpu.roll(value, HEAD_SIZE // 2, 1) * sine


def diagonal(rows):
    shape = (rows, HEAD_SIZE)
    return lax.broadcasted_iota(jnp.int32, shape, 0) == lax.broadcasted_iota(jnp.int32, shape, 1)


def project_kernel(count, rows, heads, chunks, at_ref, hidden_ref, gain_ref, weight_ref, prompt_ref, *rest):
    own_ref, square_ref, mine_ref = rest[:3]
    sends = rest[3 : 2 + count]
    hidden_buf, gain_buf, weight_buf, total, squares, sems = rest[2 + count :]
    depth = hidden_ref.shape[1]
    size = depth // chunks
    width = weight_ref.shape[1]
    cached = prompt_ref.shape[0]
    gain_copy = pltpu.make_async_copy(gain_ref, gain_buf, sems.at[2 * chunks])
    gain_copy.start()
    columns = pl.ds(pl.multiple_of(at_ref[1] * width, HEAD_SIZE), width)
    prompt_copy = pltpu.make_async_copy(prompt_ref.at[:, columns], mine_ref, sems.at[2 * chunks + 1])
    copies = []
    for c in range(chunks):
        part = pl.ds(c * size, size)
        copies.append(
            (
                pltpu.make_async_copy(hidden_ref.at[:, part], hidden_buf.at[:, part], sems.at[2 * c]),
                pltpu.make_async_copy(weight_ref.at[part, :], weight_buf.at[part, :], sems.at[2 * c + 1]),
            )
        )
        copies[-1][0].start()
        copies[-1][1].start()
    prompt_copy.start()
    gain_copy.wait()
    for c in range(chunks):
        copies[c][0].wait()
        folded, scaled = None, []
        for lane in range(c * size, (c + 1) * size, HEAD_SIZE):
            hidden = hidden_buf[:, lane : lane + HEAD_SIZE].astype(F32)
            tile = lane // HEAD_SIZE
            scaled.append((hidden * gain_buf[tile : tile + 1, :].astype(F32)).astype(BF16))
            square = hidden * hidden
            folded = square if folded is None else folded + square
        copies[c][1].wait()
        part = jnp.dot(
            jnp.concatenate(scaled, axis=1),
            weight_buf[c * size : (c + 1) * size, :],
            preferred_element_type=F32,
        )
        if c == 0:
            total[...] = part
            squares[...] = folded
        else:
            total[...] += part
            squares[...] += folded
    prompt_copy.wait()
    me = at_ref[0]
    for k in range(count):
        to = pl.ds(pl.multiple_of(peer(me, k, count) * rows, rows), rows)
        column = jnp.sum(squares[to, :], axis=1, keepdims=True)
        if k == 0:
            square_ref[...] = jnp.broadcast_to(column, (rows, HEAD_SIZE))
            out = own_ref
        else:
            out = sends[k - 1]
            line = jnp.sum(jnp.where(diagonal(rows), column, 0.0), axis=0, keepdims=True)
            high = line.astype(BF16).astype(F32)
            low = line - high
            which = lax.broadcasted_iota(jnp.int32, (16, HEAD_SIZE), 0)
            tail = jnp.where(which == 0, high, jnp.where(which == 1, low, 0.0))
            out[heads * rows : heads * rows + 16, :] = tail.astype(BF16)
            for h in range(heads):
                first = heads * rows + 16 + h * cached
                out[first : first + cached, :] = mine_ref[:, h * HEAD_SIZE : (h + 1) * HEAD_SIZE]
        for h in range(heads):
            piece = total[to, h * HEAD_SIZE : (h + 1) * HEAD_SIZE]
            out[h * rows : (h + 1) * rows, :] = piece.astype(out.dtype)


def project(at, span_hidden, norm_gain, key_value_weight, prompt_rows, count):
    length, depth = span_hidden.shape
    width = key_value_weight.shape[1]
    rows, heads = length // count, width // HEAD_SIZE
    cached = prompt_rows.shape[0]
    chunks = 4 if depth % (4 * HEAD_SIZE) == 0 else 1
    gain = norm_gain.reshape(-1, HEAD_SIZE)
    outs = [
        jax.ShapeDtypeStruct((heads * rows, HEAD_SIZE), F32),
        jax.ShapeDtypeStruct((rows, HEAD_SIZE), F32),
        jax.ShapeDtypeStruct((cached, width), BF16),
    ] + [jax.ShapeDtypeStruct((heads * (rows + cached) + 16, HEAD_SIZE), BF16)] * (count - 1)
    stay = [pltpu.with_memory_space_constraint(x, pltpu.HBM) for x in (span_hidden, gain, key_value_weight, prompt_rows)]
    return pl.pallas_call(
        functools.partial(project_kernel, count, rows, heads, chunks),
        in_specs=[SMEM, HBM, HBM, HBM, HBM],
        out_shape=outs,
        out_specs=[VMEM] * len(outs),
        scratch_shapes=[
            pltpu.VMEM((length, depth), BF16),
            pltpu.VMEM(gain.shape, BF16),
            pltpu.VMEM((depth, width), BF16),
            pltpu.VMEM((length, width), F32),
            pltpu.VMEM((length, HEAD_SIZE), F32),
            pltpu.SemaphoreType.DMA((2 * chunks + 2,)),
        ],
        compiler_params=pltpu.CompilerParams(vmem_limit_bytes=16 << 20),
        cost_estimate=pl.CostEstimate(
            flops=2 * length * depth * width, bytes_accessed=2 * depth * (length + width), transcendentals=0
        ),
        name="project",
    )(at, *stay)


def combine_kernel(rows, heads, first_ref, own_ref, square_ref, mine_ref, cosine_ref, sine_ref, *rest):
    got, (out_ref, send_ref, prompt_ref) = rest[:-3], rest[-3:]
    cached = mine_ref.shape[0]
    line = jnp.zeros((1, HEAD_SIZE), F32)
    for ref in got:
        tail = ref[heads * rows : heads * rows + 16, :].astype(F32)
        line = line + tail[0:1, :] + tail[1:2, :]
    column = jnp.sum(jnp.where(diagonal(rows), line, 0.0), axis=1, keepdims=True)
    scale = lax.rsqrt((square_ref[...] + column) / MODEL_WIDTH + EPS)
    cosine, sine = cosine_ref[...], sine_ref[...]
    for h in range(heads):
        span = slice(h * rows, (h + 1) * rows)
        lanes = slice(h * HEAD_SIZE, (h + 1) * HEAD_SIZE)
        value = own_ref[span, :]
        for ref in got:
            value = value + ref[span, :].astype(F32)
        value = value * scale
        is_key = first_ref[0] + h < KEY_HEADS
        out = jnp.where(is_key, turn(value, cosine, sine), value).astype(BF16)
        out_ref[:, lanes] = out
        send_ref[:, lanes] = out
        for i, ref in enumerate(got):
            first = heads * rows + 16 + h * cached
            prompt_ref[(i + 1) * cached : (i + 2) * cached, lanes] = ref[first : first + cached, :]
    prompt_ref[:cached, :] = mine_ref[...]


def combine(first, own, square, mine, cosine, sine, got):
    rows = square.shape[0]
    heads = own.shape[0] // rows
    block = jax.ShapeDtypeStruct((rows, heads * HEAD_SIZE), BF16)
    prompt = jax.ShapeDtypeStruct(((1 + len(got)) * mine.shape[0], heads * HEAD_SIZE), BF16)
    return pl.pallas_call(
        functools.partial(combine_kernel, rows, heads),
        in_specs=[SMEM] + [VMEM] * (5 + len(got)),
        out_shape=[block, block, prompt],
        out_specs=[VMEM, VMEM, VMEM],
        compiler_params=pltpu.CompilerParams(vmem_limit_bytes=4 << 20),
        name="combine",
    )(first, own, square, mine, cosine, sine, *got)


def queries_kernel(query_ref, own_ref, cosine_ref, sine_ref, query_out, key_out):
    tokens = cosine_ref.shape[0]
    cosine, sine = cosine_ref[...], sine_ref[...]
    for h in range(KEY_HEADS):
        span = slice(h * HEAD_SIZE, (h + 1) * HEAD_SIZE)
        key_out[:, span] = turn(own_ref[:, span].astype(F32), cosine, sine).astype(BF16)
    factor = HEAD_SIZE**-0.5 * math.log2(math.e)
    cosine, sine = cosine * factor, sine * factor
    for h in range(QUERY_HEADS):
        span = slice(h * HEAD_SIZE, (h + 1) * HEAD_SIZE)
        turned = turn(query_ref[:, span].astype(F32), cosine, sine)
        query_out[h * tokens : (h + 1) * tokens, :] = turned.astype(BF16)


def queries(cont_query, own_rows, cosine, sine):
    tokens = cosine.shape[0]
    return pl.pallas_call(
        queries_kernel,
        in_specs=[VMEM] * 4,
        out_shape=[
            jax.ShapeDtypeStruct((QUERY_HEADS * tokens, HEAD_SIZE), BF16),
            jax.ShapeDtypeStruct((tokens, KEY_COLUMNS), BF16),
        ],
        out_specs=[VMEM, VMEM],
        compiler_params=pltpu.CompilerParams(vmem_limit_bytes=8 << 20),
        cost_estimate=pl.CostEstimate(flops=8 * cont_query.size, bytes_accessed=4 * cont_query.size, transcendentals=0),
        name="queries",
    )(cont_query, own_rows, cosine, sine)


def attend_kernel(sets, count, plan, tile, first, last, spots_ref, query_ref, *rest):
    operands = 1 + max(piece[0] for piece in plan)
    pieces, rest = rest[:operands], rest[operands:]
    if first:
        key_ref, own_ref, state_out, mixed_out, cache = rest
    elif last:
        state_ref, mixed_ref, out_ref, cache = rest
    else:
        state_ref, mixed_ref, state_out, mixed_out, cache = rest
    my_set, my_seq, offset, length = (spots_ref[i] for i in range(4))
    width = cache.shape[2]
    heads = width // HEAD_SIZE
    block = query_ref.shape[0] // KEY_HEADS
    tokens = block // GROUP
    total_rows = cache.shape[1]
    for operand, start, rows, step, place in plan:
        if isinstance(place, tuple):
            place = pl.multiple_of(source(my_seq, place[0], count) * rows, rows)
        cache[source(my_set, step, sets), pl.ds(place, rows), :] = pieces[operand][start : start + rows, :]
    if first:
        prompt_rows = total_rows - tokens
        for s in range(sets):
            mine = key_ref if s * width < KEY_COLUMNS else own_ref
            cache[s, prompt_rows:, :] = mine[:, s * width : (s + 1) * width]
        place = lax.broadcasted_iota(jnp.int32, (total_rows, tokens), 0)
        token = lax.broadcasted_iota(jnp.int32, (total_rows, tokens), 1)
        live = (place < offset) & (place < prompt_rows) | (place >= prompt_rows) & (place - prompt_rows <= token)
        bias = jnp.concatenate([jnp.where(live, 0.0, NEGATIVE_LARGE)] * (tile // tokens), axis=1)
    if last:
        keep = lax.broadcasted_iota(jnp.int32, (tokens, HEAD_SIZE), 0) < length
    units = [(g, start) for g in range(KEY_HEADS) for start in range(0, block, tile)]
    scored, weighed, mixtures = {}, {}, {}

    def score(unit):
        g, start = unit
        lane = (g % heads) * HEAD_SIZE
        key = cache[g // heads, :, lane : lane + HEAD_SIZE]
        query = query_ref[g * block + start : g * block + start + tile, :]
        scores = lax.dot_general(key, query, (((1,), (1,)), ((), ())), preferred_element_type=F32)
        scored[unit] = scores + bias if first else scores

    def weigh(unit):
        g, start = unit
        scores = scored.pop(unit)
        top, shrink = jnp.max(scores, axis=0, keepdims=True), None
        if not first:
            old = state_ref[g, 0:1, start : start + tile]
            top = jnp.maximum(old, top)
            shrink = jnp.exp2(old - top)
        weights = jnp.exp2(scores - top)
        total = jnp.sum(weights, axis=0, keepdims=True)
        if not first:
            total = total + state_ref[g, 1:2, start : start + tile] * shrink
        weighed[unit] = top, shrink, total
        lane = (g % heads) * HEAD_SIZE
        value = cache[sets // 2 + g // heads, :, lane : lane + HEAD_SIZE]
        mixtures[unit] = lax.dot_general(
            value, weights.astype(BF16), (((0,), (0,)), ((), ())), preferred_element_type=F32
        )

    def finish(unit):
        g, start = unit
        top, shrink, total = weighed.pop(unit)
        mixed = mixtures.pop(unit)
        if not first:
            mixed = mixed + mixed_ref[g, :, start : start + tile] * shrink
        if last:
            mixed = (mixed * (1.0 / total)).astype(BF16).T
            for j in range(tile // tokens):
                column = (g * GROUP + start // tokens + j) * HEAD_SIZE
                piece = mixed[j * tokens : (j + 1) * tokens, :]
                out_ref[:, column : column + HEAD_SIZE] = jnp.where(keep, piece, jnp.zeros_like(piece))
        else:
            state_out[g, 0:1, start : start + tile] = top
            state_out[g, 1:2, start : start + tile] = total
            mixed_out[g, :, start : start + tile] = mixed

    for i in range(len(units) + 2):
        if i < len(units):
            score(units[i])
        if 0 <= i - 1 < len(units):
            weigh(units[i - 1])
        if 0 <= i - 2 < len(units):
            finish(units[i - 2])


def attend(spots, query, sets, count, plan, pieces, own=(), state=(), last=False):
    first = not state
    width = pieces[0].shape[1]
    block = query.shape[0] // KEY_HEADS
    tokens = block // GROUP
    per_set = {}
    for _, _, rows, step, _ in plan:
        per_set[step] = per_set.get(step, 0) + rows
    total_rows = per_set[0] + (tokens if first else 0)
    tile = block if first else block // 2
    operands = [spots, query] + list(pieces) + list(own) + list(state)
    if last:
        out_shape = jax.ShapeDtypeStruct((tokens, QUERY_HEADS * HEAD_SIZE), BF16)
        out_specs = VMEM
    else:
        out_shape = [
            jax.ShapeDtypeStruct((KEY_HEADS, 8, block), F32),
            jax.ShapeDtypeStruct((KEY_HEADS, HEAD_SIZE, block), F32),
        ]
        out_specs = [VMEM, VMEM]
    name = "attend_own" if first else "attend_last" if last else "attend_more"
    return pl.pallas_call(
        functools.partial(attend_kernel, sets, count, plan, tile, first, last),
        in_specs=[SMEM] + [VMEM] * (len(operands) - 1),
        out_shape=out_shape,
        out_specs=out_specs,
        scratch_shapes=[pltpu.VMEM((sets, total_rows, width), BF16)],
        compiler_params=pltpu.CompilerParams(vmem_limit_bytes=16 << 20),
        name=name,
    )(*operands)


def on_device(
    span_hidden,
    norm_gain,
    key_value_weight,
    prompt_key_value,
    span_offset,
    cont_query,
    continuation_key_value,
    cont_lengths,
):
    offset = span_offset[0]
    sets, count = lax.axis_size("set"), lax.axis_size("seq")
    my_set, my_seq = lax.axis_index("set"), lax.axis_index("seq")
    width = key_value_weight.shape[1]
    rows = span_hidden.shape[0] // count
    tokens = cont_query.shape[1]
    low = 2 if sets % 2 == 0 else 1

    at = jnp.stack([my_seq, my_set]).astype(jnp.int32)
    own, square, mine, *sends = project(at, span_hidden, norm_gain, key_value_weight, prompt_key_value, count)
    order = list(range(count - 1, 0, -1))
    got = [exchange(sends[k - 1], "seq", k) for k in order]

    span_cosine, span_sine = tables(offset + my_seq * rows + jnp.arange(rows, dtype=jnp.int32))
    self_cosine, self_sine = tables(offset + SPAN_LENGTH + jnp.arange(tokens, dtype=jnp.int32))
    query, key = queries(cont_query[0], continuation_key_value[0], self_cosine, self_sine)
    query, key, span_cosine = lax.optimization_barrier((query, key, span_cosine))

    first = (my_set * (width // HEAD_SIZE))[None].astype(jnp.int32)
    block, send, prompt = combine(first, own, square, mine, span_cosine, span_sine, got)

    far = list(range(low, sets, low))
    steps = [0] + far
    beside = [exchange(send, "set", step) for step in far]
    across = [exchange(send, "seq", k) for k in order[:-1]]
    nearest = exchange(jnp.concatenate([send] + beside, axis=0), "seq", order[-1])
    prompt, _ = lax.optimization_barrier((prompt, beside))
    prompts = [prompt] + [exchange(prompt, "set", step) for step in far]
    stretches = [[send] + beside]
    for value in across:
        stretches.append([value] + [exchange(value, "set", step) for step in far])

    def gather(plan, pieces, stretch, places):
        length = stretch[0].shape[0]
        rows = length // len(places)
        for step, value in zip(steps, stretch):
            for i, place in enumerate(places):
                plan.append((len(pieces), i * rows, rows, step, place))
            pieces.append(value)
        if low == 2:
            for n, step in enumerate(steps):
                for i, place in enumerate(places):
                    plan.append((len(pieces), n * length + i * rows, rows, step ^ 1, place))
            pieces.append(exchange(jnp.concatenate(stretch, axis=0), "set", 1))

    spots = jnp.stack([my_set.astype(jnp.int32), my_seq.astype(jnp.int32), offset, cont_lengths[0]])
    plan, pieces = [], []
    gather(plan, pieces, prompts, [(k,) for k in [0] + order])
    state = attend(spots, query, sets, count, plan, pieces, own=(key, continuation_key_value[0]))

    split = max(1, count // 2)
    plan, pieces = [], []
    for i, stretch in enumerate(stretches[:split]):
        gather(plan, pieces, stretch, [i * rows])
    state = attend(spots, query, sets, count, plan, pieces, state=state)

    plan, pieces = [], []
    for i, stretch in enumerate(stretches[split:]):
        gather(plan, pieces, stretch, [i * rows])
    place = (count - 1 - split) * rows
    for n, step in enumerate(steps):
        plan.append((len(pieces), n * rows, rows, step, place))
    pieces.append(nearest)
    if low == 2:
        for n, step in enumerate(steps):
            plan.append((len(pieces), n * rows, rows, step ^ 1, place))
        pieces.append(exchange(nearest, "set", 1))
    attended = attend(spots, query, sets, count, plan, pieces, state=state, last=True)
    return block, attended[None]


def solution(mesh):
    placed = (
        P("parts", "seq"),
        P("seq"),
        P("seq", "set"),
        P(("parts", "seq"), None),
        P("parts"),
        P(("parts", "set", "seq"), None, None),
        P(("parts", "set", "seq"), None, None),
        P(("parts", "set", "seq")),
    )
    return jax.shard_map(
        on_device,
        mesh=mesh,
        in_specs=placed,
        out_specs=(P(("parts", "seq"), "set"), P(("parts", "set", "seq"), None, None)),
        check_vma=False,
    )
```

```python
import functools
import math

import jax
import jax.numpy as jnp
from jax import lax
from jax.experimental import pallas as pl
from jax.experimental.pallas import tpu as pltpu
from jax.sharding import PartitionSpec as P

MODEL_WIDTH = 8192
QUERY_HEADS = 64
KEY_HEADS = 8
HEAD_SIZE = 128
SPAN_LENGTH = 256
EPS = 1e-05
NEGATIVE_LARGE = -1e30
GROUP = QUERY_HEADS // KEY_HEADS
KEY_COLUMNS = KEY_HEADS * HEAD_SIZE
BF16 = jnp.bfloat16
F32 = jnp.float32
VMEM = pl.BlockSpec(memory_space=pltpu.VMEM)
HBM = pl.BlockSpec(memory_space=pltpu.HBM)
SMEM = pl.BlockSpec(memory_space=pltpu.SMEM)


def peer(index, step, count):
    if count & (count - 1) == 0:
        return index ^ step
    return (index + step) % count


def source(index, step, count):
    if count & (count - 1) == 0:
        return index ^ step
    return (index + count - step) % count


def exchange(value, axis, step):
    count = lax.axis_size(axis)
    return lax.ppermute(value, axis, [(i, peer(i, step, count)) for i in range(count)])


def frequencies():
    base = 500000.0 ** (-(jnp.arange(HEAD_SIZE // 2).astype(F32) * 2.0) / HEAD_SIZE)
    wave = 2.0 * math.pi / base
    smooth = (8192.0 / wave - 1.0) / 3.0
    blended = (1.0 - smooth) * base / 8.0 + smooth * base
    return jnp.where(wave < 2048.0, base, jnp.where(wave > 8192.0, base / 8.0, blended))


def tables(positions):
    angles = positions.astype(F32)[:, None] * frequencies()[None, :]
    cosine, sine = jnp.cos(angles), jnp.sin(angles)
    return jnp.concatenate([cosine, cosine], -1), jnp.concatenate([-sine, sine], -1)


def turn(value, cosine, sine):
    return value * cosine + pltpu.roll(value, HEAD_SIZE // 2, 1) * sine


def diagonal(rows):
    shape = (rows, HEAD_SIZE)
    return lax.broadcasted_iota(jnp.int32, shape, 0) == lax.broadcasted_iota(jnp.int32, shape, 1)


def project_kernel(count, rows, heads, chunks, at_ref, hidden_ref, gain_ref, weight_ref, prompt_ref, *rest):
    own_ref, square_ref, mine_ref = rest[:3]
    sends = rest[3 : 2 + count]
    hidden_buf, gain_buf, weight_buf, total, squares, sems = rest[2 + count :]
    depth = hidden_ref.shape[1]
    size = depth // chunks
    width = weight_ref.shape[1]
    cached = prompt_ref.shape[0]
    gain_copy = pltpu.make_async_copy(gain_ref, gain_buf, sems.at[2 * chunks])
    gain_copy.start()
    columns = pl.ds(pl.multiple_of(at_ref[1] * width, HEAD_SIZE), width)
    prompt_copy = pltpu.make_async_copy(prompt_ref.at[:, columns], mine_ref, sems.at[2 * chunks + 1])
    copies = []
    for c in range(chunks):
        part = pl.ds(c * size, size)
        copies.append(
            (
                pltpu.make_async_copy(hidden_ref.at[:, part], hidden_buf.at[:, part], sems.at[2 * c]),
                pltpu.make_async_copy(weight_ref.at[part, :], weight_buf.at[part, :], sems.at[2 * c + 1]),
            )
        )
        copies[-1][0].start()
        copies[-1][1].start()
    prompt_copy.start()
    gain_copy.wait()
    for c in range(chunks):
        copies[c][0].wait()
        folded, scaled = None, []
        for lane in range(c * size, (c + 1) * size, HEAD_SIZE):
            hidden = hidden_buf[:, lane : lane + HEAD_SIZE].astype(F32)
            tile = lane // HEAD_SIZE
            scaled.append((hidden * gain_buf[tile : tile + 1, :].astype(F32)).astype(BF16))
            square = hidden * hidden
            folded = square if folded is None else folded + square
        copies[c][1].wait()
        part = jnp.dot(
            jnp.concatenate(scaled, axis=1),
            weight_buf[c * size : (c + 1) * size, :],
            preferred_element_type=F32,
        )
        if c == 0:
            total[...] = part
            squares[...] = folded
        else:
            total[...] += part
            squares[...] += folded
    prompt_copy.wait()
    me = at_ref[0]
    for k in range(count):
        to = pl.ds(pl.multiple_of(peer(me, k, count) * rows, rows), rows)
        column = jnp.sum(squares[to, :], axis=1, keepdims=True)
        if k == 0:
            square_ref[...] = jnp.broadcast_to(column, (rows, HEAD_SIZE))
            out = own_ref
        else:
            out = sends[k - 1]
            line = jnp.sum(jnp.where(diagonal(rows), column, 0.0), axis=0, keepdims=True)
            high = line.astype(BF16).astype(F32)
            low = line - high
            which = lax.broadcasted_iota(jnp.int32, (16, HEAD_SIZE), 0)
            tail = jnp.where(which == 0, high, jnp.where(which == 1, low, 0.0))
            out[heads * rows : heads * rows + 16, :] = tail.astype(BF16)
            for h in range(heads):
                first = heads * rows + 16 + h * cached
                out[first : first + cached, :] = mine_ref[:, h * HEAD_SIZE : (h + 1) * HEAD_SIZE]
        for h in range(heads):
            piece = total[to, h * HEAD_SIZE : (h + 1) * HEAD_SIZE]
            out[h * rows : (h + 1) * rows, :] = piece.astype(out.dtype)


def project(at, span_hidden, norm_gain, key_value_weight, prompt_rows, count):
    length, depth = span_hidden.shape
    width = key_value_weight.shape[1]
    rows, heads = length // count, width // HEAD_SIZE
    cached = prompt_rows.shape[0]
    chunks = 4 if depth % (4 * HEAD_SIZE) == 0 else 1
    gain = norm_gain.reshape(-1, HEAD_SIZE)
    outs = [
        jax.ShapeDtypeStruct((heads * rows, HEAD_SIZE), F32),
        jax.ShapeDtypeStruct((rows, HEAD_SIZE), F32),
        jax.ShapeDtypeStruct((cached, width), BF16),
    ] + [jax.ShapeDtypeStruct((heads * (rows + cached) + 16, HEAD_SIZE), BF16)] * (count - 1)
    stay = [pltpu.with_memory_space_constraint(x, pltpu.HBM) for x in (span_hidden, gain, key_value_weight, prompt_rows)]
    return pl.pallas_call(
        functools.partial(project_kernel, count, rows, heads, chunks),
        in_specs=[SMEM, HBM, HBM, HBM, HBM],
        out_shape=outs,
        out_specs=[VMEM] * len(outs),
        scratch_shapes=[
            pltpu.VMEM((length, depth), BF16),
            pltpu.VMEM(gain.shape, BF16),
            pltpu.VMEM((depth, width), BF16),
            pltpu.VMEM((length, width), F32),
            pltpu.VMEM((length, HEAD_SIZE), F32),
            pltpu.SemaphoreType.DMA((2 * chunks + 2,)),
        ],
        compiler_params=pltpu.CompilerParams(vmem_limit_bytes=16 << 20),
        cost_estimate=pl.CostEstimate(
            flops=2 * length * depth * width, bytes_accessed=2 * depth * (length + width), transcendentals=0
        ),
        name="project",
    )(at, *stay)


def combine_kernel(rows, heads, at_ref, own_ref, square_ref, mine_ref, cosine_ref, sine_ref, *rest):
    got, (out_ref, send_ref, packed_ref) = rest[:-3], rest[-3:]
    cached = mine_ref.shape[0]
    count = 1 + len(got)
    me, first = at_ref[0], at_ref[1] * heads

    def prompt_rows(k):
        return pl.ds(pl.multiple_of(rows + source(me, k, count) * cached, 16), cached)

    line = jnp.zeros((1, HEAD_SIZE), F32)
    for ref in got:
        tail = ref[heads * rows : heads * rows + 16, :].astype(F32)
        line = line + tail[0:1, :] + tail[1:2, :]
    column = jnp.sum(jnp.where(diagonal(rows), line, 0.0), axis=1, keepdims=True)
    scale = lax.rsqrt((square_ref[...] + column) / MODEL_WIDTH + EPS)
    cosine, sine = cosine_ref[...], sine_ref[...]
    for h in range(heads):
        span = slice(h * rows, (h + 1) * rows)
        lanes = slice(h * HEAD_SIZE, (h + 1) * HEAD_SIZE)
        value = own_ref[span, :]
        for ref in got:
            value = value + ref[span, :].astype(F32)
        value = value * scale
        out = jnp.where(first + h < KEY_HEADS, turn(value, cosine, sine), value).astype(BF16)
        out_ref[:, lanes] = out
        send_ref[:, lanes] = out
        packed_ref[:rows, lanes] = out
        for i, ref in enumerate(got):
            start = heads * rows + 16 + h * cached
            packed_ref[prompt_rows(count - 1 - i), lanes] = ref[start : start + cached, :]
    packed_ref[prompt_rows(0), :] = mine_ref[...]


def combine(at, own, square, mine, cosine, sine, got):
    rows = square.shape[0]
    heads = own.shape[0] // rows
    block = jax.ShapeDtypeStruct((rows, heads * HEAD_SIZE), BF16)
    packed = jax.ShapeDtypeStruct((rows + (1 + len(got)) * mine.shape[0], heads * HEAD_SIZE), BF16)
    return pl.pallas_call(
        functools.partial(combine_kernel, rows, heads),
        in_specs=[SMEM] + [VMEM] * (5 + len(got)),
        out_shape=[block, block, packed],
        out_specs=[VMEM, VMEM, VMEM],
        compiler_params=pltpu.CompilerParams(vmem_limit_bytes=4 << 20),
        name="combine",
    )(at, own, square, mine, cosine, sine, *got)


def queries_kernel(query_ref, own_ref, cosine_ref, sine_ref, query_out, key_out, value_out):
    tokens = cosine_ref.shape[0]
    cosine, sine = cosine_ref[...], sine_ref[...]
    for h in range(KEY_HEADS):
        span = slice(h * HEAD_SIZE, (h + 1) * HEAD_SIZE)
        key_out[:, span] = turn(own_ref[:, span].astype(F32), cosine, sine).astype(BF16)
    value_out[...] = own_ref[:, KEY_COLUMNS:]
    factor = HEAD_SIZE**-0.5 * math.log2(math.e)
    cosine, sine = cosine * factor, sine * factor
    for h in range(QUERY_HEADS):
        span = slice(h * HEAD_SIZE, (h + 1) * HEAD_SIZE)
        turned = turn(query_ref[:, span].astype(F32), cosine, sine)
        query_out[h * tokens : (h + 1) * tokens, :] = turned.astype(BF16)


def queries(cont_query, own_rows, cosine, sine):
    tokens = cosine.shape[0]
    return pl.pallas_call(
        queries_kernel,
        in_specs=[VMEM] * 4,
        out_shape=[
            jax.ShapeDtypeStruct((QUERY_HEADS * tokens, HEAD_SIZE), BF16),
            jax.ShapeDtypeStruct((tokens, KEY_COLUMNS), BF16),
            jax.ShapeDtypeStruct((tokens, KEY_COLUMNS), BF16),
        ],
        out_specs=[VMEM, VMEM, VMEM],
        compiler_params=pltpu.CompilerParams(vmem_limit_bytes=8 << 20),
        cost_estimate=pl.CostEstimate(flops=8 * cont_query.size, bytes_accessed=4 * cont_query.size, transcendentals=0),
        name="queries",
    )(cont_query, own_rows, cosine, sine)


def attend_kernel(tile, span_rows, last, spots_ref, query_ref, cache_ref, *rest):
    first = span_rows is not None
    if first:
        key_ref, own_ref, state_out, mixed_out = rest
    elif last:
        state_ref, mixed_ref, out_ref = rest
    else:
        state_ref, mixed_ref, state_out, mixed_out = rest
    offset, length = spots_ref[0], spots_ref[1]
    sets, cached_rows, width = cache_ref.shape
    heads = width // HEAD_SIZE
    block = query_ref.shape[0] // KEY_HEADS
    tokens = block // GROUP
    total_rows = cached_rows + (tokens if first else 0)
    if first:
        place = lax.broadcasted_iota(jnp.int32, (total_rows, tokens), 0)
        token = lax.broadcasted_iota(jnp.int32, (total_rows, tokens), 1)
        cached = place - span_rows
        seen = (place < span_rows) | (place < cached_rows) & (cached < offset)
        live = seen | (place >= cached_rows) & (place - cached_rows <= token)
        bias = jnp.concatenate([jnp.where(live, 0.0, NEGATIVE_LARGE)] * (tile // tokens), axis=1)
    if last:
        keep = lax.broadcasted_iota(jnp.int32, (tokens, HEAD_SIZE), 0) < length
    units = [(g, start) for g in range(KEY_HEADS) for start in range(0, block, tile)]
    scored, weighed, mixtures = {}, {}, {}

    def rows_of(g, at, ref):
        lane = (g % heads) * HEAD_SIZE
        rows = cache_ref[at + g // heads, :, lane : lane + HEAD_SIZE]
        if first:
            rows = jnp.concatenate([rows, ref[:, g * HEAD_SIZE : (g + 1) * HEAD_SIZE]], axis=0)
        return rows

    def score(unit):
        g, start = unit
        key = rows_of(g, 0, key_ref if first else None)
        query = query_ref[g * block + start : g * block + start + tile, :]
        scores = lax.dot_general(key, query, (((1,), (1,)), ((), ())), preferred_element_type=F32)
        scored[unit] = scores + bias if first else scores

    def weigh(unit):
        g, start = unit
        scores = scored.pop(unit)
        top, shrink = jnp.max(scores, axis=0, keepdims=True), None
        if not first:
            old = state_ref[g, 0:1, start : start + tile]
            top = jnp.maximum(old, top)
            shrink = jnp.exp2(old - top)
        weights = jnp.exp2(scores - top)
        total = jnp.sum(weights, axis=0, keepdims=True)
        if not first:
            total = total + state_ref[g, 1:2, start : start + tile] * shrink
        weighed[unit] = top, shrink, total
        value = rows_of(g, sets // 2, own_ref if first else None)
        mixtures[unit] = lax.dot_general(
            value, weights.astype(BF16), (((0,), (0,)), ((), ())), preferred_element_type=F32
        )

    def finish(unit):
        g, start = unit
        top, shrink, total = weighed.pop(unit)
        mixed = mixtures.pop(unit)
        if not first:
            mixed = mixed + mixed_ref[g, :, start : start + tile] * shrink
        if last:
            mixed = (mixed * (1.0 / total)).astype(BF16).T
            for j in range(tile // tokens):
                column = (g * GROUP + start // tokens + j) * HEAD_SIZE
                piece = mixed[j * tokens : (j + 1) * tokens, :]
                out_ref[:, column : column + HEAD_SIZE] = jnp.where(keep, piece, jnp.zeros_like(piece))
        else:
            state_out[g, 0:1, start : start + tile] = top
            state_out[g, 1:2, start : start + tile] = total
            mixed_out[g, :, start : start + tile] = mixed

    for i in range(len(units) + 2):
        if i < len(units):
            score(units[i])
        if 0 <= i - 1 < len(units):
            weigh(units[i - 1])
        if 0 <= i - 2 < len(units):
            finish(units[i - 2])


def attend(spots, query, cache, span_rows=None, own=(), state=(), last=False):
    first = not state
    block = query.shape[0] // KEY_HEADS
    tokens = block // GROUP
    tile = block if first else block // 2
    operands = [spots, query, cache] + list(own) + list(state)
    if last:
        out_shape = jax.ShapeDtypeStruct((tokens, QUERY_HEADS * HEAD_SIZE), BF16)
        out_specs = VMEM
    else:
        out_shape = [
            jax.ShapeDtypeStruct((KEY_HEADS, 8, block), F32),
            jax.ShapeDtypeStruct((KEY_HEADS, HEAD_SIZE, block), F32),
        ]
        out_specs = [VMEM, VMEM]
    name = "attend_own" if first else "attend_last" if last else "attend_more"
    return pl.pallas_call(
        functools.partial(attend_kernel, tile, span_rows, last),
        in_specs=[SMEM] + [VMEM] * (len(operands) - 1),
        out_shape=out_shape,
        out_specs=out_specs,
        compiler_params=pltpu.CompilerParams(vmem_limit_bytes=16 << 20),
        name=name,
    )(*operands)


def on_device(
    span_hidden,
    norm_gain,
    key_value_weight,
    prompt_key_value,
    span_offset,
    cont_query,
    continuation_key_value,
    cont_lengths,
):
    offset = span_offset[0]
    sets, count = lax.axis_size("set"), lax.axis_size("seq")
    my_set, my_seq = lax.axis_index("set"), lax.axis_index("seq")
    width = key_value_weight.shape[1]
    rows = span_hidden.shape[0] // count
    tokens = cont_query.shape[1]
    low = 2 if sets % 2 == 0 else 1

    at = jnp.stack([my_seq, my_set]).astype(jnp.int32)
    own, square, mine, *sends = project(at, span_hidden, norm_gain, key_value_weight, prompt_key_value, count)
    order = list(range(count - 1, 0, -1))
    got = [exchange(sends[k - 1], "seq", k) for k in order]

    span_cosine, span_sine = tables(offset + my_seq * rows + jnp.arange(rows, dtype=jnp.int32))
    self_cosine, self_sine = tables(offset + SPAN_LENGTH + jnp.arange(tokens, dtype=jnp.int32))
    query, key, value = queries(cont_query[0], continuation_key_value[0], self_cosine, self_sine)
    query, key, value, span_cosine = lax.optimization_barrier((query, key, value, span_cosine))

    block, send, packed = combine(at, own, square, mine, span_cosine, span_sine, got)

    far = list(range(low, sets, low))
    steps = [0] + far
    beside = [packed] + [exchange(packed, "set", step) for step in far]
    across = [exchange(send, "seq", k) for k in order[:-1]]
    nearest = exchange(jnp.concatenate([send] + [x[:rows] for x in beside[1:]], axis=0), "seq", order[-1])
    stretches = []
    for arrived in across:
        stretches.append([arrived] + [exchange(arrived, "set", step) for step in far])
    stretches.append([nearest[i * rows : (i + 1) * rows] for i in range(len(steps))])

    def gather(share, after=None):
        held = [jnp.concatenate([stretch[n] for stretch in share], axis=0) for n in range(len(steps))]
        if after is not None:
            held, _ = lax.optimization_barrier((held, after))
        size = held[0].shape[0]
        held = list(zip(steps, held))
        if low == 2:
            other = exchange(jnp.concatenate([part for _, part in held], axis=0), "set", 1)
            held += [(step ^ 1, other[n * size : (n + 1) * size]) for n, step in enumerate(steps)]
        cache = jnp.zeros((sets, size, width), BF16)
        for step, part in held:
            cache = lax.dynamic_update_slice(cache, part[None], (source(my_set, step, sets), 0, 0))
        return cache

    spots = jnp.stack([offset, cont_lengths[0]])
    state = attend(spots, query, gather([beside]), span_rows=rows, own=(key, value))
    attended = attend(spots, query, gather(stretches, state), state=state, last=True)
    return block, attended[None]


def solution(mesh):
    placed = (
        P("parts", "seq"),
        P("seq"),
        P("seq", "set"),
        P(("parts", "seq"), None),
        P("parts"),
        P(("parts", "set", "seq"), None, None),
        P(("parts", "set", "seq"), None, None),
        P(("parts", "set", "seq")),
    )
    return jax.shard_map(
        on_device,
        mesh=mesh,
        in_specs=placed,
        out_specs=(P(("parts", "seq"), "set"), P(("parts", "set", "seq"), None, None)),
        check_vma=False,
    )
```

```python
import functools
import math

import jax
import jax.numpy as jnp
from jax import lax
from jax.experimental import pallas as pl
from jax.experimental.pallas import tpu as pltpu
from jax.sharding import PartitionSpec as P

MODEL_WIDTH = 8192
QUERY_HEADS = 64
KEY_HEADS = 8
HEAD_SIZE = 128
SPAN_LENGTH = 256
EPS = 1e-05
NEGATIVE_LARGE = -1e30
GROUP = QUERY_HEADS // KEY_HEADS
KEY_COLUMNS = KEY_HEADS * HEAD_SIZE
BF16 = jnp.bfloat16
F32 = jnp.float32
FLUSHES = 4
VMEM = pl.BlockSpec(memory_space=pltpu.VMEM)
HBM = pl.BlockSpec(memory_space=pltpu.HBM)


def peer(index, step, count):
    if count & (count - 1) == 0:
        return index ^ step
    return (index + step) % count


def source(index, step, count):
    if count & (count - 1) == 0:
        return index ^ step
    return (index + count - step) % count


def exchange(value, axis, step):
    count = lax.axis_size(axis)
    return lax.ppermute(value, axis, [(i, peer(i, step, count)) for i in range(count)])


def frequencies():
    base = 500000.0 ** (-(jnp.arange(HEAD_SIZE // 2).astype(F32) * 2.0) / HEAD_SIZE)
    wave = 2.0 * math.pi / base
    smooth = (8192.0 / wave - 1.0) / 3.0
    blended = (1.0 - smooth) * base / 8.0 + smooth * base
    return jnp.where(wave < 2048.0, base, jnp.where(wave > 8192.0, base / 8.0, blended))


def tables(positions):
    angles = positions.astype(F32)[:, None] * frequencies()[None, :]
    cosine, sine = jnp.cos(angles), jnp.sin(angles)
    return jnp.concatenate([cosine, cosine], -1), jnp.concatenate([-sine, sine], -1)


def turn(value, cosine, sine):
    return value * cosine + pltpu.roll(value, HEAD_SIZE // 2, 1) * sine


def diagonal(rows):
    shape = (rows, HEAD_SIZE)
    return lax.broadcasted_iota(jnp.int32, shape, 0) == lax.broadcasted_iota(jnp.int32, shape, 1)


def project_kernel(count, rows, heads, chunks, hidden_ref, gain_ref, weight_ref, prompt_ref, *rest):
    own_ref, square_ref, mine_ref = rest[:3]
    sends = rest[3 : 2 + count]
    hidden_buf, gain_buf, weight_buf, total, squares, sems = rest[2 + count :]
    depth = hidden_ref.shape[1]
    size = depth // chunks
    width = weight_ref.shape[1]
    cached = prompt_ref.shape[0]
    gain_copy = pltpu.make_async_copy(gain_ref, gain_buf, sems.at[2 * chunks])
    gain_copy.start()
    columns = pl.ds(pl.multiple_of(lax.axis_index("set") * width, HEAD_SIZE), width)
    prompt_copy = pltpu.make_async_copy(prompt_ref.at[:, columns], mine_ref, sems.at[2 * chunks + 1])
    copies = []
    for c in range(chunks):
        part = pl.ds(c * size, size)
        copies.append(
            (
                pltpu.make_async_copy(hidden_ref.at[:, part], hidden_buf.at[:, part], sems.at[2 * c]),
                pltpu.make_async_copy(weight_ref.at[part, :], weight_buf.at[part, :], sems.at[2 * c + 1]),
            )
        )
        copies[-1][0].start()
        copies[-1][1].start()
    prompt_copy.start()
    gain_copy.wait()
    for c in range(chunks):
        copies[c][0].wait()
        folded, scaled = None, []
        for lane in range(c * size, (c + 1) * size, HEAD_SIZE):
            hidden = hidden_buf[:, lane : lane + HEAD_SIZE].astype(F32)
            tile = lane // HEAD_SIZE
            scaled.append((hidden * gain_buf[tile : tile + 1, :].astype(F32)).astype(BF16))
            square = hidden * hidden
            folded = square if folded is None else folded + square
        copies[c][1].wait()
        part = jnp.dot(
            jnp.concatenate(scaled, axis=1),
            weight_buf[c * size : (c + 1) * size, :],
            preferred_element_type=F32,
        )
        if c == 0:
            total[...] = part
            squares[...] = folded
        else:
            total[...] += part
            squares[...] += folded
    prompt_copy.wait()
    me = lax.axis_index("seq")
    for k in range(count):
        to = pl.ds(pl.multiple_of(peer(me, k, count) * rows, rows), rows)
        column = jnp.sum(squares[to, :], axis=1, keepdims=True)
        if k == 0:
            square_ref[...] = jnp.broadcast_to(column, (rows, HEAD_SIZE))
            out = own_ref
        else:
            out = sends[k - 1]
            line = jnp.sum(jnp.where(diagonal(rows), column, 0.0), axis=0, keepdims=True)
            high = line.astype(BF16).astype(F32)
            low = line - high
            which = lax.broadcasted_iota(jnp.int32, (16, HEAD_SIZE), 0)
            tail = jnp.where(which == 0, high, jnp.where(which == 1, low, 0.0))
            out[heads * rows : heads * rows + 16, :] = tail.astype(BF16)
            for h in range(heads):
                first = heads * rows + 16 + h * cached
                out[first : first + cached, :] = mine_ref[:, h * HEAD_SIZE : (h + 1) * HEAD_SIZE]
        for h in range(heads):
            piece = total[to, h * HEAD_SIZE : (h + 1) * HEAD_SIZE]
            out[h * rows : (h + 1) * rows, :] = piece.astype(out.dtype)


def project(span_hidden, norm_gain, key_value_weight, prompt_rows, count):
    length, depth = span_hidden.shape
    width = key_value_weight.shape[1]
    rows, heads = length // count, width // HEAD_SIZE
    cached = prompt_rows.shape[0]
    chunks = 4 if depth % (4 * HEAD_SIZE) == 0 else 1
    gain = norm_gain.reshape(-1, HEAD_SIZE)
    outs = [
        jax.ShapeDtypeStruct((heads * rows, HEAD_SIZE), F32),
        jax.ShapeDtypeStruct((rows, HEAD_SIZE), F32),
        jax.ShapeDtypeStruct((cached, width), BF16),
    ] + [jax.ShapeDtypeStruct((heads * (rows + cached) + 16, HEAD_SIZE), BF16)] * (count - 1)
    stay = [pltpu.with_memory_space_constraint(x, pltpu.HBM) for x in (span_hidden, gain, key_value_weight, prompt_rows)]
    return pl.pallas_call(
        functools.partial(project_kernel, count, rows, heads, chunks),
        in_specs=[HBM, HBM, HBM, HBM],
        out_shape=outs,
        out_specs=[VMEM] * len(outs),
        scratch_shapes=[
            pltpu.VMEM((length, depth), BF16),
            pltpu.VMEM(gain.shape, BF16),
            pltpu.VMEM((depth, width), BF16),
            pltpu.VMEM((length, width), F32),
            pltpu.VMEM((length, HEAD_SIZE), F32),
            pltpu.SemaphoreType.DMA((2 * chunks + 2,)),
        ],
        compiler_params=pltpu.CompilerParams(vmem_limit_bytes=16 << 20),
        cost_estimate=pl.CostEstimate(
            flops=2 * length * depth * width, bytes_accessed=2 * depth * (length + width), transcendentals=0
        ),
        name="project",
    )(*stay)


def combine_kernel(rows, heads, own_ref, square_ref, mine_ref, cosine_ref, sine_ref, *rest):
    got, (send_ref, packed_ref) = rest[:-2], rest[-2:]
    cached = mine_ref.shape[0]
    count = 1 + len(got)
    me, first = lax.axis_index("seq"), lax.axis_index("set") * heads

    def prompt_rows(k):
        return pl.ds(pl.multiple_of(rows + source(me, k, count) * cached, 16), cached)

    line = jnp.zeros((1, HEAD_SIZE), F32)
    for ref in got:
        tail = ref[heads * rows : heads * rows + 16, :].astype(F32)
        line = line + tail[0:1, :] + tail[1:2, :]
    column = jnp.sum(jnp.where(diagonal(rows), line, 0.0), axis=1, keepdims=True)
    scale = lax.rsqrt((square_ref[...] + column) / MODEL_WIDTH + EPS)
    cosine, sine = cosine_ref[...], sine_ref[...]
    for h in range(heads):
        span = slice(h * rows, (h + 1) * rows)
        lanes = slice(h * HEAD_SIZE, (h + 1) * HEAD_SIZE)
        value = own_ref[span, :]
        for ref in got:
            value = value + ref[span, :].astype(F32)
        value = value * scale
        out = jnp.where(first + h < KEY_HEADS, turn(value, cosine, sine), value).astype(BF16)
        send_ref[:, lanes] = out
        packed_ref[:rows, lanes] = out
        for i, ref in enumerate(got):
            start = heads * rows + 16 + h * cached
            packed_ref[prompt_rows(count - 1 - i), lanes] = ref[start : start + cached, :]
    packed_ref[prompt_rows(0), :] = mine_ref[...]


def combine(own, square, mine, cosine, sine, got):
    rows = square.shape[0]
    heads = own.shape[0] // rows
    block = pltpu.VMEM((rows, heads * HEAD_SIZE), BF16)
    packed = jax.ShapeDtypeStruct((rows + (1 + len(got)) * mine.shape[0], heads * HEAD_SIZE), BF16)
    return pl.pallas_call(
        functools.partial(combine_kernel, rows, heads),
        in_specs=[VMEM] * (5 + len(got)),
        out_shape=[block, packed],
        out_specs=[VMEM, VMEM],
        compiler_params=pltpu.CompilerParams(vmem_limit_bytes=4 << 20),
        name="combine",
    )(own, square, mine, cosine, sine, *got)


def queries_kernel(query_ref, own_ref, cosine_ref, sine_ref, query_out, key_out, value_out):
    tokens = cosine_ref.shape[0]
    cosine, sine = cosine_ref[...], sine_ref[...]
    for h in range(KEY_HEADS):
        span = slice(h * HEAD_SIZE, (h + 1) * HEAD_SIZE)
        key_out[:, span] = turn(own_ref[:, span].astype(F32), cosine, sine).astype(BF16)
    value_out[...] = own_ref[:, KEY_COLUMNS:]
    factor = HEAD_SIZE**-0.5 * math.log2(math.e)
    cosine, sine = cosine * factor, sine * factor
    for h in range(QUERY_HEADS):
        span = slice(h * HEAD_SIZE, (h + 1) * HEAD_SIZE)
        turned = turn(query_ref[:, span].astype(F32), cosine, sine)
        query_out[h * tokens : (h + 1) * tokens, :] = turned.astype(BF16)


def queries(cont_query, own_rows, cosine, sine):
    tokens = cosine.shape[0]
    return pl.pallas_call(
        queries_kernel,
        in_specs=[VMEM] * 4,
        out_shape=[
            jax.ShapeDtypeStruct((QUERY_HEADS * tokens, HEAD_SIZE), BF16),
            jax.ShapeDtypeStruct((tokens, KEY_COLUMNS), BF16),
            jax.ShapeDtypeStruct((tokens, KEY_COLUMNS), BF16),
        ],
        out_specs=[VMEM, VMEM, VMEM],
        compiler_params=pltpu.CompilerParams(vmem_limit_bytes=8 << 20),
        cost_estimate=pl.CostEstimate(flops=8 * cont_query.size, bytes_accessed=4 * cont_query.size, transcendentals=0),
        name="queries",
    )(cont_query, own_rows, cosine, sine)


def attend_kernel(plan, sets, spans, tile, last, bounds_ref, query_ref, *rest):
    own = plan is None
    if own:
        key_ref, own_ref, state_out, mixed_out = rest
    else:
        operands = 1 + max(operand for stretch in plan for operand, _ in stretch.values())
        pieces, rest = rest[:operands], rest[operands:]
        if last:
            state_ref, mixed_ref, final_ref, out_ref, sems = rest
        else:
            state_ref, mixed_ref, state_out, mixed_out = rest
    my_set = lax.axis_index("set")
    block = query_ref.shape[0] // KEY_HEADS
    tokens = block // GROUP
    offset, length = bounds_ref[0:1, :], bounds_ref[8:9, :]
    total_rows = sum(rows for rows, _ in spans)
    bias = None
    if own:
        place = lax.broadcasted_iota(jnp.int32, (tokens, tokens), 0)
        token = lax.broadcasted_iota(jnp.int32, (tokens, tokens), 1)
        bias = jnp.concatenate([jnp.where(place <= token, 0.0, NEGATIVE_LARGE)] * (tile // tokens), axis=1)
    elif any(prompt for _, prompt in spans):
        parts = []
        for rows, prompt in spans:
            place = lax.broadcasted_iota(jnp.int32, (rows, HEAD_SIZE), 0)
            parts.append(jnp.where(place < offset, 0.0, NEGATIVE_LARGE) if prompt else jnp.zeros(place.shape, F32))
        bias = jnp.concatenate([jnp.concatenate(parts, axis=0)] * (tile // HEAD_SIZE), axis=1)
    keep = lax.broadcasted_iota(jnp.int32, (tokens, HEAD_SIZE), 0) < length
    units = [(g, start) for g in range(KEY_HEADS) for start in range(0, block, tile)]
    held, scored, weighed, mixtures, copies = {}, {}, {}, {}, []

    def rows_of(column):
        if column not in held:
            if own:
                ref = key_ref if column < KEY_COLUMNS else own_ref
                held[column] = ref[:, column % KEY_COLUMNS : column % KEY_COLUMNS + HEAD_SIZE]
                return held[column]
            width = pieces[0].shape[1]
            lanes = slice(column % width, column % width + HEAD_SIZE)
            parts = []
            for stretch, (rows, _) in zip(plan, spans):
                chosen = None
                for step, (operand, first) in stretch.items():
                    part = pieces[operand][first : first + rows, lanes]
                    here = source(my_set, step, sets) == column // width
                    chosen = part if chosen is None else jnp.where(here, part, chosen)
                parts.append(chosen)
            held[column] = jnp.concatenate(parts, axis=0)
        return held[column]

    def score(unit):
        g, start = unit
        query = query_ref[g * block + start : g * block + start + tile, :]
        key = rows_of(g * HEAD_SIZE)
        scores = lax.dot_general(key, query, (((1,), (1,)), ((), ())), preferred_element_type=F32)
        scored[unit] = scores if bias is None else scores + bias

    def weigh(unit):
        g, start = unit
        scores = scored.pop(unit)
        top, shrink = jnp.max(scores, axis=0, keepdims=True), None
        if not own:
            old = state_ref[g, 0:1, start : start + tile]
            top = jnp.maximum(old, top)
            shrink = jnp.exp2(old - top)
        weights = jnp.exp2(scores - top)
        total = jnp.sum(weights, axis=0, keepdims=True)
        if not own:
            total = total + state_ref[g, 1:2, start : start + tile] * shrink
        weighed[unit] = top, shrink, total
        mixtures[unit] = lax.dot_general(
            rows_of(KEY_COLUMNS + g * HEAD_SIZE),
            weights.astype(BF16),
            (((0,), (0,)), ((), ())),
            preferred_element_type=F32,
        )

    def finish(unit):
        g, start = unit
        top, shrink, total = weighed.pop(unit)
        mixed = mixtures.pop(unit)
        if not own:
            mixed = mixed + mixed_ref[g, :, start : start + tile] * shrink
        if last:
            mixed = (mixed * (1.0 / total)).astype(BF16).T
            for j in range(tile // tokens):
                column = (g * GROUP + start // tokens + j) * HEAD_SIZE
                piece = mixed[j * tokens : (j + 1) * tokens, :]
                out_ref[:, column : column + HEAD_SIZE] = jnp.where(keep, piece, jnp.zeros_like(piece))
        else:
            state_out[g, 0:1, start : start + tile] = top
            state_out[g, 1:2, start : start + tile] = total
            mixed_out[g, :, start : start + tile] = mixed

    flush = len(units) // FLUSHES
    for i in range(len(units) + 2):
        if i < len(units):
            score(units[i])
        if 0 <= i - 1 < len(units):
            weigh(units[i - 1])
        if 0 <= i - 2 < len(units):
            finish(units[i - 2])
            if last and (i - 1) % flush == 0:
                wide = out_ref.shape[1] // FLUSHES
                part = pl.ds(len(copies) * wide, wide)
                copies.append(pltpu.make_async_copy(out_ref.at[:, part], final_ref.at[:, part], sems.at[len(copies)]))
                copies[-1].start()
    for copy in copies:
        copy.wait()


def attend(bounds, query, sets, own=None, plan=None, spans=(), pieces=(), state=(), last=False):
    block = query.shape[0] // KEY_HEADS
    tokens = block // GROUP
    spans = [(tokens, False)] if own else spans
    total_rows = sum(rows for rows, _ in spans)
    tile = block
    operands = [bounds, query] + list(own or ()) + list(pieces) + list(state)
    scratch = []
    if last:
        out_shape = jax.ShapeDtypeStruct((tokens, QUERY_HEADS * HEAD_SIZE), BF16)
        out_specs = HBM
        scratch = [pltpu.VMEM(out_shape.shape, BF16), pltpu.SemaphoreType.DMA((FLUSHES,))]
    else:
        out_shape = [
            jax.ShapeDtypeStruct((KEY_HEADS, 8, block), F32),
            jax.ShapeDtypeStruct((KEY_HEADS, HEAD_SIZE, block), F32),
        ]
        out_specs = [VMEM, VMEM]
    return pl.pallas_call(
        functools.partial(attend_kernel, plan, sets, spans, tile, last),
        in_specs=[VMEM] * len(operands),
        out_shape=out_shape,
        out_specs=out_specs,
        scratch_shapes=scratch,
        compiler_params=pltpu.CompilerParams(vmem_limit_bytes=16 << 20),
        cost_estimate=pl.CostEstimate(
            flops=4 * query.size * total_rows,
            bytes_accessed=4 * query.size,
            transcendentals=query.shape[0] * total_rows,
        ),
        name="attend_own" if own else "attend_last" if last else "attend_more",
    )(*operands)


def on_device(
    span_hidden,
    norm_gain,
    key_value_weight,
    prompt_key_value,
    span_offset,
    cont_query,
    continuation_key_value,
    cont_lengths,
):
    offset = span_offset[0]
    sets, count = lax.axis_size("set"), lax.axis_size("seq")
    my_set, my_seq = lax.axis_index("set"), lax.axis_index("seq")
    width = key_value_weight.shape[1]
    rows = span_hidden.shape[0] // count
    tokens = cont_query.shape[1]
    low = 2 if sets % 2 == 0 else 1

    own, square, mine, *sends = project(span_hidden, norm_gain, key_value_weight, prompt_key_value, count)
    order = list(range(count - 1, 0, -1))
    got = [exchange(sends[k - 1], "seq", k) for k in order]

    span_cosine, span_sine = tables(offset + my_seq * rows + jnp.arange(rows, dtype=jnp.int32))
    self_cosine, self_sine = tables(offset + SPAN_LENGTH + jnp.arange(tokens, dtype=jnp.int32))
    query, key, value = queries(cont_query[0], continuation_key_value[0], self_cosine, self_sine)
    bounds = jnp.repeat(jnp.stack([offset, cont_lengths[0]]), 8)[:, None] * jnp.ones((1, HEAD_SIZE), jnp.int32)
    state = attend(bounds, query, sets, own=(key, value))
    query, state, span_cosine = lax.optimization_barrier((query, state, span_cosine))

    block, packed = combine(own, square, mine, span_cosine, span_sine, got)

    far = list(range(low, sets, low))
    steps = [0] + far
    beside = [packed] + [exchange(packed, "set", step) for step in far]
    across = [exchange(block, "seq", k) for k in order]
    stretches = [[arrived] + [exchange(arrived, "set", step) for step in far] for arrived in across]

    def share(values, spans):
        plan, pieces = [], []
        for lines, stretch_spans in zip(values, spans):
            first = 0
            for rows, _ in stretch_spans:
                plan.append({step: (len(pieces) + n, first) for n, step in enumerate(steps)})
                first += rows
            pieces += lines
        if low == 2:
            other = exchange(jnp.concatenate([line for lines in values for line in lines], axis=0), "set", 1)
            top, at = 0, 0
            for lines, stretch_spans in zip(values, spans):
                size = lines[0].shape[0]
                first = 0
                for rows, _ in stretch_spans:
                    for n, step in enumerate(steps):
                        plan[at][step ^ 1] = (len(pieces), top + n * size + first)
                    first += rows
                    at += 1
                top += size * len(lines)
            pieces.append(other)
        return dict(plan=plan, pieces=pieces, spans=[span for stretch_spans in spans for span in stretch_spans])

    near = share([beside], [[(rows, False), (packed.shape[0] - rows, True)]])
    state = attend(bounds, query, sets, state=state, **near)
    rest = share(stretches, [[(rows, False)]] * len(stretches))
    attended = attend(bounds, query, sets, state=state, last=True, **rest)
    return block, attended[None]


def solution(mesh):
    placed = (
        P("parts", "seq"),
        P("seq"),
        P("seq", "set"),
        P(("parts", "seq"), None),
        P("parts"),
        P(("parts", "set", "seq"), None, None),
        P(("parts", "set", "seq"), None, None),
        P(("parts", "set", "seq")),
    )
    return jax.shard_map(
        on_device,
        mesh=mesh,
        in_specs=placed,
        out_specs=(P(("parts", "seq"), "set"), P(("parts", "set", "seq"), None, None)),
        check_vma=False,
    )
```

```python
import functools
import math

import jax
import jax.numpy as jnp
from jax import lax
from jax.experimental import pallas as pl
from jax.experimental.pallas import tpu as pltpu
from jax.sharding import PartitionSpec as P

MODEL_WIDTH = 8192
QUERY_HEADS = 64
KEY_HEADS = 8
HEAD_SIZE = 128
SPAN_LENGTH = 256
EPS = 1e-05
NEGATIVE_LARGE = -1e30
GROUP = QUERY_HEADS // KEY_HEADS
KEY_COLUMNS = KEY_HEADS * HEAD_SIZE
BF16 = jnp.bfloat16
F32 = jnp.float32
FLUSHES = 4
VMEM = pl.BlockSpec(memory_space=pltpu.VMEM)
HBM = pl.BlockSpec(memory_space=pltpu.HBM)


def peer(index, step, count):
    if count & (count - 1) == 0:
        return index ^ step
    return (index + step) % count


def source(index, step, count):
    if count & (count - 1) == 0:
        return index ^ step
    return (index + count - step) % count


def exchange(value, axis, step):
    count = lax.axis_size(axis)
    return lax.ppermute(value, axis, [(i, peer(i, step, count)) for i in range(count)])


def frequencies():
    base = 500000.0 ** (-(jnp.arange(HEAD_SIZE // 2).astype(F32) * 2.0) / HEAD_SIZE)
    wave = 2.0 * math.pi / base
    smooth = (8192.0 / wave - 1.0) / 3.0
    blended = (1.0 - smooth) * base / 8.0 + smooth * base
    return jnp.where(wave < 2048.0, base, jnp.where(wave > 8192.0, base / 8.0, blended))


def tables(positions):
    angles = positions.astype(F32)[:, None] * frequencies()[None, :]
    cosine, sine = jnp.cos(angles), jnp.sin(angles)
    return jnp.concatenate([cosine, cosine], -1), jnp.concatenate([-sine, sine], -1)


def turn(value, cosine, sine):
    return value * cosine + pltpu.roll(value, HEAD_SIZE // 2, 1) * sine


def diagonal(rows):
    shape = (rows, HEAD_SIZE)
    return lax.broadcasted_iota(jnp.int32, shape, 0) == lax.broadcasted_iota(jnp.int32, shape, 1)


def project_kernel(count, rows, heads, chunks, hidden_ref, gain_ref, weight_ref, *rest):
    own_ref, square_ref = rest[:2]
    sends = rest[2 : 1 + count]
    hidden_buf, gain_buf, weight_buf, total, squares, sems = rest[1 + count :]
    depth = hidden_ref.shape[1]
    size = depth // chunks
    gain_copy = pltpu.make_async_copy(gain_ref, gain_buf, sems.at[2 * chunks])
    gain_copy.start()
    copies = []
    for c in range(chunks):
        part = pl.ds(c * size, size)
        copies.append(
            (
                pltpu.make_async_copy(hidden_ref.at[:, part], hidden_buf.at[:, part], sems.at[2 * c]),
                pltpu.make_async_copy(weight_ref.at[part, :], weight_buf.at[part, :], sems.at[2 * c + 1]),
            )
        )
        copies[-1][0].start()
        copies[-1][1].start()
    gain_copy.wait()
    for c in range(chunks):
        copies[c][0].wait()
        folded, scaled = None, []
        for lane in range(c * size, (c + 1) * size, HEAD_SIZE):
            hidden = hidden_buf[:, lane : lane + HEAD_SIZE].astype(F32)
            tile = lane // HEAD_SIZE
            scaled.append((hidden * gain_buf[tile : tile + 1, :].astype(F32)).astype(BF16))
            square = hidden * hidden
            folded = square if folded is None else folded + square
        copies[c][1].wait()
        part = jnp.dot(
            jnp.concatenate(scaled, axis=1),
            weight_buf[c * size : (c + 1) * size, :],
            preferred_element_type=F32,
        )
        if c == 0:
            total[...] = part
            squares[...] = folded
        else:
            total[...] += part
            squares[...] += folded
    me = lax.axis_index("seq")
    for k in range(count):
        to = pl.ds(pl.multiple_of(peer(me, k, count) * rows, rows), rows)
        column = jnp.sum(squares[to, :], axis=1, keepdims=True)
        if k == 0:
            square_ref[...] = jnp.broadcast_to(column, (rows, HEAD_SIZE))
            out = own_ref
        else:
            out = sends[k - 1]
            line = jnp.sum(jnp.where(diagonal(rows), column, 0.0), axis=0, keepdims=True)
            high = line.astype(BF16).astype(F32)
            low = line - high
            which = lax.broadcasted_iota(jnp.int32, (16, HEAD_SIZE), 0)
            tail = jnp.where(which == 0, high, jnp.where(which == 1, low, 0.0))
            out[heads * rows : heads * rows + 16, :] = tail.astype(BF16)
        for h in range(heads):
            piece = total[to, h * HEAD_SIZE : (h + 1) * HEAD_SIZE]
            out[h * rows : (h + 1) * rows, :] = piece.astype(out.dtype)


def project(span_hidden, norm_gain, key_value_weight, count):
    length, depth = span_hidden.shape
    width = key_value_weight.shape[1]
    rows, heads = length // count, width // HEAD_SIZE
    chunks = 4 if depth % (4 * HEAD_SIZE) == 0 else 1
    gain = norm_gain.reshape(-1, HEAD_SIZE)
    outs = [
        jax.ShapeDtypeStruct((heads * rows, HEAD_SIZE), F32),
        jax.ShapeDtypeStruct((rows, HEAD_SIZE), F32),
    ] + [jax.ShapeDtypeStruct((heads * rows + 16, HEAD_SIZE), BF16)] * (count - 1)
    stay = [pltpu.with_memory_space_constraint(x, pltpu.HBM) for x in (span_hidden, gain, key_value_weight)]
    return pl.pallas_call(
        functools.partial(project_kernel, count, rows, heads, chunks),
        in_specs=[HBM, HBM, HBM],
        out_shape=outs,
        out_specs=[VMEM] * len(outs),
        scratch_shapes=[
            pltpu.VMEM((length, depth), BF16),
            pltpu.VMEM(gain.shape, BF16),
            pltpu.VMEM((depth, width), BF16),
            pltpu.VMEM((length, width), F32),
            pltpu.VMEM((length, HEAD_SIZE), F32),
            pltpu.SemaphoreType.DMA((2 * chunks + 1,)),
        ],
        compiler_params=pltpu.CompilerParams(vmem_limit_bytes=16 << 20),
        cost_estimate=pl.CostEstimate(
            flops=2 * length * depth * width, bytes_accessed=2 * depth * (length + width), transcendentals=0
        ),
        name="project",
    )(*stay)


def combine_kernel(rows, heads, count, places, own_ref, square_ref, cosine_ref, sine_ref, *rest):
    got, prompts, (send_ref, packed_ref) = rest[: count - 1], rest[count - 1 : -2], rest[-2:]
    me, first = lax.axis_index("seq"), lax.axis_index("set") * heads
    line = jnp.zeros((1, HEAD_SIZE), F32)
    for ref in got:
        tail = ref[heads * rows : heads * rows + 16, :].astype(F32)
        line = line + tail[0:1, :] + tail[1:2, :]
    column = jnp.sum(jnp.where(diagonal(rows), line, 0.0), axis=1, keepdims=True)
    scale = lax.rsqrt((square_ref[...] + column) / MODEL_WIDTH + EPS)
    cosine, sine = cosine_ref[...], sine_ref[...]
    for h in range(heads):
        span = slice(h * rows, (h + 1) * rows)
        lanes = slice(h * HEAD_SIZE, (h + 1) * HEAD_SIZE)
        value = own_ref[span, :]
        for ref in got:
            value = value + ref[span, :].astype(F32)
        value = value * scale
        out = jnp.where(first + h < KEY_HEADS, turn(value, cosine, sine), value).astype(BF16)
        send_ref[:, lanes] = out
        packed_ref[:rows, lanes] = out
    cached = prompts[0].shape[0] // len(places[0])
    for ref, steps in zip(prompts, places):
        for i, step in enumerate(steps):
            to = pl.ds(pl.multiple_of(rows + source(me, step, count) * cached, 16), cached)
            packed_ref[to, :] = ref[i * cached : (i + 1) * cached, :]


def combine(own, square, cosine, sine, got, prompts, places):
    rows = square.shape[0]
    heads = own.shape[0] // rows
    block = pltpu.VMEM((rows, heads * HEAD_SIZE), BF16)
    cached = sum(part.shape[0] for part in prompts)
    packed = jax.ShapeDtypeStruct((rows + cached, heads * HEAD_SIZE), BF16)
    return pl.pallas_call(
        functools.partial(combine_kernel, rows, heads, 1 + len(got), places),
        in_specs=[VMEM] * (4 + len(got) + len(prompts)),
        out_shape=[block, packed],
        out_specs=[VMEM, VMEM],
        compiler_params=pltpu.CompilerParams(vmem_limit_bytes=4 << 20),
        name="combine",
    )(own, square, cosine, sine, *got, *prompts)


def queries_kernel(query_ref, own_ref, cosine_ref, sine_ref, query_out, key_out, value_out):
    tokens = cosine_ref.shape[0]
    cosine, sine = cosine_ref[...], sine_ref[...]
    for h in range(KEY_HEADS):
        span = slice(h * HEAD_SIZE, (h + 1) * HEAD_SIZE)
        key_out[:, span] = turn(own_ref[:, span].astype(F32), cosine, sine).astype(BF16)
    value_out[...] = own_ref[:, KEY_COLUMNS:]
    factor = HEAD_SIZE**-0.5 * math.log2(math.e)
    cosine, sine = cosine * factor, sine * factor
    for h in range(QUERY_HEADS):
        span = slice(h * HEAD_SIZE, (h + 1) * HEAD_SIZE)
        turned = turn(query_ref[:, span].astype(F32), cosine, sine)
        query_out[h * tokens : (h + 1) * tokens, :] = turned.astype(BF16)


def queries(cont_query, own_rows, cosine, sine):
    tokens = cosine.shape[0]
    return pl.pallas_call(
        queries_kernel,
        in_specs=[VMEM] * 4,
        out_shape=[
            jax.ShapeDtypeStruct((QUERY_HEADS * tokens, HEAD_SIZE), BF16),
            jax.ShapeDtypeStruct((tokens, KEY_COLUMNS), BF16),
            jax.ShapeDtypeStruct((tokens, KEY_COLUMNS), BF16),
        ],
        out_specs=[VMEM, VMEM, VMEM],
        compiler_params=pltpu.CompilerParams(vmem_limit_bytes=8 << 20),
        cost_estimate=pl.CostEstimate(flops=8 * cont_query.size, bytes_accessed=4 * cont_query.size, transcendentals=0),
        name="queries",
    )(cont_query, own_rows, cosine, sine)


def attend_kernel(plan, sets, spans, tile, last, bounds_ref, query_ref, *rest):
    own = plan is None
    if own:
        key_ref, own_ref, state_out, mixed_out = rest
    else:
        operands = 1 + max(operand for stretch in plan for operand, _ in stretch.values())
        pieces, rest = rest[:operands], rest[operands:]
        if last:
            state_ref, mixed_ref, block_ref, final_ref, block_out, out_ref, sems = rest
        else:
            state_ref, mixed_ref, state_out, mixed_out = rest
    my_set = lax.axis_index("set")
    block = query_ref.shape[0] // KEY_HEADS
    tokens = block // GROUP
    offset, length = bounds_ref[0:1, :], bounds_ref[8:9, :]
    total_rows = sum(rows for rows, _ in spans)
    bias = None
    if own:
        place = lax.broadcasted_iota(jnp.int32, (tokens, tokens), 0)
        token = lax.broadcasted_iota(jnp.int32, (tokens, tokens), 1)
        bias = jnp.concatenate([jnp.where(place <= token, 0.0, NEGATIVE_LARGE)] * (tile // tokens), axis=1)
    elif any(prompt for _, prompt in spans):
        parts = []
        for rows, prompt in spans:
            place = lax.broadcasted_iota(jnp.int32, (rows, HEAD_SIZE), 0)
            parts.append(jnp.where(place < offset, 0.0, NEGATIVE_LARGE) if prompt else jnp.zeros(place.shape, F32))
        bias = jnp.concatenate([jnp.concatenate(parts, axis=0)] * (tile // HEAD_SIZE), axis=1)
    keep = lax.broadcasted_iota(jnp.int32, (tokens, HEAD_SIZE), 0) < length
    units = [(g, start) for g in range(KEY_HEADS) for start in range(0, block, tile)]
    held, scored, weighed, mixtures, copies = {}, {}, {}, {}, []
    if last:
        block_copy = pltpu.make_async_copy(block_ref, block_out, sems.at[FLUSHES])
        block_copy.start()

    def rows_of(column):
        if column not in held:
            if own:
                ref = key_ref if column < KEY_COLUMNS else own_ref
                held[column] = ref[:, column % KEY_COLUMNS : column % KEY_COLUMNS + HEAD_SIZE]
                return held[column]
            width = pieces[0].shape[1]
            lanes = slice(column % width, column % width + HEAD_SIZE)
            parts = []
            for stretch, (rows, _) in zip(plan, spans):
                chosen = None
                for step, (operand, first) in stretch.items():
                    part = pieces[operand][first : first + rows, lanes]
                    here = source(my_set, step, sets) == column // width
                    chosen = part if chosen is None else jnp.where(here, part, chosen)
                parts.append(chosen)
            held[column] = jnp.concatenate(parts, axis=0)
        return held[column]

    def score(unit):
        g, start = unit
        query = query_ref[g * block + start : g * block + start + tile, :]
        key = rows_of(g * HEAD_SIZE)
        scores = lax.dot_general(key, query, (((1,), (1,)), ((), ())), preferred_element_type=F32)
        scored[unit] = scores if bias is None else scores + bias

    def weigh(unit):
        g, start = unit
        scores = scored.pop(unit)
        top, shrink = jnp.max(scores, axis=0, keepdims=True), None
        if not own:
            old = state_ref[g, 0:1, start : start + tile]
            top = jnp.maximum(old, top)
            shrink = jnp.exp2(old - top)
        weights = jnp.exp2(scores - top)
        total = jnp.sum(weights, axis=0, keepdims=True)
        if not own:
            total = total + state_ref[g, 1:2, start : start + tile] * shrink
        weighed[unit] = top, shrink, total
        mixtures[unit] = lax.dot_general(
            rows_of(KEY_COLUMNS + g * HEAD_SIZE),
            weights.astype(BF16),
            (((0,), (0,)), ((), ())),
            preferred_element_type=F32,
        )

    def finish(unit):
        g, start = unit
        top, shrink, total = weighed.pop(unit)
        mixed = mixtures.pop(unit)
        if not own:
            mixed = mixed + mixed_ref[g, :, start : start + tile] * shrink
        if last:
            mixed = (mixed * (1.0 / total)).astype(BF16).T
            for j in range(tile // tokens):
                column = (g * GROUP + start // tokens + j) * HEAD_SIZE
                piece = mixed[j * tokens : (j + 1) * tokens, :]
                out_ref[:, column : column + HEAD_SIZE] = jnp.where(keep, piece, jnp.zeros_like(piece))
        else:
            state_out[g, 0:1, start : start + tile] = top
            state_out[g, 1:2, start : start + tile] = total
            mixed_out[g, :, start : start + tile] = mixed

    flush = len(units) // FLUSHES
    for i in range(len(units) + 2):
        if i < len(units):
            score(units[i])
        if 0 <= i - 1 < len(units):
            weigh(units[i - 1])
        if 0 <= i - 2 < len(units):
            finish(units[i - 2])
            if last and (i - 1) % flush == 0:
                wide = out_ref.shape[1] // FLUSHES
                part = pl.ds(len(copies) * wide, wide)
                copies.append(pltpu.make_async_copy(out_ref.at[:, part], final_ref.at[:, part], sems.at[len(copies)]))
                copies[-1].start()
    for copy in copies:
        copy.wait()
    if last:
        block_copy.wait()


def attend(bounds, query, sets, own=None, plan=None, spans=(), pieces=(), state=(), last=None):
    block = query.shape[0] // KEY_HEADS
    tokens = block // GROUP
    spans = [(tokens, False)] if own else spans
    total_rows = sum(rows for rows, _ in spans)
    tile = block
    operands = [bounds, query] + list(own or ()) + list(pieces) + list(state) + ([] if last is None else [last])
    scratch = []
    if last is not None:
        wide = (tokens, QUERY_HEADS * HEAD_SIZE)
        out_shape = [jax.ShapeDtypeStruct(wide, BF16), jax.ShapeDtypeStruct(last.shape, BF16)]
        out_specs = [HBM, HBM]
        scratch = [pltpu.VMEM(wide, BF16), pltpu.SemaphoreType.DMA((FLUSHES + 1,))]
    else:
        out_shape = [
            jax.ShapeDtypeStruct((KEY_HEADS, 8, block), F32),
            jax.ShapeDtypeStruct((KEY_HEADS, HEAD_SIZE, block), F32),
        ]
        out_specs = [VMEM, VMEM]
    return pl.pallas_call(
        functools.partial(attend_kernel, plan, sets, spans, tile, last is not None),
        in_specs=[VMEM] * len(operands),
        out_shape=out_shape,
        out_specs=out_specs,
        scratch_shapes=scratch,
        compiler_params=pltpu.CompilerParams(vmem_limit_bytes=16 << 20),
        cost_estimate=pl.CostEstimate(
            flops=4 * query.size * total_rows,
            bytes_accessed=4 * query.size,
            transcendentals=query.shape[0] * total_rows,
        ),
        name="attend_own" if own else "attend_more" if last is None else "attend_last",
    )(*operands)


def on_device(
    span_hidden,
    norm_gain,
    key_value_weight,
    prompt_key_value,
    span_offset,
    cont_query,
    continuation_key_value,
    cont_lengths,
):
    sets, count = lax.axis_size("set"), lax.axis_size("seq")
    my_set, my_seq = lax.axis_index("set"), lax.axis_index("seq")
    width = key_value_weight.shape[1]
    rows = span_hidden.shape[0] // count
    tokens = cont_query.shape[1]
    low = 2 if sets % 2 == 0 else 1

    order = list(range(count - 1, 0, -1))
    mine = lax.dynamic_slice_in_dim(prompt_key_value, my_set * width, width, 1)
    prompts, places = [mine], [[0]]
    doubling = count & (count - 1) == 0
    leaps = [count >> i for i in range(1, count.bit_length())] if doubling else order
    early = [exchange(mine, "seq", k) for k in leaps[:1]]

    own, square, *sends = project(span_hidden, norm_gain, key_value_weight, count)
    got = [exchange(sends[k - 1], "seq", k) for k in order]

    for k in leaps:
        come = [step ^ k for steps in places for step in steps] if doubling else [k]
        if k != leaps[0]:
            early.append(exchange(jnp.concatenate(prompts, axis=0) if doubling else mine, "seq", k))
        prompts.append(early[-1])
        places.append(come)

    span_offset, cont_query, continuation_key_value, *_ = lax.optimization_barrier(
        (span_offset, cont_query, continuation_key_value, prompts[1:2])
    )
    offset = span_offset[0]
    span_cosine, span_sine = tables(offset + my_seq * rows + jnp.arange(rows, dtype=jnp.int32))
    self_cosine, self_sine = tables(offset + SPAN_LENGTH + jnp.arange(tokens, dtype=jnp.int32))
    query, key, value = queries(cont_query[0], continuation_key_value[0], self_cosine, self_sine)
    bounds = jnp.repeat(jnp.stack([offset, cont_lengths[0]]), 8)[:, None] * jnp.ones((1, HEAD_SIZE), jnp.int32)
    state = attend(bounds, query, sets, own=(key, value))
    query, state, span_cosine = lax.optimization_barrier((query, state, span_cosine))

    block, packed = combine(own, square, span_cosine, span_sine, got, prompts, places)

    far = list(range(low, sets, low))
    steps = [0] + far
    beside = [packed] + [exchange(packed, "set", step) for step in far]
    across = [exchange(block, "seq", k) for k in order]
    stretches = [[arrived] + [exchange(arrived, "set", step) for step in far] for arrived in across]

    def share(values, spans):
        plan, pieces = [], []
        for lines, stretch_spans in zip(values, spans):
            first = 0
            for rows, _ in stretch_spans:
                plan.append({step: (len(pieces) + n, first) for n, step in enumerate(steps)})
                first += rows
            pieces += lines
        if low == 2:
            other = exchange(jnp.concatenate([line for lines in values for line in lines], axis=0), "set", 1)
            top, at = 0, 0
            for lines, stretch_spans in zip(values, spans):
                size = lines[0].shape[0]
                first = 0
                for rows, _ in stretch_spans:
                    for n, step in enumerate(steps):
                        plan[at][step ^ 1] = (len(pieces), top + n * size + first)
                    first += rows
                    at += 1
                top += size * len(lines)
            pieces.append(other)
        return dict(plan=plan, pieces=pieces, spans=[span for stretch_spans in spans for span in stretch_spans])

    near = share([beside], [[(rows, False), (packed.shape[0] - rows, True)]])
    state = attend(bounds, query, sets, state=state, **near)
    rest = share(stretches, [[(rows, False)]] * len(stretches))
    attended, block = attend(bounds, query, sets, state=state, last=block, **rest)
    return block, attended[None]


def solution(mesh):
    placed = (
        P("parts", "seq"),
        P("seq"),
        P("seq", "set"),
        P(("parts", "seq"), None),
        P("parts"),
        P(("parts", "set", "seq"), None, None),
        P(("parts", "set", "seq"), None, None),
        P(("parts", "set", "seq")),
    )
    return jax.shard_map(
        on_device,
        mesh=mesh,
        in_specs=placed,
        out_specs=(P(("parts", "seq"), "set"), P(("parts", "set", "seq"), None, None)),
        check_vma=False,
    )
```

```python
import functools
import math

import jax
import jax.numpy as jnp
import numpy as np
from jax import lax
from jax.experimental import pallas as pl
from jax.experimental.pallas import tpu as pltpu
from jax.sharding import PartitionSpec as P

MODEL_WIDTH = 8192
QUERY_HEADS = 64
KEY_HEADS = 8
HEAD_SIZE = 128
SPAN_LENGTH = 256
EPS = 1e-05
NEGATIVE_LARGE = -1e30
GROUP = QUERY_HEADS // KEY_HEADS
KEY_COLUMNS = KEY_HEADS * HEAD_SIZE
BF16 = jnp.bfloat16
F32 = jnp.float32
FLUSHES = 4
SMEM = pl.BlockSpec(memory_space=pltpu.SMEM)
VMEM = pl.BlockSpec(memory_space=pltpu.VMEM)
HBM = pl.BlockSpec(memory_space=pltpu.HBM)


def peer(index, step, count):
    if count & (count - 1) == 0:
        return index ^ step
    return (index + step) % count


def source(index, step, count):
    if count & (count - 1) == 0:
        return index ^ step
    return (index + count - step) % count


def exchange(value, axis, step):
    count = lax.axis_size(axis)
    return lax.ppermute(value, axis, [(i, peer(i, step, count)) for i in range(count)])


def frequencies():
    base = 500000.0 ** (-(np.arange(HEAD_SIZE // 2) * 2.0) / HEAD_SIZE)
    wave = 2.0 * math.pi / base
    smooth = (8192.0 / wave - 1.0) / 3.0
    blended = (1.0 - smooth) * base / 8.0 + smooth * base
    rescaled = np.where(wave < 2048.0, base, np.where(wave > 8192.0, base / 8.0, blended))
    return jnp.asarray(np.tile(rescaled, 2)[None], F32)


def turn(value, cosine, sine):
    return value * cosine + pltpu.roll(value, HEAD_SIZE // 2, 1) * sine


def diagonal(rows):
    shape = (rows, HEAD_SIZE)
    return lax.broadcasted_iota(jnp.int32, shape, 0) == lax.broadcasted_iota(jnp.int32, shape, 1)


def project_kernel(count, rows, heads, chunks, hidden_ref, gain_ref, weight_ref, *rest):
    own_ref, square_ref = rest[:2]
    sends = rest[2 : 1 + count]
    hidden_buf, gain_buf, weight_buf, total, squares, sems = rest[1 + count :]
    depth = hidden_ref.shape[1]
    size = depth // chunks
    gain_copy = pltpu.make_async_copy(gain_ref, gain_buf, sems.at[2 * chunks])
    gain_copy.start()
    copies = []
    for c in range(chunks):
        part = pl.ds(c * size, size)
        copies.append(
            (
                pltpu.make_async_copy(hidden_ref.at[:, part], hidden_buf.at[:, part], sems.at[2 * c]),
                pltpu.make_async_copy(weight_ref.at[part, :], weight_buf.at[part, :], sems.at[2 * c + 1]),
            )
        )
        copies[-1][0].start()
        copies[-1][1].start()
    gain_copy.wait()
    for c in range(chunks):
        copies[c][0].wait()
        folded, scaled = None, []
        for lane in range(c * size, (c + 1) * size, HEAD_SIZE):
            hidden = hidden_buf[:, lane : lane + HEAD_SIZE].astype(F32)
            tile = lane // HEAD_SIZE
            scaled.append((hidden * gain_buf[tile : tile + 1, :].astype(F32)).astype(BF16))
            square = hidden * hidden
            folded = square if folded is None else folded + square
        copies[c][1].wait()
        part = jnp.dot(
            jnp.concatenate(scaled, axis=1),
            weight_buf[c * size : (c + 1) * size, :],
            preferred_element_type=F32,
        )
        if c == 0:
            total[...] = part
            squares[...] = folded
        else:
            total[...] += part
            squares[...] += folded
    me = lax.axis_index("seq")
    for k in range(count):
        to = pl.ds(pl.multiple_of(peer(me, k, count) * rows, rows), rows)
        column = jnp.sum(squares[to, :], axis=1, keepdims=True)
        if k == 0:
            square_ref[...] = jnp.broadcast_to(column, (rows, HEAD_SIZE))
            out = own_ref
        else:
            out = sends[k - 1]
            line = jnp.sum(jnp.where(diagonal(rows), column, 0.0), axis=0, keepdims=True)
            high = line.astype(BF16).astype(F32)
            low = line - high
            which = lax.broadcasted_iota(jnp.int32, (16, HEAD_SIZE), 0)
            tail = jnp.where(which == 0, high, jnp.where(which == 1, low, 0.0))
            out[heads * rows : heads * rows + 16, :] = tail.astype(BF16)
        for h in range(heads):
            piece = total[to, h * HEAD_SIZE : (h + 1) * HEAD_SIZE]
            out[h * rows : (h + 1) * rows, :] = piece.astype(out.dtype)


def project(span_hidden, norm_gain, key_value_weight, count):
    length, depth = span_hidden.shape
    width = key_value_weight.shape[1]
    rows, heads = length // count, width // HEAD_SIZE
    chunks = 4 if depth % (4 * HEAD_SIZE) == 0 else 1
    gain = norm_gain.reshape(-1, HEAD_SIZE)
    outs = [
        jax.ShapeDtypeStruct((heads * rows, HEAD_SIZE), F32),
        jax.ShapeDtypeStruct((rows, HEAD_SIZE), F32),
    ] + [jax.ShapeDtypeStruct((heads * rows + 16, HEAD_SIZE), BF16)] * (count - 1)
    stay = [pltpu.with_memory_space_constraint(x, pltpu.HBM) for x in (span_hidden, gain, key_value_weight)]
    return pl.pallas_call(
        functools.partial(project_kernel, count, rows, heads, chunks),
        in_specs=[HBM, HBM, HBM],
        out_shape=outs,
        out_specs=[VMEM] * len(outs),
        scratch_shapes=[
            pltpu.VMEM((length, depth), BF16),
            pltpu.VMEM(gain.shape, BF16),
            pltpu.VMEM((depth, width), BF16),
            pltpu.VMEM((length, width), F32),
            pltpu.VMEM((length, HEAD_SIZE), F32),
            pltpu.SemaphoreType.DMA((2 * chunks + 1,)),
        ],
        compiler_params=pltpu.CompilerParams(vmem_limit_bytes=16 << 20),
        cost_estimate=pl.CostEstimate(
            flops=2 * length * depth * width, bytes_accessed=2 * depth * (length + width), transcendentals=0
        ),
        name="project",
    )(*stay)


def combine_kernel(rows, heads, own_ref, square_ref, cosine_ref, sine_ref, *rest):
    got, out_ref = rest[:-1], rest[-1]
    first = lax.axis_index("set") * heads
    line = jnp.zeros((1, HEAD_SIZE), F32)
    for ref in got:
        tail = ref[heads * rows :, :].astype(F32)
        line = line + tail[0:1, :] + tail[1:2, :]
    column = jnp.sum(jnp.where(diagonal(rows), line, 0.0), axis=1, keepdims=True)
    scale = lax.rsqrt((square_ref[...] + column) / MODEL_WIDTH + EPS)
    cosine, sine = cosine_ref[...], sine_ref[...]
    for h in range(heads):
        span = slice(h * rows, (h + 1) * rows)
        value = own_ref[span, :]
        for ref in got:
            value = value + ref[span, :].astype(F32)
        value = value * scale
        out = jnp.where(first + h < KEY_HEADS, turn(value, cosine, sine), value)
        out_ref[:, h * HEAD_SIZE : (h + 1) * HEAD_SIZE] = out.astype(BF16)


def combine(own, square, cosine, sine, got):
    rows = square.shape[0]
    heads = own.shape[0] // rows
    return pl.pallas_call(
        functools.partial(combine_kernel, rows, heads),
        in_specs=[VMEM] * (4 + len(got)),
        out_shape=pltpu.VMEM((rows, heads * HEAD_SIZE), BF16),
        out_specs=VMEM,
        compiler_params=pltpu.CompilerParams(vmem_limit_bytes=4 << 20),
        name="combine",
    )(own, square, cosine, sine, *got)


def prepare_kernel(
    sets, tile, offset_ref, length_ref, frequency_ref, query_ref, own_ref, cosine_out, sine_out, query_out, state_out, mixed_out, key_buf, value_buf
):
    def table(rows, first):
        place = lax.broadcasted_iota(jnp.int32, (rows, HEAD_SIZE), 0) + first
        angles = place.astype(F32) * frequency_ref[...]
        front = lax.broadcasted_iota(jnp.int32, (rows, HEAD_SIZE), 1) < HEAD_SIZE // 2
        return jnp.cos(angles), jnp.where(front, -1.0, 1.0) * jnp.sin(angles)

    offset = offset_ref[0]
    rows, tokens = cosine_out.shape[0], query_ref.shape[0]
    cosine_out[...], sine_out[...] = table(rows, offset + lax.axis_index("seq") * rows)
    cosine, sine = table(tokens, offset + SPAN_LENGTH)
    for h in range(KEY_HEADS):
        span = slice(h * HEAD_SIZE, (h + 1) * HEAD_SIZE)
        key_buf[:, span] = turn(own_ref[:, span].astype(F32), cosine, sine).astype(BF16)
    value_buf[...] = own_ref[:, KEY_COLUMNS:]
    factor = HEAD_SIZE**-0.5 * math.log2(math.e)
    cosine, sine = cosine * factor, sine * factor
    for h in range(QUERY_HEADS):
        span = slice(h * HEAD_SIZE, (h + 1) * HEAD_SIZE)
        turned = turn(query_ref[:, span].astype(F32), cosine, sine)
        query_out[h * tokens : (h + 1) * tokens, :] = turned.astype(BF16)
    attend_kernel(
        None, sets, [(tokens, ())], tile, False, offset_ref, length_ref, query_out, key_buf, value_buf, state_out, mixed_out
    )


def state_shapes(block):
    return [
        jax.ShapeDtypeStruct((KEY_HEADS, 8, block), F32),
        jax.ShapeDtypeStruct((KEY_HEADS, HEAD_SIZE, block), F32),
    ]


def prepare(offset, length, cont_query, own_rows, sets, rows):
    tokens = cont_query.shape[0]
    block = GROUP * tokens
    table = jax.ShapeDtypeStruct((rows, HEAD_SIZE), F32)
    return pl.pallas_call(
        functools.partial(prepare_kernel, sets, block),
        in_specs=[SMEM, SMEM, VMEM, VMEM, VMEM],
        out_shape=[table, table, jax.ShapeDtypeStruct((QUERY_HEADS * tokens, HEAD_SIZE), BF16)] + state_shapes(block),
        out_specs=[VMEM] * 5,
        scratch_shapes=[pltpu.VMEM((tokens, KEY_COLUMNS), BF16)] * 2,
        compiler_params=pltpu.CompilerParams(vmem_limit_bytes=16 << 20),
        name="prepare",
    )(offset, length, frequencies(), cont_query, own_rows)


def attend_kernel(plan, sets, spans, tile, last, offset_ref, length_ref, query_ref, *rest):
    own = plan is None
    if own:
        key_ref, own_ref, state_out, mixed_out = rest
    else:
        operands = 1 + max(operand for stretch in plan for operand, _ in stretch.values())
        pieces, rest = rest[:operands], rest[operands:]
        if last:
            state_ref, mixed_ref, block_ref, final_ref, block_out, out_ref, sems = rest
        else:
            state_ref, mixed_ref, state_out, mixed_out = rest
    my_set = lax.axis_index("set")
    block = query_ref.shape[0] // KEY_HEADS
    tokens = block // GROUP
    offset, length = offset_ref[0], length_ref[0]
    total_rows = sum(rows for rows, _ in spans)
    bias = None
    if own:
        place = lax.broadcasted_iota(jnp.int32, (tokens, tokens), 0)
        token = lax.broadcasted_iota(jnp.int32, (tokens, tokens), 1)
        bias = jnp.concatenate([jnp.where(place <= token, 0.0, NEGATIVE_LARGE)] * (tile // tokens), axis=1)
    elif any(leaps for _, leaps in spans):
        parts = []
        for rows, leaps in spans:
            place = lax.broadcasted_iota(jnp.int32, (rows, HEAD_SIZE), 0)
            dead = jnp.zeros(place.shape, F32)
            if leaps:
                size = rows // len(leaps)
                for i, step in enumerate(leaps):
                    first = source(lax.axis_index("seq"), step, len(leaps)) * size - i * size
                    here = (place >= i * size) & (place < (i + 1) * size)
                    dead = jnp.where(here & (place + first >= offset), NEGATIVE_LARGE, dead)
            parts.append(dead)
        bias = jnp.concatenate([jnp.concatenate(parts, axis=0)] * (tile // HEAD_SIZE), axis=1)
    keep = lax.broadcasted_iota(jnp.int32, (tokens, HEAD_SIZE), 0) < length
    units = [(g, start) for g in range(KEY_HEADS) for start in range(0, block, tile)]
    held, scored, weighed, mixtures, copies = {}, {}, {}, {}, []
    if last:
        block_copy = pltpu.make_async_copy(block_ref, block_out, sems.at[FLUSHES])
        block_copy.start()

    def rows_of(column):
        if column not in held:
            if own:
                ref = key_ref if column < KEY_COLUMNS else own_ref
                held[column] = ref[:, column % KEY_COLUMNS : column % KEY_COLUMNS + HEAD_SIZE]
                return held[column]
            width = pieces[0].shape[1]
            lanes = slice(column % width, column % width + HEAD_SIZE)
            parts = []
            for stretch, (rows, _) in zip(plan, spans):
                chosen = None
                for step, (operand, first) in stretch.items():
                    part = pieces[operand][first : first + rows, lanes]
                    here = source(my_set, step, sets) == column // width
                    chosen = part if chosen is None else jnp.where(here, part, chosen)
                parts.append(chosen)
            held[column] = jnp.concatenate(parts, axis=0)
        return held[column]

    def score(unit):
        g, start = unit
        query = query_ref[g * block + start : g * block + start + tile, :]
        key = rows_of(g * HEAD_SIZE)
        scores = lax.dot_general(key, query, (((1,), (1,)), ((), ())), preferred_element_type=F32)
        scored[unit] = scores if bias is None else scores + bias

    def weigh(unit):
        g, start = unit
        scores = scored.pop(unit)
        top, shrink = jnp.max(scores, axis=0, keepdims=True), None
        if not own:
            old = state_ref[g, 0:1, start : start + tile]
            top = jnp.maximum(old, top)
            shrink = jnp.exp2(old - top)
        weights = jnp.exp2(scores - top)
        total = jnp.sum(weights, axis=0, keepdims=True)
        if not own:
            total = total + state_ref[g, 1:2, start : start + tile] * shrink
        weighed[unit] = top, shrink, total
        mixtures[unit] = lax.dot_general(
            rows_of(KEY_COLUMNS + g * HEAD_SIZE),
            weights.astype(BF16),
            (((0,), (0,)), ((), ())),
            preferred_element_type=F32,
        )

    def finish(unit):
        g, start = unit
        top, shrink, total = weighed.pop(unit)
        mixed = mixtures.pop(unit)
        if not own:
            mixed = mixed + mixed_ref[g, :, start : start + tile] * shrink
        if last:
            mixed = (mixed * (1.0 / total)).astype(BF16).T
            for j in range(tile // tokens):
                column = (g * GROUP + start // tokens + j) * HEAD_SIZE
                piece = mixed[j * tokens : (j + 1) * tokens, :]
                out_ref[:, column : column + HEAD_SIZE] = jnp.where(keep, piece, jnp.zeros_like(piece))
        else:
            state_out[g, 0:1, start : start + tile] = top
            state_out[g, 1:2, start : start + tile] = total
            mixed_out[g, :, start : start + tile] = mixed

    flush = len(units) // FLUSHES
    for i in range(len(units) + 2):
        if i < len(units):
            score(units[i])
        if 0 <= i - 1 < len(units):
            weigh(units[i - 1])
        if 0 <= i - 2 < len(units):
            finish(units[i - 2])
            if last and (i - 1) % flush == 0:
                wide = out_ref.shape[1] // FLUSHES
                part = pl.ds(len(copies) * wide, wide)
                copies.append(pltpu.make_async_copy(out_ref.at[:, part], final_ref.at[:, part], sems.at[len(copies)]))
                copies[-1].start()
    for copy in copies:
        copy.wait()
    if last:
        block_copy.wait()


def attend(offset, length, query, sets, plan, spans, pieces, state, last=None):
    block = query.shape[0] // KEY_HEADS
    tokens = block // GROUP
    total_rows = sum(rows for rows, _ in spans)
    tile = block if total_rows % 128 else block // 2
    operands = [query] + list(pieces) + list(state) + ([] if last is None else [last])
    out_shape, scratch = state_shapes(block), []
    if last is not None:
        wide = (tokens, QUERY_HEADS * HEAD_SIZE)
        out_shape = [jax.ShapeDtypeStruct(wide, BF16), jax.ShapeDtypeStruct(last.shape, BF16)]
        scratch = [pltpu.VMEM(wide, BF16), pltpu.SemaphoreType.DMA((FLUSHES + 1,))]
    return pl.pallas_call(
        functools.partial(attend_kernel, plan, sets, spans, tile, last is not None),
        in_specs=[SMEM, SMEM] + [VMEM] * len(operands),
        out_shape=out_shape,
        out_specs=[VMEM, VMEM] if last is None else [HBM, HBM],
        scratch_shapes=scratch,
        compiler_params=pltpu.CompilerParams(vmem_limit_bytes=16 << 20),
        name="attend_more" if last is None else "attend_last",
    )(offset, length, *operands)


def on_device(
    span_hidden,
    norm_gain,
    key_value_weight,
    prompt_key_value,
    span_offset,
    cont_query,
    continuation_key_value,
    cont_lengths,
):
    sets, count = lax.axis_size("set"), lax.axis_size("seq")
    rows = span_hidden.shape[0] // count
    low = 2 if sets % 2 == 0 else 1

    order = list(range(count - 1, 0, -1))
    my_set, width = lax.axis_index("set"), key_value_weight.shape[1]
    mine = lax.dynamic_slice_in_dim(prompt_key_value, my_set * width, width, 1)
    doubling = count & (count - 1) == 0
    leaps = [count >> i for i in range(1, count.bit_length())] if doubling else order
    come = exchange(mine, "seq", leaps[0])

    own, square, *sends = project(span_hidden, norm_gain, key_value_weight, count)
    got = [exchange(sends[k - 1], "seq", k) for k in order]

    prompt, places = jnp.concatenate([mine, come], axis=0), [0, leaps[0]]
    prompt, mine, _ = lax.optimization_barrier((prompt, mine, own))
    cont_query, _ = lax.optimization_barrier((cont_query, prompt))
    for k in leaps[1:]:
        come = exchange(prompt if doubling else mine, "seq", k)
        prompt = jnp.concatenate([prompt, come], axis=0)
        places += [place ^ k for place in places] if doubling else [k]

    cosine, sine, query, *state = prepare(
        span_offset, cont_lengths, cont_query[0], continuation_key_value[0], sets, rows
    )
    block = combine(own, square, cosine, sine, got)
    block, prompt = lax.optimization_barrier((block, prompt))

    far = list(range(low, sets, low))
    steps = [0] + far
    half = max(1, (count - 1) // 2)
    beside = [exchange(block, "set", step) for step in far]
    across = [exchange(block, "seq", k) for k in order[:half]]
    both = jnp.concatenate([block] + beside, axis=0)
    together = [exchange(both, "seq", k) for k in order[half:]]
    prompts = [prompt] + [exchange(prompt, "set", step) for step in far]
    stretches = [[block] + beside]
    for arrived in across:
        stretches.append([arrived] + [exchange(arrived, "set", step) for step in far])
    stretches += [[arrived] for arrived in together]

    def share(values, spans):
        plan, pieces = [], []
        for lines, (size, _) in zip(values, spans):
            whole = len(lines) == 1
            plan.append({step: (len(pieces) + (0 if whole else n), n * size if whole else 0) for n, step in enumerate(steps)})
            pieces += lines
        if low == 2:
            other = exchange(jnp.concatenate([line for lines in values for line in lines], axis=0), "set", 1)
            first = 0
            for stretch, (size, _) in zip(plan, spans):
                for step in steps:
                    stretch[step ^ 1] = (len(pieces), first)
                    first += size
            pieces.append(other)
        return dict(plan=plan, pieces=pieces, spans=spans)

    ends = span_offset, cont_lengths
    state = attend(*ends, query, sets, state=state, **share([prompts], [(prompt.shape[0], places)]))
    near = stretches[: 1 + half]
    state = attend(*ends, query, sets, state=state, **share(near, [(rows, ())] * len(near)))
    rest = stretches[1 + half :]
    attended, block = attend(*ends, query, sets, state=state, last=block, **share(rest, [(rows, ())] * len(rest)))
    return block, attended[None]


def solution(mesh):
    placed = (
        P("parts", "seq"),
        P("seq"),
        P("seq", "set"),
        P(("parts", "seq"), None),
        P("parts"),
        P(("parts", "set", "seq"), None, None),
        P(("parts", "set", "seq"), None, None),
        P(("parts", "set", "seq")),
    )
    return jax.shard_map(
        on_device,
        mesh=mesh,
        in_specs=placed,
        out_specs=(P(("parts", "seq"), "set"), P(("parts", "set", "seq"), None, None)),
        check_vma=False,
    )
```

```python
import functools
import math

import jax
import jax.numpy as jnp
import numpy as np
from jax import lax
from jax.experimental import pallas as pl
from jax.experimental.pallas import tpu as pltpu
from jax.sharding import PartitionSpec as P

MODEL_WIDTH = 8192
QUERY_HEADS = 64
KEY_HEADS = 8
HEAD_SIZE = 128
SPAN_LENGTH = 256
EPS = 1e-05
NEGATIVE_LARGE = -1e30
GROUP = QUERY_HEADS // KEY_HEADS
KEY_COLUMNS = KEY_HEADS * HEAD_SIZE
BF16 = jnp.bfloat16
F32 = jnp.float32
FLUSHES = 4
SMEM = pl.BlockSpec(memory_space=pltpu.SMEM)
VMEM = pl.BlockSpec(memory_space=pltpu.VMEM)
HBM = pl.BlockSpec(memory_space=pltpu.HBM)


def peer(index, step, count):
    if count & (count - 1) == 0:
        return index ^ step
    return (index + step) % count


def source(index, step, count):
    if count & (count - 1) == 0:
        return index ^ step
    return (index + count - step) % count


def exchange(value, axis, step):
    count = lax.axis_size(axis)
    return lax.ppermute(value, axis, [(i, peer(i, step, count)) for i in range(count)])


def frequencies():
    base = 500000.0 ** (-(np.arange(HEAD_SIZE // 2) * 2.0) / HEAD_SIZE)
    wave = 2.0 * math.pi / base
    smooth = (8192.0 / wave - 1.0) / 3.0
    blended = (1.0 - smooth) * base / 8.0 + smooth * base
    rescaled = np.where(wave < 2048.0, base, np.where(wave > 8192.0, base / 8.0, blended))
    return jnp.asarray(np.tile(rescaled, 2)[None], F32)


def turn(value, cosine, sine):
    return value * cosine + pltpu.roll(value, HEAD_SIZE // 2, 1) * sine


def diagonal(rows):
    shape = (rows, HEAD_SIZE)
    return lax.broadcasted_iota(jnp.int32, shape, 0) == lax.broadcasted_iota(jnp.int32, shape, 1)


def project_kernel(count, rows, heads, chunks, hidden_ref, gain_ref, weight_ref, prompt_ref, *rest):
    own_ref, square_ref, mine_ref = rest[:3]
    sends = rest[3 : 2 + count]
    hidden_buf, gain_buf, weight_buf, total, squares, sems = rest[2 + count :]
    depth = hidden_ref.shape[1]
    size = depth // chunks
    width = weight_ref.shape[1]
    cached = prompt_ref.shape[0]
    gain_copy = pltpu.make_async_copy(gain_ref, gain_buf, sems.at[2 * chunks])
    gain_copy.start()
    columns = pl.ds(pl.multiple_of(lax.axis_index("set") * width, HEAD_SIZE), width)
    prompt_copy = pltpu.make_async_copy(prompt_ref.at[:, columns], mine_ref, sems.at[2 * chunks + 1])
    copies = []
    for c in range(chunks):
        part = pl.ds(c * size, size)
        copies.append(
            (
                pltpu.make_async_copy(hidden_ref.at[:, part], hidden_buf.at[:, part], sems.at[2 * c]),
                pltpu.make_async_copy(weight_ref.at[part, :], weight_buf.at[part, :], sems.at[2 * c + 1]),
            )
        )
        copies[-1][0].start()
        copies[-1][1].start()
    prompt_copy.start()
    gain_copy.wait()
    for c in range(chunks):
        copies[c][0].wait()
        folded, scaled = None, []
        for lane in range(c * size, (c + 1) * size, HEAD_SIZE):
            hidden = hidden_buf[:, lane : lane + HEAD_SIZE].astype(F32)
            tile = lane // HEAD_SIZE
            scaled.append((hidden * gain_buf[tile : tile + 1, :].astype(F32)).astype(BF16))
            square = hidden * hidden
            folded = square if folded is None else folded + square
        copies[c][1].wait()
        part = jnp.dot(
            jnp.concatenate(scaled, axis=1),
            weight_buf[c * size : (c + 1) * size, :],
            preferred_element_type=F32,
        )
        if c == 0:
            total[...] = part
            squares[...] = folded
        else:
            total[...] += part
            squares[...] += folded
    prompt_copy.wait()
    me = lax.axis_index("seq")
    for k in range(count):
        to = pl.ds(pl.multiple_of(peer(me, k, count) * rows, rows), rows)
        column = jnp.sum(squares[to, :], axis=1, keepdims=True)
        if k == 0:
            square_ref[...] = jnp.broadcast_to(column, (rows, HEAD_SIZE))
            out = own_ref
        else:
            out = sends[k - 1]
            line = jnp.sum(jnp.where(diagonal(rows), column, 0.0), axis=0, keepdims=True)
            high = line.astype(BF16).astype(F32)
            low = line - high
            which = lax.broadcasted_iota(jnp.int32, (16, HEAD_SIZE), 0)
            tail = jnp.where(which == 0, high, jnp.where(which == 1, low, 0.0))
            out[heads * rows : heads * rows + 16, :] = tail.astype(BF16)
            for h in range(heads):
                first = heads * rows + 16 + h * cached
                out[first : first + cached, :] = mine_ref[:, h * HEAD_SIZE : (h + 1) * HEAD_SIZE]
        for h in range(heads):
            piece = total[to, h * HEAD_SIZE : (h + 1) * HEAD_SIZE]
            out[h * rows : (h + 1) * rows, :] = piece.astype(out.dtype)


def project(span_hidden, norm_gain, key_value_weight, prompt_rows, count):
    length, depth = span_hidden.shape
    width = key_value_weight.shape[1]
    rows, heads = length // count, width // HEAD_SIZE
    cached = prompt_rows.shape[0]
    chunks = 4 if depth % (4 * HEAD_SIZE) == 0 else 1
    gain = norm_gain.reshape(-1, HEAD_SIZE)
    outs = [
        jax.ShapeDtypeStruct((heads * rows, HEAD_SIZE), F32),
        jax.ShapeDtypeStruct((rows, HEAD_SIZE), F32),
        jax.ShapeDtypeStruct((cached, width), BF16),
    ] + [jax.ShapeDtypeStruct((heads * (rows + cached) + 16, HEAD_SIZE), BF16)] * (count - 1)
    stay = [pltpu.with_memory_space_constraint(x, pltpu.HBM) for x in (span_hidden, gain, key_value_weight, prompt_rows)]
    return pl.pallas_call(
        functools.partial(project_kernel, count, rows, heads, chunks),
        in_specs=[HBM, HBM, HBM, HBM],
        out_shape=outs,
        out_specs=[VMEM] * len(outs),
        scratch_shapes=[
            pltpu.VMEM((length, depth), BF16),
            pltpu.VMEM(gain.shape, BF16),
            pltpu.VMEM((depth, width), BF16),
            pltpu.VMEM((length, width), F32),
            pltpu.VMEM((length, HEAD_SIZE), F32),
            pltpu.SemaphoreType.DMA((2 * chunks + 2,)),
        ],
        compiler_params=pltpu.CompilerParams(vmem_limit_bytes=16 << 20),
        cost_estimate=pl.CostEstimate(
            flops=2 * length * depth * width, bytes_accessed=2 * depth * (length + width), transcendentals=0
        ),
        name="project",
    )(*stay)


def combine_kernel(rows, heads, own_ref, square_ref, mine_ref, cosine_ref, sine_ref, *rest):
    got, (send_ref, prompt_ref) = rest[:-2], rest[-2:]
    cached = mine_ref.shape[0]
    count = 1 + len(got)
    me, first = lax.axis_index("seq"), lax.axis_index("set") * heads

    def prompt_rows(k):
        return pl.ds(pl.multiple_of(source(me, k, count) * cached, 16), cached)

    line = jnp.zeros((1, HEAD_SIZE), F32)
    for ref in got:
        tail = ref[heads * rows : heads * rows + 16, :].astype(F32)
        line = line + tail[0:1, :] + tail[1:2, :]
    column = jnp.sum(jnp.where(diagonal(rows), line, 0.0), axis=1, keepdims=True)
    scale = lax.rsqrt((square_ref[...] + column) / MODEL_WIDTH + EPS)
    cosine, sine = cosine_ref[...], sine_ref[...]
    for h in range(heads):
        span = slice(h * rows, (h + 1) * rows)
        lanes = slice(h * HEAD_SIZE, (h + 1) * HEAD_SIZE)
        value = own_ref[span, :]
        for ref in got:
            value = value + ref[span, :].astype(F32)
        value = value * scale
        out = jnp.where(first + h < KEY_HEADS, turn(value, cosine, sine), value).astype(BF16)
        send_ref[:, lanes] = out
        for i, ref in enumerate(got):
            start = heads * rows + 16 + h * cached
            prompt_ref[prompt_rows(count - 1 - i), lanes] = ref[start : start + cached, :]
    prompt_ref[prompt_rows(0), :] = mine_ref[...]


def combine(own, square, mine, cosine, sine, got):
    rows = square.shape[0]
    heads = own.shape[0] // rows
    block = pltpu.VMEM((rows, heads * HEAD_SIZE), BF16)
    prompt = jax.ShapeDtypeStruct(((1 + len(got)) * mine.shape[0], heads * HEAD_SIZE), BF16)
    return pl.pallas_call(
        functools.partial(combine_kernel, rows, heads),
        in_specs=[VMEM] * (5 + len(got)),
        out_shape=[block, prompt],
        out_specs=[VMEM, VMEM],
        compiler_params=pltpu.CompilerParams(vmem_limit_bytes=4 << 20),
        name="combine",
    )(own, square, mine, cosine, sine, *got)


def prepare_kernel(
    sets, tile, offset_ref, length_ref, frequency_ref, query_ref, own_ref, cosine_out, sine_out, query_out, state_out, mixed_out, key_buf, value_buf
):
    def table(rows, first):
        place = lax.broadcasted_iota(jnp.int32, (rows, HEAD_SIZE), 0) + first
        angles = place.astype(F32) * frequency_ref[...]
        front = lax.broadcasted_iota(jnp.int32, (rows, HEAD_SIZE), 1) < HEAD_SIZE // 2
        return jnp.cos(angles), jnp.where(front, -1.0, 1.0) * jnp.sin(angles)

    offset = offset_ref[0]
    rows, tokens = cosine_out.shape[0], query_ref.shape[0]
    cosine_out[...], sine_out[...] = table(rows, offset + lax.axis_index("seq") * rows)
    cosine, sine = table(tokens, offset + SPAN_LENGTH)
    for h in range(KEY_HEADS):
        span = slice(h * HEAD_SIZE, (h + 1) * HEAD_SIZE)
        key_buf[:, span] = turn(own_ref[:, span].astype(F32), cosine, sine).astype(BF16)
    value_buf[...] = own_ref[:, KEY_COLUMNS:]
    factor = HEAD_SIZE**-0.5 * math.log2(math.e)
    cosine, sine = cosine * factor, sine * factor
    for h in range(QUERY_HEADS):
        span = slice(h * HEAD_SIZE, (h + 1) * HEAD_SIZE)
        turned = turn(query_ref[:, span].astype(F32), cosine, sine)
        query_out[h * tokens : (h + 1) * tokens, :] = turned.astype(BF16)
    attend_kernel(
        None, sets, [(tokens, False)], tile, False, offset_ref, length_ref, query_out, key_buf, value_buf, state_out, mixed_out
    )


def state_shapes(block):
    return [
        jax.ShapeDtypeStruct((KEY_HEADS, 8, block), F32),
        jax.ShapeDtypeStruct((KEY_HEADS, HEAD_SIZE, block), F32),
    ]


def prepare(offset, length, cont_query, own_rows, sets, rows):
    tokens = cont_query.shape[0]
    block = GROUP * tokens
    table = jax.ShapeDtypeStruct((rows, HEAD_SIZE), F32)
    return pl.pallas_call(
        functools.partial(prepare_kernel, sets, block),
        in_specs=[SMEM, SMEM, VMEM, VMEM, VMEM],
        out_shape=[table, table, jax.ShapeDtypeStruct((QUERY_HEADS * tokens, HEAD_SIZE), BF16)] + state_shapes(block),
        out_specs=[VMEM] * 5,
        scratch_shapes=[pltpu.VMEM((tokens, KEY_COLUMNS), BF16)] * 2,
        compiler_params=pltpu.CompilerParams(vmem_limit_bytes=16 << 20),
        name="prepare",
    )(offset, length, frequencies(), cont_query, own_rows)


def attend_kernel(plan, sets, spans, tile, last, offset_ref, length_ref, query_ref, *rest):
    own = plan is None
    if own:
        key_ref, own_ref, state_out, mixed_out = rest
    else:
        operands = 1 + max(operand for stretch in plan for operand, _ in stretch.values())
        pieces, rest = rest[:operands], rest[operands:]
        if last:
            state_ref, mixed_ref, block_ref, final_ref, block_out, out_ref, sems = rest
        else:
            state_ref, mixed_ref, state_out, mixed_out = rest
    my_set = lax.axis_index("set")
    block = query_ref.shape[0] // KEY_HEADS
    tokens = block // GROUP
    offset, length = offset_ref[0], length_ref[0]
    total_rows = sum(rows for rows, _ in spans)
    bias = None
    if own:
        place = lax.broadcasted_iota(jnp.int32, (tokens, tokens), 0)
        token = lax.broadcasted_iota(jnp.int32, (tokens, tokens), 1)
        bias = jnp.concatenate([jnp.where(place <= token, 0.0, NEGATIVE_LARGE)] * (tile // tokens), axis=1)
    elif any(prompt for _, prompt in spans):
        parts = []
        for rows, prompt in spans:
            place = lax.broadcasted_iota(jnp.int32, (rows, HEAD_SIZE), 0)
            parts.append(jnp.where(place < offset, 0.0, NEGATIVE_LARGE) if prompt else jnp.zeros(place.shape, F32))
        bias = jnp.concatenate([jnp.concatenate(parts, axis=0)] * (tile // HEAD_SIZE), axis=1)
    keep = lax.broadcasted_iota(jnp.int32, (tokens, HEAD_SIZE), 0) < length
    units = [(g, start) for g in range(KEY_HEADS) for start in range(0, block, tile)]
    held, scored, weighed, mixtures, copies = {}, {}, {}, {}, []
    if last:
        block_copy = pltpu.make_async_copy(block_ref, block_out, sems.at[FLUSHES])
        block_copy.start()

    def rows_of(column):
        if column not in held:
            if own:
                ref = key_ref if column < KEY_COLUMNS else own_ref
                held[column] = ref[:, column % KEY_COLUMNS : column % KEY_COLUMNS + HEAD_SIZE]
                return held[column]
            width = pieces[0].shape[1]
            lanes = slice(column % width, column % width + HEAD_SIZE)
            parts = []
            for stretch, (rows, _) in zip(plan, spans):
                chosen = None
                for step, (operand, first) in stretch.items():
                    part = pieces[operand][first : first + rows, lanes]
                    here = source(my_set, step, sets) == column // width
                    chosen = part if chosen is None else jnp.where(here, part, chosen)
                parts.append(chosen)
            held[column] = jnp.concatenate(parts, axis=0)
        return held[column]

    def score(unit):
        g, start = unit
        query = query_ref[g * block + start : g * block + start + tile, :]
        key = rows_of(g * HEAD_SIZE)
        scores = lax.dot_general(key, query, (((1,), (1,)), ((), ())), preferred_element_type=F32)
        scored[unit] = scores if bias is None else scores + bias

    def weigh(unit):
        g, start = unit
        scores = scored.pop(unit)
        top, shrink = jnp.max(scores, axis=0, keepdims=True), None
        if not own:
            old = state_ref[g, 0:1, start : start + tile]
            top = jnp.maximum(old, top)
            shrink = jnp.exp2(old - top)
        weights = jnp.exp2(scores - top)
        total = jnp.sum(weights, axis=0, keepdims=True)
        if not own:
            total = total + state_ref[g, 1:2, start : start + tile] * shrink
        weighed[unit] = top, shrink, total
        mixtures[unit] = lax.dot_general(
            rows_of(KEY_COLUMNS + g * HEAD_SIZE),
            weights.astype(BF16),
            (((0,), (0,)), ((), ())),
            preferred_element_type=F32,
        )

    def finish(unit):
        g, start = unit
        top, shrink, total = weighed.pop(unit)
        mixed = mixtures.pop(unit)
        if not own:
            mixed = mixed + mixed_ref[g, :, start : start + tile] * shrink
        if last:
            mixed = (mixed * (1.0 / total)).astype(BF16).T
            for j in range(tile // tokens):
                column = (g * GROUP + start // tokens + j) * HEAD_SIZE
                piece = mixed[j * tokens : (j + 1) * tokens, :]
                out_ref[:, column : column + HEAD_SIZE] = jnp.where(keep, piece, jnp.zeros_like(piece))
        else:
            state_out[g, 0:1, start : start + tile] = top
            state_out[g, 1:2, start : start + tile] = total
            mixed_out[g, :, start : start + tile] = mixed

    flush = len(units) // FLUSHES
    for i in range(len(units) + 2):
        if i < len(units):
            score(units[i])
        if 0 <= i - 1 < len(units):
            weigh(units[i - 1])
        if 0 <= i - 2 < len(units):
            finish(units[i - 2])
            if last and (i - 1) % flush == 0:
                wide = out_ref.shape[1] // FLUSHES
                part = pl.ds(len(copies) * wide, wide)
                copies.append(pltpu.make_async_copy(out_ref.at[:, part], final_ref.at[:, part], sems.at[len(copies)]))
                copies[-1].start()
    for copy in copies:
        copy.wait()
    if last:
        block_copy.wait()


def attend(offset, length, query, sets, plan, spans, pieces, state, last=None):
    block = query.shape[0] // KEY_HEADS
    tokens = block // GROUP
    total_rows = sum(rows for rows, _ in spans)
    tile = block if total_rows % 128 else block // 2
    operands = [query] + list(pieces) + list(state) + ([] if last is None else [last])
    out_shape, scratch = state_shapes(block), []
    if last is not None:
        wide = (tokens, QUERY_HEADS * HEAD_SIZE)
        out_shape = [jax.ShapeDtypeStruct(wide, BF16), jax.ShapeDtypeStruct(last.shape, BF16)]
        scratch = [pltpu.VMEM(wide, BF16), pltpu.SemaphoreType.DMA((FLUSHES + 1,))]
    return pl.pallas_call(
        functools.partial(attend_kernel, plan, sets, spans, tile, last is not None),
        in_specs=[SMEM, SMEM] + [VMEM] * len(operands),
        out_shape=out_shape,
        out_specs=[VMEM, VMEM] if last is None else [HBM, HBM],
        scratch_shapes=scratch,
        compiler_params=pltpu.CompilerParams(vmem_limit_bytes=16 << 20),
        name="attend_more" if last is None else "attend_last",
    )(offset, length, *operands)


def on_device(
    span_hidden,
    norm_gain,
    key_value_weight,
    prompt_key_value,
    span_offset,
    cont_query,
    continuation_key_value,
    cont_lengths,
):
    sets, count = lax.axis_size("set"), lax.axis_size("seq")
    rows = span_hidden.shape[0] // count
    low = 2 if sets % 2 == 0 else 1

    own, square, mine, *sends = project(span_hidden, norm_gain, key_value_weight, prompt_key_value, count)
    order = list(range(count - 1, 0, -1))
    got = [exchange(sends[k - 1], "seq", k) for k in order]

    cosine, sine, query, *state = prepare(
        span_offset, cont_lengths, cont_query[0], continuation_key_value[0], sets, rows
    )
    block, prompt = combine(own, square, mine, cosine, sine, got)

    far = list(range(low, sets, low))
    steps = [0] + far
    half = max(1, (count - 1) // 2)
    beside = [exchange(block, "set", step) for step in far]
    across = [exchange(block, "seq", k) for k in order[:half]]
    both = jnp.concatenate([block] + beside, axis=0)
    together = [exchange(both, "seq", k) for k in order[half:]]
    prompts = [prompt] + [exchange(prompt, "set", step) for step in far]
    stretches = [[block] + beside]
    for arrived in across:
        stretches.append([arrived] + [exchange(arrived, "set", step) for step in far])
    stretches += [[arrived] for arrived in together]

    def share(values, spans):
        plan, pieces = [], []
        for lines, (size, _) in zip(values, spans):
            whole = len(lines) == 1
            plan.append({step: (len(pieces) + (0 if whole else n), n * size if whole else 0) for n, step in enumerate(steps)})
            pieces += lines
        if low == 2:
            other = exchange(jnp.concatenate([line for lines in values for line in lines], axis=0), "set", 1)
            first = 0
            for stretch, (size, _) in zip(plan, spans):
                for step in steps:
                    stretch[step ^ 1] = (len(pieces), first)
                    first += size
            pieces.append(other)
        return dict(plan=plan, pieces=pieces, spans=spans)

    ends = span_offset, cont_lengths
    state = attend(*ends, query, sets, state=state, **share([prompts], [(prompt.shape[0], True)]))
    near = stretches[: 1 + half]
    state = attend(*ends, query, sets, state=state, **share(near, [(rows, False)] * len(near)))
    rest = stretches[1 + half :]
    attended, block = attend(*ends, query, sets, state=state, last=block, **share(rest, [(rows, False)] * len(rest)))
    return block, attended[None]


def solution(mesh):
    placed = (
        P("parts", "seq"),
        P("seq"),
        P("seq", "set"),
        P(("parts", "seq"), None),
        P("parts"),
        P(("parts", "set", "seq"), None, None),
        P(("parts", "set", "seq"), None, None),
        P(("parts", "set", "seq")),
    )
    return jax.shard_map(
        on_device,
        mesh=mesh,
        in_specs=placed,
        out_specs=(P(("parts", "seq"), "set"), P(("parts", "set", "seq"), None, None)),
        check_vma=False,
    )
```

```python
import functools
import math

import jax
import jax.numpy as jnp
import numpy as np
from jax import lax
from jax.experimental import pallas as pl
from jax.experimental.pallas import tpu as pltpu
from jax.sharding import PartitionSpec as P

MODEL_WIDTH = 8192
QUERY_HEADS = 64
KEY_HEADS = 8
HEAD_SIZE = 128
SPAN_LENGTH = 256
EPS = 1e-05
NEGATIVE_LARGE = -1e30
GROUP = QUERY_HEADS // KEY_HEADS
KEY_COLUMNS = KEY_HEADS * HEAD_SIZE
BF16 = jnp.bfloat16
F32 = jnp.float32
FLUSHES = 4
SMEM = pl.BlockSpec(memory_space=pltpu.SMEM)
VMEM = pl.BlockSpec(memory_space=pltpu.VMEM)
HBM = pl.BlockSpec(memory_space=pltpu.HBM)


def peer(index, step, count):
    if count & (count - 1) == 0:
        return index ^ step
    return (index + step) % count


def source(index, step, count):
    if count & (count - 1) == 0:
        return index ^ step
    return (index + count - step) % count


def exchange(value, axis, step):
    count = lax.axis_size(axis)
    return lax.ppermute(value, axis, [(i, peer(i, step, count)) for i in range(count)])


def frequencies():
    base = 500000.0 ** (-(np.arange(HEAD_SIZE // 2) * 2.0) / HEAD_SIZE)
    wave = 2.0 * math.pi / base
    smooth = (8192.0 / wave - 1.0) / 3.0
    blended = (1.0 - smooth) * base / 8.0 + smooth * base
    rescaled = np.where(wave < 2048.0, base, np.where(wave > 8192.0, base / 8.0, blended))
    return jnp.asarray(np.tile(rescaled, 2)[None], F32)


def turn(value, cosine, sine):
    return value * cosine + pltpu.roll(value, HEAD_SIZE // 2, 1) * sine


def diagonal(rows):
    shape = (rows, HEAD_SIZE)
    return lax.broadcasted_iota(jnp.int32, shape, 0) == lax.broadcasted_iota(jnp.int32, shape, 1)


def project_kernel(count, rows, heads, chunks, hidden_ref, gain_ref, weight_ref, prompt_ref, *rest):
    own_ref, square_ref, mine_ref = rest[:3]
    sends = rest[3 : 2 + count]
    hidden_buf, gain_buf, weight_buf, total, squares, sems = rest[2 + count :]
    depth = hidden_ref.shape[1]
    size = depth // chunks
    width = weight_ref.shape[1]
    cached = prompt_ref.shape[0]
    gain_copy = pltpu.make_async_copy(gain_ref, gain_buf, sems.at[2 * chunks])
    gain_copy.start()
    columns = pl.ds(pl.multiple_of(lax.axis_index("set") * width, HEAD_SIZE), width)
    prompt_copy = pltpu.make_async_copy(prompt_ref.at[:, columns], mine_ref, sems.at[2 * chunks + 1])
    copies = []
    for c in range(chunks):
        part = pl.ds(c * size, size)
        copies.append(
            (
                pltpu.make_async_copy(hidden_ref.at[:, part], hidden_buf.at[:, part], sems.at[2 * c]),
                pltpu.make_async_copy(weight_ref.at[part, :], weight_buf.at[part, :], sems.at[2 * c + 1]),
            )
        )
        copies[-1][0].start()
        copies[-1][1].start()
    prompt_copy.start()
    gain_copy.wait()
    for c in range(chunks):
        copies[c][0].wait()
        folded, scaled = None, []
        for lane in range(c * size, (c + 1) * size, HEAD_SIZE):
            hidden = hidden_buf[:, lane : lane + HEAD_SIZE].astype(F32)
            tile = lane // HEAD_SIZE
            scaled.append((hidden * gain_buf[tile : tile + 1, :].astype(F32)).astype(BF16))
            square = hidden * hidden
            folded = square if folded is None else folded + square
        copies[c][1].wait()
        part = jnp.dot(
            jnp.concatenate(scaled, axis=1),
            weight_buf[c * size : (c + 1) * size, :],
            preferred_element_type=F32,
        )
        if c == 0:
            total[...] = part
            squares[...] = folded
        else:
            total[...] += part
            squares[...] += folded
    prompt_copy.wait()
    me = lax.axis_index("seq")
    for k in range(count):
        to = pl.ds(pl.multiple_of(peer(me, k, count) * rows, rows), rows)
        column = jnp.sum(squares[to, :], axis=1, keepdims=True)
        if k == 0:
            square_ref[...] = jnp.broadcast_to(column, (rows, HEAD_SIZE))
            out = own_ref
        else:
            out = sends[k - 1]
            line = jnp.sum(jnp.where(diagonal(rows), column, 0.0), axis=0, keepdims=True)
            high = line.astype(BF16).astype(F32)
            low = line - high
            which = lax.broadcasted_iota(jnp.int32, (16, HEAD_SIZE), 0)
            tail = jnp.where(which == 0, high, jnp.where(which == 1, low, 0.0))
            out[heads * rows : heads * rows + 16, :] = tail.astype(BF16)
            for h in range(heads):
                first = heads * rows + 16 + h * cached
                out[first : first + cached, :] = mine_ref[:, h * HEAD_SIZE : (h + 1) * HEAD_SIZE]
        for h in range(heads):
            piece = total[to, h * HEAD_SIZE : (h + 1) * HEAD_SIZE]
            out[h * rows : (h + 1) * rows, :] = piece.astype(out.dtype)


def project(span_hidden, norm_gain, key_value_weight, prompt_rows, count):
    length, depth = span_hidden.shape
    width = key_value_weight.shape[1]
    rows, heads = length // count, width // HEAD_SIZE
    cached = prompt_rows.shape[0]
    chunks = 4 if depth % (4 * HEAD_SIZE) == 0 else 1
    gain = norm_gain.reshape(-1, HEAD_SIZE)
    outs = [
        jax.ShapeDtypeStruct((heads * rows, HEAD_SIZE), F32),
        jax.ShapeDtypeStruct((rows, HEAD_SIZE), F32),
        jax.ShapeDtypeStruct((cached, width), BF16),
    ] + [jax.ShapeDtypeStruct((heads * (rows + cached) + 16, HEAD_SIZE), BF16)] * (count - 1)
    stay = [pltpu.with_memory_space_constraint(x, pltpu.HBM) for x in (span_hidden, gain, key_value_weight, prompt_rows)]
    return pl.pallas_call(
        functools.partial(project_kernel, count, rows, heads, chunks),
        in_specs=[HBM, HBM, HBM, HBM],
        out_shape=outs,
        out_specs=[VMEM] * len(outs),
        scratch_shapes=[
            pltpu.VMEM((length, depth), BF16),
            pltpu.VMEM(gain.shape, BF16),
            pltpu.VMEM((depth, width), BF16),
            pltpu.VMEM((length, width), F32),
            pltpu.VMEM((length, HEAD_SIZE), F32),
            pltpu.SemaphoreType.DMA((2 * chunks + 2,)),
        ],
        compiler_params=pltpu.CompilerParams(vmem_limit_bytes=16 << 20),
        cost_estimate=pl.CostEstimate(
            flops=2 * length * depth * width, bytes_accessed=2 * depth * (length + width), transcendentals=0
        ),
        name="project",
    )(*stay)


def combine_kernel(rows, heads, own_ref, square_ref, mine_ref, cosine_ref, sine_ref, *rest):
    got, (send_ref, prompt_ref) = rest[:-2], rest[-2:]
    cached = mine_ref.shape[0]
    count = 1 + len(got)
    me, first = lax.axis_index("seq"), lax.axis_index("set") * heads

    def prompt_rows(k):
        return pl.ds(pl.multiple_of(source(me, k, count) * cached, 16), cached)

    line = jnp.zeros((1, HEAD_SIZE), F32)
    for ref in got:
        tail = ref[heads * rows : heads * rows + 16, :].astype(F32)
        line = line + tail[0:1, :] + tail[1:2, :]
    column = jnp.sum(jnp.where(diagonal(rows), line, 0.0), axis=1, keepdims=True)
    scale = lax.rsqrt((square_ref[...] + column) / MODEL_WIDTH + EPS)
    cosine, sine = cosine_ref[...], sine_ref[...]
    for h in range(heads):
        span = slice(h * rows, (h + 1) * rows)
        lanes = slice(h * HEAD_SIZE, (h + 1) * HEAD_SIZE)
        value = own_ref[span, :]
        for ref in got:
            value = value + ref[span, :].astype(F32)
        value = value * scale
        out = jnp.where(first + h < KEY_HEADS, turn(value, cosine, sine), value).astype(BF16)
        send_ref[:, lanes] = out
        for i, ref in enumerate(got):
            start = heads * rows + 16 + h * cached
            prompt_ref[prompt_rows(count - 1 - i), lanes] = ref[start : start + cached, :]
    prompt_ref[prompt_rows(0), :] = mine_ref[...]


def combine(own, square, mine, cosine, sine, got):
    rows = square.shape[0]
    heads = own.shape[0] // rows
    block = pltpu.VMEM((rows, heads * HEAD_SIZE), BF16)
    prompt = jax.ShapeDtypeStruct(((1 + len(got)) * mine.shape[0], heads * HEAD_SIZE), BF16)
    return pl.pallas_call(
        functools.partial(combine_kernel, rows, heads),
        in_specs=[VMEM] * (5 + len(got)),
        out_shape=[block, prompt],
        out_specs=[VMEM, VMEM],
        compiler_params=pltpu.CompilerParams(vmem_limit_bytes=4 << 20),
        name="combine",
    )(own, square, mine, cosine, sine, *got)


def prepare_kernel(
    sets, tile, offset_ref, length_ref, frequency_ref, query_ref, own_ref, cosine_out, sine_out, query_out, state_out, mixed_out, key_buf, value_buf
):
    def table(rows, first):
        place = lax.broadcasted_iota(jnp.int32, (rows, HEAD_SIZE), 0) + first
        angles = place.astype(F32) * frequency_ref[...]
        front = lax.broadcasted_iota(jnp.int32, (rows, HEAD_SIZE), 1) < HEAD_SIZE // 2
        return jnp.cos(angles), jnp.where(front, -1.0, 1.0) * jnp.sin(angles)

    offset = offset_ref[0]
    rows, tokens = cosine_out.shape[0], query_ref.shape[0]
    cosine_out[...], sine_out[...] = table(rows, offset + lax.axis_index("seq") * rows)
    cosine, sine = table(tokens, offset + SPAN_LENGTH)
    for h in range(KEY_HEADS):
        span = slice(h * HEAD_SIZE, (h + 1) * HEAD_SIZE)
        key_buf[:, span] = turn(own_ref[:, span].astype(F32), cosine, sine).astype(BF16)
    value_buf[...] = own_ref[:, KEY_COLUMNS:]
    factor = HEAD_SIZE**-0.5 * math.log2(math.e)
    cosine, sine = cosine * factor, sine * factor
    for h in range(QUERY_HEADS):
        span = slice(h * HEAD_SIZE, (h + 1) * HEAD_SIZE)
        turned = turn(query_ref[:, span].astype(F32), cosine, sine)
        query_out[h * tokens : (h + 1) * tokens, :] = turned.astype(BF16)
    attend_kernel(
        None, sets, [(tokens, False)], tile, False, offset_ref, length_ref, query_out, key_buf, value_buf, state_out, mixed_out
    )


def state_shapes(block):
    return [
        jax.ShapeDtypeStruct((KEY_HEADS, 8, block), F32),
        jax.ShapeDtypeStruct((KEY_HEADS, HEAD_SIZE, block), F32),
    ]


def prepare(offset, length, cont_query, own_rows, sets, rows):
    tokens = cont_query.shape[0]
    block = GROUP * tokens
    table = jax.ShapeDtypeStruct((rows, HEAD_SIZE), F32)
    return pl.pallas_call(
        functools.partial(prepare_kernel, sets, block),
        in_specs=[SMEM, SMEM, VMEM, VMEM, VMEM],
        out_shape=[table, table, jax.ShapeDtypeStruct((QUERY_HEADS * tokens, HEAD_SIZE), BF16)] + state_shapes(block),
        out_specs=[VMEM] * 5,
        scratch_shapes=[pltpu.VMEM((tokens, KEY_COLUMNS), BF16)] * 2,
        compiler_params=pltpu.CompilerParams(vmem_limit_bytes=16 << 20),
        name="prepare",
    )(offset, length, frequencies(), cont_query, own_rows)


def attend_kernel(plan, sets, spans, tile, last, offset_ref, length_ref, query_ref, *rest):
    own = plan is None
    if own:
        key_ref, own_ref, state_out, mixed_out = rest
    else:
        operands = 1 + max(operand for stretch in plan for operand, _ in stretch.values())
        pieces, rest = rest[:operands], rest[operands:]
        if last:
            state_ref, mixed_ref, block_ref, final_ref, block_out, out_ref, sems = rest
        else:
            state_ref, mixed_ref, state_out, mixed_out = rest
    my_set = lax.axis_index("set")
    block = query_ref.shape[0] // KEY_HEADS
    tokens = block // GROUP
    offset, length = offset_ref[0], length_ref[0]
    total_rows = sum(rows for rows, _ in spans)
    bias = None
    if own:
        place = lax.broadcasted_iota(jnp.int32, (tokens, tokens), 0)
        token = lax.broadcasted_iota(jnp.int32, (tokens, tokens), 1)
        bias = jnp.concatenate([jnp.where(place <= token, 0.0, NEGATIVE_LARGE)] * (tile // tokens), axis=1)
    elif any(prompt for _, prompt in spans):
        parts = []
        for rows, prompt in spans:
            place = lax.broadcasted_iota(jnp.int32, (rows, HEAD_SIZE), 0)
            parts.append(jnp.where(place < offset, 0.0, NEGATIVE_LARGE) if prompt else jnp.zeros(place.shape, F32))
        bias = jnp.concatenate([jnp.concatenate(parts, axis=0)] * (tile // HEAD_SIZE), axis=1)
    keep = lax.broadcasted_iota(jnp.int32, (tokens, HEAD_SIZE), 0) < length
    units = [(g, start) for g in range(KEY_HEADS) for start in range(0, block, tile)]
    held, scored, weighed, mixtures, copies = {}, {}, {}, {}, []
    if last:
        block_copy = pltpu.make_async_copy(block_ref, block_out, sems.at[FLUSHES])
        block_copy.start()

    def rows_of(column):
        if column not in held:
            if own:
                ref = key_ref if column < KEY_COLUMNS else own_ref
                held[column] = ref[:, column % KEY_COLUMNS : column % KEY_COLUMNS + HEAD_SIZE]
                return held[column]
            width = pieces[0].shape[1]
            lanes = slice(column % width, column % width + HEAD_SIZE)
            parts = []
            for stretch, (rows, _) in zip(plan, spans):
                chosen = None
                for step, (operand, first) in stretch.items():
                    part = pieces[operand][first : first + rows, lanes]
                    here = source(my_set, step, sets) == column // width
                    chosen = part if chosen is None else jnp.where(here, part, chosen)
                parts.append(chosen)
            held[column] = jnp.concatenate(parts, axis=0)
        return held[column]

    def score(unit):
        g, start = unit
        query = query_ref[g * block + start : g * block + start + tile, :]
        key = rows_of(g * HEAD_SIZE)
        scores = lax.dot_general(key, query, (((1,), (1,)), ((), ())), preferred_element_type=F32)
        scored[unit] = scores if bias is None else scores + bias

    def weigh(unit):
        g, start = unit
        scores = scored.pop(unit)
        top, shrink = jnp.max(scores, axis=0, keepdims=True), None
        if not own:
            old = state_ref[g, 0:1, start : start + tile]
            top = jnp.maximum(old, top)
            shrink = jnp.exp2(old - top)
        weights = jnp.exp2(scores - top)
        total = jnp.sum(weights, axis=0, keepdims=True)
        if not own:
            total = total + state_ref[g, 1:2, start : start + tile] * shrink
        weighed[unit] = top, shrink, total
        mixtures[unit] = lax.dot_general(
            rows_of(KEY_COLUMNS + g * HEAD_SIZE),
            weights.astype(BF16),
            (((0,), (0,)), ((), ())),
            preferred_element_type=F32,
        )

    def finish(unit):
        g, start = unit
        top, shrink, total = weighed.pop(unit)
        mixed = mixtures.pop(unit)
        if not own:
            mixed = mixed + mixed_ref[g, :, start : start + tile] * shrink
        if last:
            mixed = (mixed * (1.0 / total)).astype(BF16).T
            for j in range(tile // tokens):
                column = (g * GROUP + start // tokens + j) * HEAD_SIZE
                piece = mixed[j * tokens : (j + 1) * tokens, :]
                out_ref[:, column : column + HEAD_SIZE] = jnp.where(keep, piece, jnp.zeros_like(piece))
        else:
            state_out[g, 0:1, start : start + tile] = top
            state_out[g, 1:2, start : start + tile] = total
            mixed_out[g, :, start : start + tile] = mixed

    flush = len(units) // FLUSHES
    for i in range(len(units) + 2):
        if i < len(units):
            score(units[i])
        if 0 <= i - 1 < len(units):
            weigh(units[i - 1])
        if 0 <= i - 2 < len(units):
            finish(units[i - 2])
            if last and (i - 1) % flush == 0:
                wide = out_ref.shape[1] // FLUSHES
                part = pl.ds(len(copies) * wide, wide)
                copies.append(pltpu.make_async_copy(out_ref.at[:, part], final_ref.at[:, part], sems.at[len(copies)]))
                copies[-1].start()
    for copy in copies:
        copy.wait()
    if last:
        block_copy.wait()


def attend(offset, length, query, sets, plan, spans, pieces, state, last=None):
    block = query.shape[0] // KEY_HEADS
    tokens = block // GROUP
    total_rows = sum(rows for rows, _ in spans)
    tile = block if total_rows % 128 else block // 2
    operands = [query] + list(pieces) + list(state) + ([] if last is None else [last])
    out_shape, scratch = state_shapes(block), []
    if last is not None:
        wide = (tokens, QUERY_HEADS * HEAD_SIZE)
        out_shape = [jax.ShapeDtypeStruct(wide, BF16), jax.ShapeDtypeStruct(last.shape, BF16)]
        scratch = [pltpu.VMEM(wide, BF16), pltpu.SemaphoreType.DMA((FLUSHES + 1,))]
    return pl.pallas_call(
        functools.partial(attend_kernel, plan, sets, spans, tile, last is not None),
        in_specs=[SMEM, SMEM] + [VMEM] * len(operands),
        out_shape=out_shape,
        out_specs=[VMEM, VMEM] if last is None else [HBM, HBM],
        scratch_shapes=scratch,
        compiler_params=pltpu.CompilerParams(vmem_limit_bytes=16 << 20),
        name="attend_more" if last is None else "attend_last",
    )(offset, length, *operands)


def on_device(
    span_hidden,
    norm_gain,
    key_value_weight,
    prompt_key_value,
    span_offset,
    cont_query,
    continuation_key_value,
    cont_lengths,
):
    sets, count = lax.axis_size("set"), lax.axis_size("seq")
    rows = span_hidden.shape[0] // count
    low = 2 if sets % 2 == 0 else 1

    own, square, mine, *sends = project(span_hidden, norm_gain, key_value_weight, prompt_key_value, count)
    order = list(range(count - 1, 0, -1))
    got = [exchange(sends[k - 1], "seq", k) for k in order]

    cosine, sine, query, *state = prepare(
        span_offset, cont_lengths, cont_query[0], continuation_key_value[0], sets, rows
    )
    block, prompt = combine(own, square, mine, cosine, sine, got)

    far = list(range(low, sets, low))
    steps = [0] + far
    half = max(1, (count - 1) // 2)
    beside = [exchange(block, "set", step) for step in far]
    across = [exchange(block, "seq", k) for k in order[:half]]
    both = jnp.concatenate([block] + beside, axis=0)
    together = [exchange(both, "seq", k) for k in order[half:]]
    prompts = [prompt] + [exchange(prompt, "set", step) for step in far]
    stretches = [[block] + beside]
    for arrived in across:
        stretches.append([arrived] + [exchange(arrived, "set", step) for step in far])
    stretches += [[arrived] for arrived in together]

    def share(values, spans):
        plan, pieces = [], []
        for lines, (size, _) in zip(values, spans):
            whole = len(lines) == 1
            plan.append({step: (len(pieces) + (0 if whole else n), n * size if whole else 0) for n, step in enumerate(steps)})
            pieces += lines
        if low == 2:
            other = exchange(jnp.concatenate([line for lines in values for line in lines], axis=0), "set", 1)
            first = 0
            for stretch, (size, _) in zip(plan, spans):
                for step in steps:
                    stretch[step ^ 1] = (len(pieces), first)
                    first += size
            pieces.append(other)
        return dict(plan=plan, pieces=pieces, spans=spans)

    ends = span_offset, cont_lengths
    near = share([stretches[0], prompts], [(rows, False), (prompt.shape[0], True)])
    state = attend(*ends, query, sets, state=state, **near)
    rest = stretches[1:]
    attended, block = attend(*ends, query, sets, state=state, last=block, **share(rest, [(rows, False)] * len(rest)))
    return block, attended[None]


def solution(mesh):
    placed = (
        P("parts", "seq"),
        P("seq"),
        P("seq", "set"),
        P(("parts", "seq"), None),
        P("parts"),
        P(("parts", "set", "seq"), None, None),
        P(("parts", "set", "seq"), None, None),
        P(("parts", "set", "seq")),
    )
    return jax.shard_map(
        on_device,
        mesh=mesh,
        in_specs=placed,
        out_specs=(P(("parts", "seq"), "set"), P(("parts", "set", "seq"), None, None)),
        check_vma=False,
    )
```

```python
import functools
import math

import jax
import jax.numpy as jnp
import numpy as np
from jax import lax
from jax.experimental import pallas as pl
from jax.experimental.pallas import tpu as pltpu
from jax.sharding import PartitionSpec as P

MODEL_WIDTH = 8192
QUERY_HEADS = 64
KEY_HEADS = 8
HEAD_SIZE = 128
SPAN_LENGTH = 256
EPS = 1e-05
NEGATIVE_LARGE = -1e30
GROUP = QUERY_HEADS // KEY_HEADS
KEY_COLUMNS = KEY_HEADS * HEAD_SIZE
BF16 = jnp.bfloat16
F32 = jnp.float32
FLUSHES = 4
SMEM = pl.BlockSpec(memory_space=pltpu.SMEM)
VMEM = pl.BlockSpec(memory_space=pltpu.VMEM)
HBM = pl.BlockSpec(memory_space=pltpu.HBM)


def peer(index, step, count):
    if count & (count - 1) == 0:
        return index ^ step
    return (index + step) % count


def source(index, step, count):
    if count & (count - 1) == 0:
        return index ^ step
    return (index + count - step) % count


def exchange(value, axis, step):
    count = lax.axis_size(axis)
    return lax.ppermute(value, axis, [(i, peer(i, step, count)) for i in range(count)])


def frequencies():
    base = 500000.0 ** (-(np.arange(HEAD_SIZE // 2) * 2.0) / HEAD_SIZE)
    wave = 2.0 * math.pi / base
    smooth = (8192.0 / wave - 1.0) / 3.0
    blended = (1.0 - smooth) * base / 8.0 + smooth * base
    rescaled = np.where(wave < 2048.0, base, np.where(wave > 8192.0, base / 8.0, blended))
    return jnp.asarray(np.tile(rescaled, 2)[None], F32)


def turn(value, cosine, sine):
    return value * cosine + pltpu.roll(value, HEAD_SIZE // 2, 1) * sine


def diagonal(rows):
    shape = (rows, HEAD_SIZE)
    return lax.broadcasted_iota(jnp.int32, shape, 0) == lax.broadcasted_iota(jnp.int32, shape, 1)


def project_kernel(count, rows, heads, chunks, hidden_ref, gain_ref, weight_ref, prompt_ref, *rest):
    own_ref, square_ref, mine_ref = rest[:3]
    sends = rest[3 : 2 + count]
    hidden_buf, gain_buf, weight_buf, total, squares, sems = rest[2 + count :]
    depth = hidden_ref.shape[1]
    size = depth // chunks
    width = weight_ref.shape[1]
    cached = prompt_ref.shape[0]
    gain_copy = pltpu.make_async_copy(gain_ref, gain_buf, sems.at[2 * chunks])
    gain_copy.start()
    columns = pl.ds(pl.multiple_of(lax.axis_index("set") * width, HEAD_SIZE), width)
    prompt_copy = pltpu.make_async_copy(prompt_ref.at[:, columns], mine_ref, sems.at[2 * chunks + 1])
    copies = []
    for c in range(chunks):
        part = pl.ds(c * size, size)
        copies.append(
            (
                pltpu.make_async_copy(hidden_ref.at[:, part], hidden_buf.at[:, part], sems.at[2 * c]),
                pltpu.make_async_copy(weight_ref.at[part, :], weight_buf.at[part, :], sems.at[2 * c + 1]),
            )
        )
        copies[-1][0].start()
        copies[-1][1].start()
    prompt_copy.start()
    gain_copy.wait()
    for c in range(chunks):
        copies[c][0].wait()
        folded, scaled = None, []
        for lane in range(c * size, (c + 1) * size, HEAD_SIZE):
            hidden = hidden_buf[:, lane : lane + HEAD_SIZE].astype(F32)
            tile = lane // HEAD_SIZE
            scaled.append((hidden * gain_buf[tile : tile + 1, :].astype(F32)).astype(BF16))
            square = hidden * hidden
            folded = square if folded is None else folded + square
        copies[c][1].wait()
        part = jnp.dot(
            jnp.concatenate(scaled, axis=1),
            weight_buf[c * size : (c + 1) * size, :],
            preferred_element_type=F32,
        )
        if c == 0:
            total[...] = part
            squares[...] = folded
        else:
            total[...] += part
            squares[...] += folded
    prompt_copy.wait()
    me = lax.axis_index("seq")
    for k in range(count):
        to = pl.ds(pl.multiple_of(peer(me, k, count) * rows, rows), rows)
        column = jnp.sum(squares[to, :], axis=1, keepdims=True)
        if k == 0:
            square_ref[...] = jnp.broadcast_to(column, (rows, HEAD_SIZE))
            out = own_ref
        else:
            out = sends[k - 1]
            line = jnp.sum(jnp.where(diagonal(rows), column, 0.0), axis=0, keepdims=True)
            high = line.astype(BF16).astype(F32)
            low = line - high
            which = lax.broadcasted_iota(jnp.int32, (16, HEAD_SIZE), 0)
            tail = jnp.where(which == 0, high, jnp.where(which == 1, low, 0.0))
            out[heads * rows : heads * rows + 16, :] = tail.astype(BF16)
            for h in range(heads):
                first = heads * rows + 16 + h * cached
                out[first : first + cached, :] = mine_ref[:, h * HEAD_SIZE : (h + 1) * HEAD_SIZE]
        for h in range(heads):
            piece = total[to, h * HEAD_SIZE : (h + 1) * HEAD_SIZE]
            out[h * rows : (h + 1) * rows, :] = piece.astype(out.dtype)


def project(span_hidden, norm_gain, key_value_weight, prompt_rows, count):
    length, depth = span_hidden.shape
    width = key_value_weight.shape[1]
    rows, heads = length // count, width // HEAD_SIZE
    cached = prompt_rows.shape[0]
    chunks = 4 if depth % (4 * HEAD_SIZE) == 0 else 1
    gain = norm_gain.reshape(-1, HEAD_SIZE)
    outs = [
        jax.ShapeDtypeStruct((heads * rows, HEAD_SIZE), F32),
        jax.ShapeDtypeStruct((rows, HEAD_SIZE), F32),
        jax.ShapeDtypeStruct((cached, width), BF16),
    ] + [jax.ShapeDtypeStruct((heads * (rows + cached) + 16, HEAD_SIZE), BF16)] * (count - 1)
    stay = [pltpu.with_memory_space_constraint(x, pltpu.HBM) for x in (span_hidden, gain, key_value_weight, prompt_rows)]
    return pl.pallas_call(
        functools.partial(project_kernel, count, rows, heads, chunks),
        in_specs=[HBM, HBM, HBM, HBM],
        out_shape=outs,
        out_specs=[VMEM] * len(outs),
        scratch_shapes=[
            pltpu.VMEM((length, depth), BF16),
            pltpu.VMEM(gain.shape, BF16),
            pltpu.VMEM((depth, width), BF16),
            pltpu.VMEM((length, width), F32),
            pltpu.VMEM((length, HEAD_SIZE), F32),
            pltpu.SemaphoreType.DMA((2 * chunks + 2,)),
        ],
        compiler_params=pltpu.CompilerParams(vmem_limit_bytes=16 << 20),
        cost_estimate=pl.CostEstimate(
            flops=2 * length * depth * width, bytes_accessed=2 * depth * (length + width), transcendentals=0
        ),
        name="project",
    )(*stay)


def combine_kernel(rows, heads, order, own_ref, square_ref, mine_ref, cosine_ref, sine_ref, *rest):
    got, (send_ref, prompt_ref) = rest[:-2], rest[-2:]
    cached = mine_ref.shape[0]
    count = 1 + len(got)
    me, first = lax.axis_index("seq"), lax.axis_index("set") * heads

    def prompt_rows(k):
        return pl.ds(pl.multiple_of(source(me, k, count) * cached, 16), cached)

    line = jnp.zeros((1, HEAD_SIZE), F32)
    for ref in got:
        tail = ref[heads * rows : heads * rows + 16, :].astype(F32)
        line = line + tail[0:1, :] + tail[1:2, :]
    column = jnp.sum(jnp.where(diagonal(rows), line, 0.0), axis=1, keepdims=True)
    scale = lax.rsqrt((square_ref[...] + column) / MODEL_WIDTH + EPS)
    cosine, sine = cosine_ref[...], sine_ref[...]
    for h in range(heads):
        span = slice(h * rows, (h + 1) * rows)
        lanes = slice(h * HEAD_SIZE, (h + 1) * HEAD_SIZE)
        value = own_ref[span, :]
        for ref in got:
            value = value + ref[span, :].astype(F32)
        value = value * scale
        out = jnp.where(first + h < KEY_HEADS, turn(value, cosine, sine), value).astype(BF16)
        send_ref[:, lanes] = out
        for i, ref in enumerate(got):
            start = heads * rows + 16 + h * cached
            prompt_ref[prompt_rows(order[i]), lanes] = ref[start : start + cached, :]
    prompt_ref[prompt_rows(0), :] = mine_ref[...]


def combine(own, square, mine, cosine, sine, got, order):
    rows = square.shape[0]
    heads = own.shape[0] // rows
    block = pltpu.VMEM((rows, heads * HEAD_SIZE), BF16)
    prompt = jax.ShapeDtypeStruct(((1 + len(got)) * mine.shape[0], heads * HEAD_SIZE), BF16)
    return pl.pallas_call(
        functools.partial(combine_kernel, rows, heads, order),
        in_specs=[VMEM] * (5 + len(got)),
        out_shape=[block, prompt],
        out_specs=[VMEM, VMEM],
        compiler_params=pltpu.CompilerParams(vmem_limit_bytes=4 << 20),
        name="combine",
    )(own, square, mine, cosine, sine, *got)


def prepare_kernel(
    sets, tile, offset_ref, length_ref, frequency_ref, query_ref, own_ref, cosine_out, sine_out, query_out, state_out, mixed_out, key_buf, value_buf
):
    def table(rows, first):
        place = lax.broadcasted_iota(jnp.int32, (rows, HEAD_SIZE), 0) + first
        angles = place.astype(F32) * frequency_ref[...]
        front = lax.broadcasted_iota(jnp.int32, (rows, HEAD_SIZE), 1) < HEAD_SIZE // 2
        return jnp.cos(angles), jnp.where(front, -1.0, 1.0) * jnp.sin(angles)

    offset = offset_ref[0]
    rows, tokens = cosine_out.shape[0], query_ref.shape[0]
    cosine_out[...], sine_out[...] = table(rows, offset + lax.axis_index("seq") * rows)
    cosine, sine = table(tokens, offset + SPAN_LENGTH)
    for h in range(KEY_HEADS):
        span = slice(h * HEAD_SIZE, (h + 1) * HEAD_SIZE)
        key_buf[:, span] = turn(own_ref[:, span].astype(F32), cosine, sine).astype(BF16)
    value_buf[...] = own_ref[:, KEY_COLUMNS:]
    factor = HEAD_SIZE**-0.5 * math.log2(math.e)
    cosine, sine = cosine * factor, sine * factor
    for h in range(QUERY_HEADS):
        span = slice(h * HEAD_SIZE, (h + 1) * HEAD_SIZE)
        turned = turn(query_ref[:, span].astype(F32), cosine, sine)
        query_out[h * tokens : (h + 1) * tokens, :] = turned.astype(BF16)
    attend_kernel(
        None, sets, [(tokens, False)], tile, False, offset_ref, length_ref, query_out, key_buf, value_buf, state_out, mixed_out
    )


def state_shapes(block):
    return [
        jax.ShapeDtypeStruct((KEY_HEADS, 8, block), F32),
        jax.ShapeDtypeStruct((KEY_HEADS, HEAD_SIZE, block), F32),
    ]


def prepare(offset, length, cont_query, own_rows, sets, rows):
    tokens = cont_query.shape[0]
    block = GROUP * tokens
    table = jax.ShapeDtypeStruct((rows, HEAD_SIZE), F32)
    return pl.pallas_call(
        functools.partial(prepare_kernel, sets, block),
        in_specs=[SMEM, SMEM, VMEM, VMEM, VMEM],
        out_shape=[table, table, jax.ShapeDtypeStruct((QUERY_HEADS * tokens, HEAD_SIZE), BF16)] + state_shapes(block),
        out_specs=[VMEM] * 5,
        scratch_shapes=[pltpu.VMEM((tokens, KEY_COLUMNS), BF16)] * 2,
        compiler_params=pltpu.CompilerParams(vmem_limit_bytes=16 << 20),
        name="prepare",
    )(offset, length, frequencies(), cont_query, own_rows)


def attend_kernel(plan, sets, spans, tile, last, offset_ref, length_ref, query_ref, *rest):
    own = plan is None
    if own:
        key_ref, own_ref, state_out, mixed_out = rest
    else:
        operands = 1 + max(operand for stretch in plan for operand, _ in stretch.values())
        pieces, rest = rest[:operands], rest[operands:]
        if last:
            state_ref, mixed_ref, block_ref, final_ref, block_out, out_ref, sems = rest
        else:
            state_ref, mixed_ref, state_out, mixed_out = rest
    my_set = lax.axis_index("set")
    block = query_ref.shape[0] // KEY_HEADS
    tokens = block // GROUP
    offset, length = offset_ref[0], length_ref[0]
    total_rows = sum(rows for rows, _ in spans)
    bias = None
    if own:
        place = lax.broadcasted_iota(jnp.int32, (tokens, tokens), 0)
        token = lax.broadcasted_iota(jnp.int32, (tokens, tokens), 1)
        bias = jnp.concatenate([jnp.where(place <= token, 0.0, NEGATIVE_LARGE)] * (tile // tokens), axis=1)
    elif any(prompt for _, prompt in spans):
        parts = []
        for rows, prompt in spans:
            place = lax.broadcasted_iota(jnp.int32, (rows, HEAD_SIZE), 0)
            parts.append(jnp.where(place < offset, 0.0, NEGATIVE_LARGE) if prompt else jnp.zeros(place.shape, F32))
        bias = jnp.concatenate([jnp.concatenate(parts, axis=0)] * (tile // HEAD_SIZE), axis=1)
    keep = lax.broadcasted_iota(jnp.int32, (tokens, HEAD_SIZE), 0) < length
    units = [(g, start) for g in range(KEY_HEADS) for start in range(0, block, tile)]
    held, scored, weighed, mixtures, copies = {}, {}, {}, {}, []
    if last:
        block_copy = pltpu.make_async_copy(block_ref, block_out, sems.at[FLUSHES])
        block_copy.start()

    def rows_of(column):
        if column not in held:
            if own:
                ref = key_ref if column < KEY_COLUMNS else own_ref
                held[column] = ref[:, column % KEY_COLUMNS : column % KEY_COLUMNS + HEAD_SIZE]
                return held[column]
            width = pieces[0].shape[1]
            lanes = slice(column % width, column % width + HEAD_SIZE)
            parts = []
            for stretch, (rows, _) in zip(plan, spans):
                chosen = None
                for step, (operand, first) in stretch.items():
                    part = pieces[operand][first : first + rows, lanes]
                    here = source(my_set, step, sets) == column // width
                    chosen = part if chosen is None else jnp.where(here, part, chosen)
                parts.append(chosen)
            held[column] = jnp.concatenate(parts, axis=0)
        return held[column]

    def score(unit):
        g, start = unit
        query = query_ref[g * block + start : g * block + start + tile, :]
        key = rows_of(g * HEAD_SIZE)
        scores = lax.dot_general(key, query, (((1,), (1,)), ((), ())), preferred_element_type=F32)
        scored[unit] = scores if bias is None else scores + bias

    def weigh(unit):
        g, start = unit
        scores = scored.pop(unit)
        top, shrink = jnp.max(scores, axis=0, keepdims=True), None
        if not own:
            old = state_ref[g, 0:1, start : start + tile]
            top = jnp.maximum(old, top)
            shrink = jnp.exp2(old - top)
        weights = jnp.exp2(scores - top)
        total = jnp.sum(weights, axis=0, keepdims=True)
        if not own:
            total = total + state_ref[g, 1:2, start : start + tile] * shrink
        weighed[unit] = top, shrink, total
        mixtures[unit] = lax.dot_general(
            rows_of(KEY_COLUMNS + g * HEAD_SIZE),
            weights.astype(BF16),
            (((0,), (0,)), ((), ())),
            preferred_element_type=F32,
        )

    def finish(unit):
        g, start = unit
        top, shrink, total = weighed.pop(unit)
        mixed = mixtures.pop(unit)
        if not own:
            mixed = mixed + mixed_ref[g, :, start : start + tile] * shrink
        if last:
            mixed = (mixed * (1.0 / total)).astype(BF16).T
            for j in range(tile // tokens):
                column = (g * GROUP + start // tokens + j) * HEAD_SIZE
                piece = mixed[j * tokens : (j + 1) * tokens, :]
                out_ref[:, column : column + HEAD_SIZE] = jnp.where(keep, piece, jnp.zeros_like(piece))
        else:
            state_out[g, 0:1, start : start + tile] = top
            state_out[g, 1:2, start : start + tile] = total
            mixed_out[g, :, start : start + tile] = mixed

    flush = len(units) // FLUSHES
    for i in range(len(units) + 2):
        if i < len(units):
            score(units[i])
        if 0 <= i - 1 < len(units):
            weigh(units[i - 1])
        if 0 <= i - 2 < len(units):
            finish(units[i - 2])
            if last and (i - 1) % flush == 0:
                wide = out_ref.shape[1] // FLUSHES
                part = pl.ds(len(copies) * wide, wide)
                copies.append(pltpu.make_async_copy(out_ref.at[:, part], final_ref.at[:, part], sems.at[len(copies)]))
                copies[-1].start()
    for copy in copies:
        copy.wait()
    if last:
        block_copy.wait()


def attend(offset, length, query, sets, plan, spans, pieces, state, last=None):
    block = query.shape[0] // KEY_HEADS
    tokens = block // GROUP
    total_rows = sum(rows for rows, _ in spans)
    tile = block if total_rows % 128 else block // 2
    operands = [query] + list(pieces) + list(state) + ([] if last is None else [last])
    out_shape, scratch = state_shapes(block), []
    if last is not None:
        wide = (tokens, QUERY_HEADS * HEAD_SIZE)
        out_shape = [jax.ShapeDtypeStruct(wide, BF16), jax.ShapeDtypeStruct(last.shape, BF16)]
        scratch = [pltpu.VMEM(wide, BF16), pltpu.SemaphoreType.DMA((FLUSHES + 1,))]
    return pl.pallas_call(
        functools.partial(attend_kernel, plan, sets, spans, tile, last is not None),
        in_specs=[SMEM, SMEM] + [VMEM] * len(operands),
        out_shape=out_shape,
        out_specs=[VMEM, VMEM] if last is None else [HBM, HBM],
        scratch_shapes=scratch,
        compiler_params=pltpu.CompilerParams(vmem_limit_bytes=16 << 20),
        name="attend_more" if last is None else "attend_last",
    )(offset, length, *operands)


def on_device(
    span_hidden,
    norm_gain,
    key_value_weight,
    prompt_key_value,
    span_offset,
    cont_query,
    continuation_key_value,
    cont_lengths,
):
    sets, count = lax.axis_size("set"), lax.axis_size("seq")
    rows = span_hidden.shape[0] // count
    low = 2 if sets % 2 == 0 else 1

    own, square, mine, *sends = project(span_hidden, norm_gain, key_value_weight, prompt_key_value, count)
    order = list(range(count - 1, 0, -1))
    sums = order[1:] + order[:1]
    got = [exchange(sends[k - 1], "seq", k) for k in sums]

    cosine, sine, query, *state = prepare(
        span_offset, cont_lengths, cont_query[0], continuation_key_value[0], sets, rows
    )
    block, prompt = combine(own, square, mine, cosine, sine, got, sums)

    far = list(range(low, sets, low))
    steps = [0] + far
    half = max(1, (count - 1) // 2)
    beside = [exchange(block, "set", step) for step in far]
    across = [exchange(block, "seq", k) for k in order[:half]]
    both = jnp.concatenate([block] + beside, axis=0)
    together = [exchange(both, "seq", k) for k in reversed(order[half:])]
    prompts = [prompt] + [exchange(prompt, "set", step) for step in far]
    stretches = [[block] + beside]
    for arrived in across:
        stretches.append([arrived] + [exchange(arrived, "set", step) for step in far])
    stretches += [[arrived] for arrived in together]

    def share(values, spans):
        plan, pieces = [], []
        for lines, (size, _) in zip(values, spans):
            whole = len(lines) == 1
            plan.append({step: (len(pieces) + (0 if whole else n), n * size if whole else 0) for n, step in enumerate(steps)})
            pieces += lines
        if low == 2:
            other = exchange(jnp.concatenate([line for lines in values for line in lines], axis=0), "set", 1)
            first = 0
            for stretch, (size, _) in zip(plan, spans):
                for step in steps:
                    stretch[step ^ 1] = (len(pieces), first)
                    first += size
            pieces.append(other)
        return dict(plan=plan, pieces=pieces, spans=spans)

    ends = span_offset, cont_lengths
    near = share([stretches[0], prompts], [(rows, False), (prompt.shape[0], True)])
    state = attend(*ends, query, sets, state=state, **near)
    rest = stretches[1:]
    attended, block = attend(*ends, query, sets, state=state, last=block, **share(rest, [(rows, False)] * len(rest)))
    return block, attended[None]


def solution(mesh):
    placed = (
        P("parts", "seq"),
        P("seq"),
        P("seq", "set"),
        P(("parts", "seq"), None),
        P("parts"),
        P(("parts", "set", "seq"), None, None),
        P(("parts", "set", "seq"), None, None),
        P(("parts", "set", "seq")),
    )
    return jax.shard_map(
        on_device,
        mesh=mesh,
        in_specs=placed,
        out_specs=(P(("parts", "seq"), "set"), P(("parts", "set", "seq"), None, None)),
        check_vma=False,
    )
```

```python
import functools
import math

import jax
import jax.numpy as jnp
import numpy as np
from jax import lax
from jax.experimental import pallas as pl
from jax.experimental.pallas import tpu as pltpu
from jax.sharding import PartitionSpec as P

MODEL_WIDTH = 8192
QUERY_HEADS = 64
KEY_HEADS = 8
HEAD_SIZE = 128
SPAN_LENGTH = 256
EPS = 1e-05
NEGATIVE_LARGE = -1e30
GROUP = QUERY_HEADS // KEY_HEADS
KEY_COLUMNS = KEY_HEADS * HEAD_SIZE
BF16 = jnp.bfloat16
F32 = jnp.float32
FLUSHES = 4
SMEM = pl.BlockSpec(memory_space=pltpu.SMEM)
VMEM = pl.BlockSpec(memory_space=pltpu.VMEM)
HBM = pl.BlockSpec(memory_space=pltpu.HBM)


def peer(index, step, count):
    if count & (count - 1) == 0:
        return index ^ step
    return (index + step) % count


def source(index, step, count):
    if count & (count - 1) == 0:
        return index ^ step
    return (index + count - step) % count


def exchange(value, axis, step):
    count = lax.axis_size(axis)
    return lax.ppermute(value, axis, [(i, peer(i, step, count)) for i in range(count)])


def frequencies():
    base = 500000.0 ** (-(np.arange(HEAD_SIZE // 2) * 2.0) / HEAD_SIZE)
    wave = 2.0 * math.pi / base
    smooth = (8192.0 / wave - 1.0) / 3.0
    blended = (1.0 - smooth) * base / 8.0 + smooth * base
    rescaled = np.where(wave < 2048.0, base, np.where(wave > 8192.0, base / 8.0, blended))
    return jnp.asarray(np.tile(rescaled, 2)[None], F32)


def turn(value, cosine, sine):
    return value * cosine + pltpu.roll(value, HEAD_SIZE // 2, 1) * sine


def diagonal(rows):
    shape = (rows, HEAD_SIZE)
    return lax.broadcasted_iota(jnp.int32, shape, 0) == lax.broadcasted_iota(jnp.int32, shape, 1)


def project_kernel(count, rows, heads, chunks, hidden_ref, gain_ref, weight_ref, prompt_ref, *rest):
    own_ref, square_ref, mine_ref = rest[:3]
    sends = rest[3 : 2 + count]
    hidden_buf, gain_buf, weight_buf, total, squares, sems = rest[2 + count :]
    depth = hidden_ref.shape[1]
    size = depth // chunks
    width = weight_ref.shape[1]
    cached = prompt_ref.shape[0]
    gain_copy = pltpu.make_async_copy(gain_ref, gain_buf, sems.at[2 * chunks])
    gain_copy.start()
    columns = pl.ds(pl.multiple_of(lax.axis_index("set") * width, HEAD_SIZE), width)
    prompt_copy = pltpu.make_async_copy(prompt_ref.at[:, columns], mine_ref, sems.at[2 * chunks + 1])
    copies = []
    for c in range(chunks):
        part = pl.ds(c * size, size)
        copies.append(
            (
                pltpu.make_async_copy(hidden_ref.at[:, part], hidden_buf.at[:, part], sems.at[2 * c]),
                pltpu.make_async_copy(weight_ref.at[part, :], weight_buf.at[part, :], sems.at[2 * c + 1]),
            )
        )
        copies[-1][0].start()
        copies[-1][1].start()
    prompt_copy.start()
    gain_copy.wait()
    for c in range(chunks):
        copies[c][0].wait()
        folded, scaled = None, []
        for lane in range(c * size, (c + 1) * size, HEAD_SIZE):
            hidden = hidden_buf[:, lane : lane + HEAD_SIZE].astype(F32)
            tile = lane // HEAD_SIZE
            scaled.append((hidden * gain_buf[tile : tile + 1, :].astype(F32)).astype(BF16))
            square = hidden * hidden
            folded = square if folded is None else folded + square
        copies[c][1].wait()
        part = jnp.dot(
            jnp.concatenate(scaled, axis=1),
            weight_buf[c * size : (c + 1) * size, :],
            preferred_element_type=F32,
        )
        if c == 0:
            total[...] = part
            squares[...] = folded
        else:
            total[...] += part
            squares[...] += folded
    prompt_copy.wait()
    me = lax.axis_index("seq")
    for k in range(count):
        to = pl.ds(pl.multiple_of(lax.rem(me + k, count) * rows, rows), rows)
        column = jnp.sum(squares[to, :], axis=1, keepdims=True)
        if k == 0:
            square_ref[...] = jnp.broadcast_to(column, (rows, HEAD_SIZE))
            out = own_ref
        else:
            out = sends[k - 1]
            line = jnp.sum(jnp.where(diagonal(rows), column, 0.0), axis=0, keepdims=True)
            high = line.astype(BF16).astype(F32)
            low = line - high
            which = lax.broadcasted_iota(jnp.int32, (16, HEAD_SIZE), 0)
            tail = jnp.where(which == 0, high, jnp.where(which == 1, low, 0.0))
            out[heads * rows : heads * rows + 16, :] = tail.astype(BF16)
            for h in range(heads):
                first = heads * rows + 16 + h * cached
                out[first : first + cached, :] = mine_ref[:, h * HEAD_SIZE : (h + 1) * HEAD_SIZE]
        for h in range(heads):
            piece = total[to, h * HEAD_SIZE : (h + 1) * HEAD_SIZE]
            out[h * rows : (h + 1) * rows, :] = piece.astype(out.dtype)


def project(span_hidden, norm_gain, key_value_weight, prompt_rows, count):
    length, depth = span_hidden.shape
    width = key_value_weight.shape[1]
    rows, heads = length // count, width // HEAD_SIZE
    cached = prompt_rows.shape[0]
    chunks = 4 if depth % (4 * HEAD_SIZE) == 0 else 1
    gain = norm_gain.reshape(-1, HEAD_SIZE)
    outs = [
        jax.ShapeDtypeStruct((heads * rows, HEAD_SIZE), F32),
        jax.ShapeDtypeStruct((rows, HEAD_SIZE), F32),
        jax.ShapeDtypeStruct((cached, width), BF16),
    ] + [jax.ShapeDtypeStruct((heads * (rows + cached) + 16, HEAD_SIZE), BF16)] * (count - 1)
    stay = [pltpu.with_memory_space_constraint(x, pltpu.HBM) for x in (span_hidden, gain, key_value_weight, prompt_rows)]
    return pl.pallas_call(
        functools.partial(project_kernel, count, rows, heads, chunks),
        in_specs=[HBM, HBM, HBM, HBM],
        out_shape=outs,
        out_specs=[VMEM] * len(outs),
        scratch_shapes=[
            pltpu.VMEM((length, depth), BF16),
            pltpu.VMEM(gain.shape, BF16),
            pltpu.VMEM((depth, width), BF16),
            pltpu.VMEM((length, width), F32),
            pltpu.VMEM((length, HEAD_SIZE), F32),
            pltpu.SemaphoreType.DMA((2 * chunks + 2,)),
        ],
        compiler_params=pltpu.CompilerParams(vmem_limit_bytes=16 << 20),
        cost_estimate=pl.CostEstimate(
            flops=2 * length * depth * width, bytes_accessed=2 * depth * (length + width), transcendentals=0
        ),
        name="project",
    )(*stay)


def combine_kernel(rows, heads, order, own_ref, square_ref, mine_ref, cosine_ref, sine_ref, *rest):
    got, (send_ref, prompt_ref) = rest[:-2], rest[-2:]
    cached = mine_ref.shape[0]
    count = 1 + len(got)
    me, first = lax.axis_index("seq"), lax.axis_index("set") * heads

    def prompt_rows(k):
        return pl.ds(pl.multiple_of(lax.rem(me + count - k, count) * cached, 16), cached)

    line = jnp.zeros((1, HEAD_SIZE), F32)
    for ref in got:
        tail = ref[heads * rows : heads * rows + 16, :].astype(F32)
        line = line + tail[0:1, :] + tail[1:2, :]
    column = jnp.sum(jnp.where(diagonal(rows), line, 0.0), axis=1, keepdims=True)
    scale = lax.rsqrt((square_ref[...] + column) / MODEL_WIDTH + EPS)
    cosine, sine = cosine_ref[...], sine_ref[...]
    for h in range(heads):
        span = slice(h * rows, (h + 1) * rows)
        lanes = slice(h * HEAD_SIZE, (h + 1) * HEAD_SIZE)
        value = own_ref[span, :]
        for ref in got:
            value = value + ref[span, :].astype(F32)
        value = value * scale
        out = jnp.where(first + h < KEY_HEADS, turn(value, cosine, sine), value).astype(BF16)
        send_ref[:, lanes] = out
        for i, ref in enumerate(got):
            start = heads * rows + 16 + h * cached
            prompt_ref[prompt_rows(order[i]), lanes] = ref[start : start + cached, :]
    prompt_ref[prompt_rows(0), :] = mine_ref[...]


def combine(own, square, mine, cosine, sine, got, order):
    rows = square.shape[0]
    heads = own.shape[0] // rows
    block = pltpu.VMEM((rows, heads * HEAD_SIZE), BF16)
    prompt = jax.ShapeDtypeStruct(((1 + len(got)) * mine.shape[0], heads * HEAD_SIZE), BF16)
    return pl.pallas_call(
        functools.partial(combine_kernel, rows, heads, order),
        in_specs=[VMEM] * (5 + len(got)),
        out_shape=[block, prompt],
        out_specs=[VMEM, VMEM],
        compiler_params=pltpu.CompilerParams(vmem_limit_bytes=4 << 20),
        name="combine",
    )(own, square, mine, cosine, sine, *got)


def prepare_kernel(
    sets, tile, offset_ref, length_ref, frequency_ref, query_ref, own_ref, cosine_out, sine_out, query_out, state_out, mixed_out, key_buf, value_buf
):
    def table(rows, first):
        place = lax.broadcasted_iota(jnp.int32, (rows, HEAD_SIZE), 0) + first
        angles = place.astype(F32) * frequency_ref[...]
        front = lax.broadcasted_iota(jnp.int32, (rows, HEAD_SIZE), 1) < HEAD_SIZE // 2
        return jnp.cos(angles), jnp.where(front, -1.0, 1.0) * jnp.sin(angles)

    offset = offset_ref[0]
    rows, tokens = cosine_out.shape[0], query_ref.shape[0]
    cosine_out[...], sine_out[...] = table(rows, offset + lax.axis_index("seq") * rows)
    cosine, sine = table(tokens, offset + SPAN_LENGTH)
    for h in range(KEY_HEADS):
        span = slice(h * HEAD_SIZE, (h + 1) * HEAD_SIZE)
        key_buf[:, span] = turn(own_ref[:, span].astype(F32), cosine, sine).astype(BF16)
    value_buf[...] = own_ref[:, KEY_COLUMNS:]
    factor = HEAD_SIZE**-0.5 * math.log2(math.e)
    cosine, sine = cosine * factor, sine * factor
    for h in range(QUERY_HEADS):
        span = slice(h * HEAD_SIZE, (h + 1) * HEAD_SIZE)
        turned = turn(query_ref[:, span].astype(F32), cosine, sine)
        query_out[h * tokens : (h + 1) * tokens, :] = turned.astype(BF16)
    attend_kernel(
        None, sets, [(tokens, False)], tile, False, offset_ref, length_ref, query_out, key_buf, value_buf, state_out, mixed_out
    )


def state_shapes(block):
    return [
        jax.ShapeDtypeStruct((KEY_HEADS, 8, block), F32),
        jax.ShapeDtypeStruct((KEY_HEADS, HEAD_SIZE, block), F32),
    ]


def prepare(offset, length, cont_query, own_rows, sets, rows):
    tokens = cont_query.shape[0]
    block = GROUP * tokens
    table = jax.ShapeDtypeStruct((rows, HEAD_SIZE), F32)
    return pl.pallas_call(
        functools.partial(prepare_kernel, sets, block),
        in_specs=[SMEM, SMEM, VMEM, VMEM, VMEM],
        out_shape=[table, table, jax.ShapeDtypeStruct((QUERY_HEADS * tokens, HEAD_SIZE), BF16)] + state_shapes(block),
        out_specs=[VMEM] * 5,
        scratch_shapes=[pltpu.VMEM((tokens, KEY_COLUMNS), BF16)] * 2,
        compiler_params=pltpu.CompilerParams(vmem_limit_bytes=16 << 20),
        name="prepare",
    )(offset, length, frequencies(), cont_query, own_rows)


def attend_kernel(plan, sets, spans, tile, last, offset_ref, length_ref, query_ref, *rest):
    own = plan is None
    if own:
        key_ref, own_ref, state_out, mixed_out = rest
    else:
        operands = 1 + max(operand for stretch in plan for operand, _ in stretch.values())
        pieces, rest = rest[:operands], rest[operands:]
        if last:
            state_ref, mixed_ref, block_ref, final_ref, block_out, out_ref, sems = rest
        else:
            state_ref, mixed_ref, state_out, mixed_out = rest
    my_set = lax.axis_index("set")
    block = query_ref.shape[0] // KEY_HEADS
    tokens = block // GROUP
    offset, length = offset_ref[0], length_ref[0]
    total_rows = sum(rows for rows, _ in spans)
    bias = None
    if own:
        place = lax.broadcasted_iota(jnp.int32, (tokens, tokens), 0)
        token = lax.broadcasted_iota(jnp.int32, (tokens, tokens), 1)
        bias = jnp.concatenate([jnp.where(place <= token, 0.0, NEGATIVE_LARGE)] * (tile // tokens), axis=1)
    elif any(prompt for _, prompt in spans):
        parts = []
        for rows, prompt in spans:
            place = lax.broadcasted_iota(jnp.int32, (rows, HEAD_SIZE), 0)
            parts.append(jnp.where(place < offset, 0.0, NEGATIVE_LARGE) if prompt else jnp.zeros(place.shape, F32))
        bias = jnp.concatenate([jnp.concatenate(parts, axis=0)] * (tile // HEAD_SIZE), axis=1)
    keep = lax.broadcasted_iota(jnp.int32, (tokens, HEAD_SIZE), 0) < length
    units = [(g, start) for g in range(KEY_HEADS) for start in range(0, block, tile)]
    held, scored, weighed, mixtures, copies = {}, {}, {}, {}, []
    if last:
        block_copy = pltpu.make_async_copy(block_ref, block_out, sems.at[FLUSHES])
        block_copy.start()

    def rows_of(column):
        if column not in held:
            if own:
                ref = key_ref if column < KEY_COLUMNS else own_ref
                held[column] = ref[:, column % KEY_COLUMNS : column % KEY_COLUMNS + HEAD_SIZE]
                return held[column]
            width = pieces[0].shape[1]
            lanes = slice(column % width, column % width + HEAD_SIZE)
            parts = []
            for stretch, (rows, _) in zip(plan, spans):
                chosen = None
                for step, (operand, first) in stretch.items():
                    part = pieces[operand][first : first + rows, lanes]
                    here = source(my_set, step, sets) == column // width
                    chosen = part if chosen is None else jnp.where(here, part, chosen)
                parts.append(chosen)
            held[column] = jnp.concatenate(parts, axis=0)
        return held[column]

    def score(unit):
        g, start = unit
        query = query_ref[g * block + start : g * block + start + tile, :]
        key = rows_of(g * HEAD_SIZE)
        scores = lax.dot_general(key, query, (((1,), (1,)), ((), ())), preferred_element_type=F32)
        scored[unit] = scores if bias is None else scores + bias

    def weigh(unit):
        g, start = unit
        scores = scored.pop(unit)
        top, shrink = jnp.max(scores, axis=0, keepdims=True), None
        if not own:
            old = state_ref[g, 0:1, start : start + tile]
            top = jnp.maximum(old, top)
            shrink = jnp.exp2(old - top)
        weights = jnp.exp2(scores - top)
        total = jnp.sum(weights, axis=0, keepdims=True)
        if not own:
            total = total + state_ref[g, 1:2, start : start + tile] * shrink
        weighed[unit] = top, shrink, total
        mixtures[unit] = lax.dot_general(
            rows_of(KEY_COLUMNS + g * HEAD_SIZE),
            weights.astype(BF16),
            (((0,), (0,)), ((), ())),
            preferred_element_type=F32,
        )

    def finish(unit):
        g, start = unit
        top, shrink, total = weighed.pop(unit)
        mixed = mixtures.pop(unit)
        if not own:
            mixed = mixed + mixed_ref[g, :, start : start + tile] * shrink
        if last:
            mixed = (mixed * (1.0 / total)).astype(BF16).T
            for j in range(tile // tokens):
                column = (g * GROUP + start // tokens + j) * HEAD_SIZE
                piece = mixed[j * tokens : (j + 1) * tokens, :]
                out_ref[:, column : column + HEAD_SIZE] = jnp.where(keep, piece, jnp.zeros_like(piece))
        else:
            state_out[g, 0:1, start : start + tile] = top
            state_out[g, 1:2, start : start + tile] = total
            mixed_out[g, :, start : start + tile] = mixed

    flush = len(units) // FLUSHES
    for i in range(len(units) + 2):
        if i < len(units):
            score(units[i])
        if 0 <= i - 1 < len(units):
            weigh(units[i - 1])
        if 0 <= i - 2 < len(units):
            finish(units[i - 2])
            if last and (i - 1) % flush == 0:
                wide = out_ref.shape[1] // FLUSHES
                part = pl.ds(len(copies) * wide, wide)
                copies.append(pltpu.make_async_copy(out_ref.at[:, part], final_ref.at[:, part], sems.at[len(copies)]))
                copies[-1].start()
    for copy in copies:
        copy.wait()
    if last:
        block_copy.wait()


def attend(offset, length, query, sets, plan, spans, pieces, state, last=None):
    block = query.shape[0] // KEY_HEADS
    tokens = block // GROUP
    total_rows = sum(rows for rows, _ in spans)
    tile = block if total_rows % 128 else block // 2
    operands = [query] + list(pieces) + list(state) + ([] if last is None else [last])
    out_shape, scratch = state_shapes(block), []
    if last is not None:
        wide = (tokens, QUERY_HEADS * HEAD_SIZE)
        out_shape = [jax.ShapeDtypeStruct(wide, BF16), jax.ShapeDtypeStruct(last.shape, BF16)]
        scratch = [pltpu.VMEM(wide, BF16), pltpu.SemaphoreType.DMA((FLUSHES + 1,))]
    return pl.pallas_call(
        functools.partial(attend_kernel, plan, sets, spans, tile, last is not None),
        in_specs=[SMEM, SMEM] + [VMEM] * len(operands),
        out_shape=out_shape,
        out_specs=[VMEM, VMEM] if last is None else [HBM, HBM],
        scratch_shapes=scratch,
        compiler_params=pltpu.CompilerParams(vmem_limit_bytes=16 << 20),
        name="attend_more" if last is None else "attend_last",
    )(offset, length, *operands)


def on_device(
    span_hidden,
    norm_gain,
    key_value_weight,
    prompt_key_value,
    span_offset,
    cont_query,
    continuation_key_value,
    cont_lengths,
):
    sets, count = lax.axis_size("set"), lax.axis_size("seq")
    rows = span_hidden.shape[0] // count
    low = 2 if sets % 2 == 0 else 1

    own, square, mine, *sends = project(span_hidden, norm_gain, key_value_weight, prompt_key_value, count)
    order = list(range(count - 1, 0, -1))
    sums = order[1:] + order[:1]
    got = [lax.ppermute(sends[k - 1], "seq", [(i, (i + k) % count) for i in range(count)]) for k in sums]

    cosine, sine, query, *state = prepare(
        span_offset, cont_lengths, cont_query[0], continuation_key_value[0], sets, rows
    )
    block, prompt = combine(own, square, mine, cosine, sine, got, sums)

    far = list(range(low, sets, low))
    steps = [0] + far
    half = max(1, (count - 1) // 2)
    beside = [exchange(block, "set", step) for step in far]
    across = [exchange(block, "seq", k) for k in order[:half]]
    both = jnp.concatenate([block] + beside, axis=0)
    together = [exchange(both, "seq", k) for k in reversed(order[half:])]
    prompts = [prompt] + [exchange(prompt, "set", step) for step in far]
    stretches = [[block] + beside]
    for arrived in across:
        stretches.append([arrived] + [exchange(arrived, "set", step) for step in far])
    stretches += [[arrived] for arrived in together]

    def share(values, spans):
        plan, pieces = [], []
        for lines, (size, _) in zip(values, spans):
            whole = len(lines) == 1
            plan.append({step: (len(pieces) + (0 if whole else n), n * size if whole else 0) for n, step in enumerate(steps)})
            pieces += lines
        if low == 2:
            other = exchange(jnp.concatenate([line for lines in values for line in lines], axis=0), "set", 1)
            first = 0
            for stretch, (size, _) in zip(plan, spans):
                for step in steps:
                    stretch[step ^ 1] = (len(pieces), first)
                    first += size
            pieces.append(other)
        return dict(plan=plan, pieces=pieces, spans=spans)

    ends = span_offset, cont_lengths
    near = share([stretches[0], prompts], [(rows, False), (prompt.shape[0], True)])
    state = attend(*ends, query, sets, state=state, **near)
    rest = stretches[1:]
    attended, block = attend(*ends, query, sets, state=state, last=block, **share(rest, [(rows, False)] * len(rest)))
    return block, attended[None]


def solution(mesh):
    placed = (
        P("parts", "seq"),
        P("seq"),
        P("seq", "set"),
        P(("parts", "seq"), None),
        P("parts"),
        P(("parts", "set", "seq"), None, None),
        P(("parts", "set", "seq"), None, None),
        P(("parts", "set", "seq")),
    )
    return jax.shard_map(
        on_device,
        mesh=mesh,
        in_specs=placed,
        out_specs=(P(("parts", "seq"), "set"), P(("parts", "set", "seq"), None, None)),
        check_vma=False,
    )
```

```python
import functools
import math

import jax
import jax.numpy as jnp
import numpy as np
from jax import lax
from jax.experimental import pallas as pl
from jax.experimental.pallas import tpu as pltpu
from jax.sharding import PartitionSpec as P

MODEL_WIDTH = 8192
QUERY_HEADS = 64
KEY_HEADS = 8
HEAD_SIZE = 128
SPAN_LENGTH = 256
EPS = 1e-05
NEGATIVE_LARGE = -1e30
GROUP = QUERY_HEADS // KEY_HEADS
KEY_COLUMNS = KEY_HEADS * HEAD_SIZE
BF16 = jnp.bfloat16
F32 = jnp.float32
FLUSHES = 8
SMEM = pl.BlockSpec(memory_space=pltpu.SMEM)
VMEM = pl.BlockSpec(memory_space=pltpu.VMEM)
HBM = pl.BlockSpec(memory_space=pltpu.HBM)


def peer(index, step, count):
    if count & (count - 1) == 0:
        return index ^ step
    return (index + step) % count


def source(index, step, count):
    if count & (count - 1) == 0:
        return index ^ step
    return (index + count - step) % count


def exchange(value, axis, step):
    count = lax.axis_size(axis)
    return lax.ppermute(value, axis, [(i, peer(i, step, count)) for i in range(count)])


def frequencies():
    base = 500000.0 ** (-(np.arange(HEAD_SIZE // 2) * 2.0) / HEAD_SIZE)
    wave = 2.0 * math.pi / base
    smooth = (8192.0 / wave - 1.0) / 3.0
    blended = (1.0 - smooth) * base / 8.0 + smooth * base
    rescaled = np.where(wave < 2048.0, base, np.where(wave > 8192.0, base / 8.0, blended))
    return jnp.asarray(np.tile(rescaled, 2)[None], F32)


def turn(value, cosine, sine):
    return value * cosine + pltpu.roll(value, HEAD_SIZE // 2, 1) * sine


def diagonal(rows):
    shape = (rows, HEAD_SIZE)
    return lax.broadcasted_iota(jnp.int32, shape, 0) == lax.broadcasted_iota(jnp.int32, shape, 1)


def project_kernel(count, rows, heads, chunks, hidden_ref, gain_ref, weight_ref, prompt_ref, *rest):
    own_ref, square_ref, mine_ref = rest[:3]
    sends = rest[3 : 2 + count]
    hidden_buf, gain_buf, weight_buf, total, squares, sems = rest[2 + count :]
    depth = hidden_ref.shape[1]
    size = depth // chunks
    width = weight_ref.shape[1]
    cached = prompt_ref.shape[0]
    gain_copy = pltpu.make_async_copy(gain_ref, gain_buf, sems.at[2 * chunks])
    gain_copy.start()
    columns = pl.ds(pl.multiple_of(lax.axis_index("set") * width, HEAD_SIZE), width)
    prompt_copy = pltpu.make_async_copy(prompt_ref.at[:, columns], mine_ref, sems.at[2 * chunks + 1])
    copies = []
    for c in range(chunks):
        part = pl.ds(c * size, size)
        copies.append(
            (
                pltpu.make_async_copy(hidden_ref.at[:, part], hidden_buf.at[:, part], sems.at[2 * c]),
                pltpu.make_async_copy(weight_ref.at[part, :], weight_buf.at[part, :], sems.at[2 * c + 1]),
            )
        )
        copies[-1][0].start()
        copies[-1][1].start()
    prompt_copy.start()
    gain_copy.wait()
    for c in range(chunks):
        copies[c][0].wait()
        folded, scaled = None, []
        for lane in range(c * size, (c + 1) * size, HEAD_SIZE):
            hidden = hidden_buf[:, lane : lane + HEAD_SIZE].astype(F32)
            tile = lane // HEAD_SIZE
            scaled.append((hidden * gain_buf[tile : tile + 1, :].astype(F32)).astype(BF16))
            square = hidden * hidden
            folded = square if folded is None else folded + square
        copies[c][1].wait()
        part = jnp.dot(
            jnp.concatenate(scaled, axis=1),
            weight_buf[c * size : (c + 1) * size, :],
            preferred_element_type=F32,
        )
        if c == 0:
            total[...] = part
            squares[...] = folded
        else:
            total[...] += part
            squares[...] += folded
    prompt_copy.wait()
    me = lax.axis_index("seq")
    for k in range(count):
        to = pl.ds(pl.multiple_of(lax.rem(me + k, count) * rows, rows), rows)
        column = jnp.sum(squares[to, :], axis=1, keepdims=True)
        if k == 0:
            square_ref[...] = jnp.broadcast_to(column, (rows, HEAD_SIZE))
            out = own_ref
        else:
            out = sends[k - 1]
            line = jnp.sum(jnp.where(diagonal(rows), column, 0.0), axis=0, keepdims=True)
            high = line.astype(BF16).astype(F32)
            low = line - high
            which = lax.broadcasted_iota(jnp.int32, (16, HEAD_SIZE), 0)
            tail = jnp.where(which == 0, high, jnp.where(which == 1, low, 0.0))
            out[heads * rows : heads * rows + 16, :] = tail.astype(BF16)
            for h in range(heads):
                first = heads * rows + 16 + h * cached
                out[first : first + cached, :] = mine_ref[:, h * HEAD_SIZE : (h + 1) * HEAD_SIZE]
        for h in range(heads):
            piece = total[to, h * HEAD_SIZE : (h + 1) * HEAD_SIZE]
            out[h * rows : (h + 1) * rows, :] = piece.astype(out.dtype)


def project(span_hidden, norm_gain, key_value_weight, prompt_rows, count):
    length, depth = span_hidden.shape
    width = key_value_weight.shape[1]
    rows, heads = length // count, width // HEAD_SIZE
    cached = prompt_rows.shape[0]
    chunks = 4 if depth % (4 * HEAD_SIZE) == 0 else 1
    gain = norm_gain.reshape(-1, HEAD_SIZE)
    outs = [
        jax.ShapeDtypeStruct((heads * rows, HEAD_SIZE), F32),
        jax.ShapeDtypeStruct((rows, HEAD_SIZE), F32),
        jax.ShapeDtypeStruct((cached, width), BF16),
    ] + [jax.ShapeDtypeStruct((heads * (rows + cached) + 16, HEAD_SIZE), BF16)] * (count - 1)
    stay = [pltpu.with_memory_space_constraint(x, pltpu.HBM) for x in (span_hidden, gain, key_value_weight, prompt_rows)]
    return pl.pallas_call(
        functools.partial(project_kernel, count, rows, heads, chunks),
        in_specs=[HBM, HBM, HBM, HBM],
        out_shape=outs,
        out_specs=[VMEM] * len(outs),
        scratch_shapes=[
            pltpu.VMEM((length, depth), BF16),
            pltpu.VMEM(gain.shape, BF16),
            pltpu.VMEM((depth, width), BF16),
            pltpu.VMEM((length, width), F32),
            pltpu.VMEM((length, HEAD_SIZE), F32),
            pltpu.SemaphoreType.DMA((2 * chunks + 2,)),
        ],
        compiler_params=pltpu.CompilerParams(vmem_limit_bytes=16 << 20),
        cost_estimate=pl.CostEstimate(
            flops=2 * length * depth * width, bytes_accessed=2 * depth * (length + width), transcendentals=0
        ),
        name="project",
    )(*stay)


def combine_kernel(rows, heads, order, own_ref, square_ref, mine_ref, cosine_ref, sine_ref, *rest):
    got, (send_ref, prompt_ref) = rest[:-2], rest[-2:]
    cached = mine_ref.shape[0]
    count = 1 + len(got)
    me, first = lax.axis_index("seq"), lax.axis_index("set") * heads

    def prompt_rows(k):
        return pl.ds(pl.multiple_of(lax.rem(me + count - k, count) * cached, 16), cached)

    line = jnp.zeros((1, HEAD_SIZE), F32)
    for ref in got:
        tail = ref[heads * rows : heads * rows + 16, :].astype(F32)
        line = line + tail[0:1, :] + tail[1:2, :]
    column = jnp.sum(jnp.where(diagonal(rows), line, 0.0), axis=1, keepdims=True)
    scale = lax.rsqrt((square_ref[...] + column) / MODEL_WIDTH + EPS)
    cosine, sine = cosine_ref[...], sine_ref[...]
    for h in range(heads):
        span = slice(h * rows, (h + 1) * rows)
        lanes = slice(h * HEAD_SIZE, (h + 1) * HEAD_SIZE)
        value = own_ref[span, :]
        for ref in got:
            value = value + ref[span, :].astype(F32)
        value = value * scale
        out = jnp.where(first + h < KEY_HEADS, turn(value, cosine, sine), value).astype(BF16)
        send_ref[:, lanes] = out
        for i, ref in enumerate(got):
            start = heads * rows + 16 + h * cached
            prompt_ref[prompt_rows(order[i]), lanes] = ref[start : start + cached, :]
    prompt_ref[prompt_rows(0), :] = mine_ref[...]


def combine(own, square, mine, cosine, sine, got, order):
    rows = square.shape[0]
    heads = own.shape[0] // rows
    block = pltpu.VMEM((rows, heads * HEAD_SIZE), BF16)
    prompt = jax.ShapeDtypeStruct(((1 + len(got)) * mine.shape[0], heads * HEAD_SIZE), BF16)
    return pl.pallas_call(
        functools.partial(combine_kernel, rows, heads, order),
        in_specs=[VMEM] * (5 + len(got)),
        out_shape=[block, prompt],
        out_specs=[VMEM, VMEM],
        compiler_params=pltpu.CompilerParams(vmem_limit_bytes=4 << 20),
        name="combine",
    )(own, square, mine, cosine, sine, *got)


def prepare_kernel(
    sets, tile, offset_ref, length_ref, frequency_ref, query_ref, own_ref, cosine_out, sine_out, query_out, state_out, mixed_out, key_buf, value_buf
):
    def table(rows, first):
        place = lax.broadcasted_iota(jnp.int32, (rows, HEAD_SIZE), 0) + first
        angles = place.astype(F32) * frequency_ref[...]
        front = lax.broadcasted_iota(jnp.int32, (rows, HEAD_SIZE), 1) < HEAD_SIZE // 2
        return jnp.cos(angles), jnp.where(front, -1.0, 1.0) * jnp.sin(angles)

    offset = offset_ref[0]
    rows, tokens = cosine_out.shape[0], query_ref.shape[0]
    cosine_out[...], sine_out[...] = table(rows, offset + lax.axis_index("seq") * rows)
    cosine, sine = table(tokens, offset + SPAN_LENGTH)
    for h in range(KEY_HEADS):
        span = slice(h * HEAD_SIZE, (h + 1) * HEAD_SIZE)
        key_buf[:, span] = turn(own_ref[:, span].astype(F32), cosine, sine).astype(BF16)
    value_buf[...] = own_ref[:, KEY_COLUMNS:]
    factor = HEAD_SIZE**-0.5 * math.log2(math.e)
    cosine, sine = cosine * factor, sine * factor
    for h in range(QUERY_HEADS):
        span = slice(h * HEAD_SIZE, (h + 1) * HEAD_SIZE)
        turned = turn(query_ref[:, span].astype(F32), cosine, sine)
        query_out[h * tokens : (h + 1) * tokens, :] = turned.astype(BF16)
    attend_kernel(
        None, sets, [(tokens, False)], tile, False, offset_ref, length_ref, query_out, key_buf, value_buf, state_out, mixed_out
    )


def state_shapes(block):
    return [
        jax.ShapeDtypeStruct((KEY_HEADS, 8, block), F32),
        jax.ShapeDtypeStruct((KEY_HEADS, HEAD_SIZE, block), F32),
    ]


def prepare(offset, length, cont_query, own_rows, sets, rows):
    tokens = cont_query.shape[0]
    block = GROUP * tokens
    table = jax.ShapeDtypeStruct((rows, HEAD_SIZE), F32)
    return pl.pallas_call(
        functools.partial(prepare_kernel, sets, block),
        in_specs=[SMEM, SMEM, VMEM, VMEM, VMEM],
        out_shape=[table, table, jax.ShapeDtypeStruct((QUERY_HEADS * tokens, HEAD_SIZE), BF16)] + state_shapes(block),
        out_specs=[VMEM] * 5,
        scratch_shapes=[pltpu.VMEM((tokens, KEY_COLUMNS), BF16)] * 2,
        compiler_params=pltpu.CompilerParams(vmem_limit_bytes=16 << 20),
        name="prepare",
    )(offset, length, frequencies(), cont_query, own_rows)


def attend_kernel(plan, sets, spans, tile, last, offset_ref, length_ref, query_ref, *rest):
    own = plan is None
    if own:
        key_ref, own_ref, state_out, mixed_out = rest
    else:
        operands = 1 + max(operand for stretch in plan for operand, _ in stretch.values())
        pieces, rest = rest[:operands], rest[operands:]
        if last:
            state_ref, mixed_ref, block_ref, final_ref, block_out, out_ref, sems = rest
        else:
            state_ref, mixed_ref, state_out, mixed_out = rest
    my_set = lax.axis_index("set")
    block = query_ref.shape[0] // KEY_HEADS
    tokens = block // GROUP
    offset, length = offset_ref[0], length_ref[0]
    total_rows = sum(rows for rows, _ in spans)
    bias = None
    if own:
        place = lax.broadcasted_iota(jnp.int32, (tokens, tokens), 0)
        token = lax.broadcasted_iota(jnp.int32, (tokens, tokens), 1)
        bias = jnp.concatenate([jnp.where(place <= token, 0.0, NEGATIVE_LARGE)] * (tile // tokens), axis=1)
    elif any(prompt for _, prompt in spans):
        parts = []
        for rows, prompt in spans:
            place = lax.broadcasted_iota(jnp.int32, (rows, HEAD_SIZE), 0)
            parts.append(jnp.where(place < offset, 0.0, NEGATIVE_LARGE) if prompt else jnp.zeros(place.shape, F32))
        bias = jnp.concatenate([jnp.concatenate(parts, axis=0)] * (tile // HEAD_SIZE), axis=1)
    keep = lax.broadcasted_iota(jnp.int32, (tokens, HEAD_SIZE), 0) < length
    units = [(g, start) for g in range(KEY_HEADS) for start in range(0, block, tile)]
    held, scored, weighed, mixtures, copies = {}, {}, {}, {}, []
    if last:
        block_copy = pltpu.make_async_copy(block_ref, block_out, sems.at[FLUSHES])
        block_copy.start()

    def rows_of(column):
        if column not in held:
            if own:
                ref = key_ref if column < KEY_COLUMNS else own_ref
                held[column] = ref[:, column % KEY_COLUMNS : column % KEY_COLUMNS + HEAD_SIZE]
                return held[column]
            width = pieces[0].shape[1]
            lanes = slice(column % width, column % width + HEAD_SIZE)
            parts = []
            for stretch, (rows, _) in zip(plan, spans):
                chosen = None
                for step, (operand, first) in stretch.items():
                    part = pieces[operand][first : first + rows, lanes]
                    here = source(my_set, step, sets) == column // width
                    chosen = part if chosen is None else jnp.where(here, part, chosen)
                parts.append(chosen)
            held[column] = jnp.concatenate(parts, axis=0)
        return held[column]

    def score(unit):
        g, start = unit
        query = query_ref[g * block + start : g * block + start + tile, :]
        key = rows_of(g * HEAD_SIZE)
        scores = lax.dot_general(key, query, (((1,), (1,)), ((), ())), preferred_element_type=F32)
        scored[unit] = scores if bias is None else scores + bias

    def weigh(unit):
        g, start = unit
        scores = scored.pop(unit)
        top, shrink = jnp.max(scores, axis=0, keepdims=True), None
        if not own:
            old = state_ref[g, 0:1, start : start + tile]
            top = jnp.maximum(old, top)
            shrink = jnp.exp2(old - top)
        weights = jnp.exp2(scores - top)
        total = jnp.sum(weights, axis=0, keepdims=True)
        if not own:
            total = total + state_ref[g, 1:2, start : start + tile] * shrink
        weighed[unit] = top, shrink, total
        mixtures[unit] = lax.dot_general(
            rows_of(KEY_COLUMNS + g * HEAD_SIZE),
            weights.astype(BF16),
            (((0,), (0,)), ((), ())),
            preferred_element_type=F32,
        )

    def finish(unit):
        g, start = unit
        top, shrink, total = weighed.pop(unit)
        mixed = mixtures.pop(unit)
        if not own:
            mixed = mixed + mixed_ref[g, :, start : start + tile] * shrink
        if last:
            mixed = (mixed * (1.0 / total)).astype(BF16).T
            for j in range(tile // tokens):
                column = (g * GROUP + start // tokens + j) * HEAD_SIZE
                piece = mixed[j * tokens : (j + 1) * tokens, :]
                out_ref[:, column : column + HEAD_SIZE] = jnp.where(keep, piece, jnp.zeros_like(piece))
        else:
            state_out[g, 0:1, start : start + tile] = top
            state_out[g, 1:2, start : start + tile] = total
            mixed_out[g, :, start : start + tile] = mixed

    flush = len(units) // FLUSHES
    for i in range(len(units) + 2):
        if i < len(units):
            score(units[i])
        if 0 <= i - 1 < len(units):
            weigh(units[i - 1])
        if 0 <= i - 2 < len(units):
            finish(units[i - 2])
            if last and (i - 1) % flush == 0:
                wide = out_ref.shape[1] // FLUSHES
                part = pl.ds(len(copies) * wide, wide)
                copies.append(pltpu.make_async_copy(out_ref.at[:, part], final_ref.at[:, part], sems.at[len(copies)]))
                copies[-1].start()
    for copy in copies:
        copy.wait()
    if last:
        block_copy.wait()


def attend(offset, length, query, sets, plan, spans, pieces, state, last=None):
    block = query.shape[0] // KEY_HEADS
    tokens = block // GROUP
    total_rows = sum(rows for rows, _ in spans)
    tile = block if total_rows % 128 else block // 2
    operands = [query] + list(pieces) + list(state) + ([] if last is None else [last])
    out_shape, scratch = state_shapes(block), []
    if last is not None:
        wide = (tokens, QUERY_HEADS * HEAD_SIZE)
        out_shape = [jax.ShapeDtypeStruct(wide, BF16), jax.ShapeDtypeStruct(last.shape, BF16)]
        scratch = [pltpu.VMEM(wide, BF16), pltpu.SemaphoreType.DMA((FLUSHES + 1,))]
    return pl.pallas_call(
        functools.partial(attend_kernel, plan, sets, spans, tile, last is not None),
        in_specs=[SMEM, SMEM] + [VMEM] * len(operands),
        out_shape=out_shape,
        out_specs=[VMEM, VMEM] if last is None else [HBM, HBM],
        scratch_shapes=scratch,
        compiler_params=pltpu.CompilerParams(vmem_limit_bytes=16 << 20),
        name="attend_more" if last is None else "attend_last",
    )(offset, length, *operands)


def on_device(
    span_hidden,
    norm_gain,
    key_value_weight,
    prompt_key_value,
    span_offset,
    cont_query,
    continuation_key_value,
    cont_lengths,
):
    sets, count = lax.axis_size("set"), lax.axis_size("seq")
    rows = span_hidden.shape[0] // count
    low = 2 if sets % 2 == 0 else 1

    own, square, mine, *sends = project(span_hidden, norm_gain, key_value_weight, prompt_key_value, count)
    order = list(range(count - 1, 0, -1))
    sums = [order[1], order[0]] + order[2:]
    got = [lax.ppermute(sends[k - 1], "seq", [(i, (i + k) % count) for i in range(count)]) for k in sums]

    cosine, sine, query, *state = prepare(
        span_offset, cont_lengths, cont_query[0], continuation_key_value[0], sets, rows
    )
    block, prompt = combine(own, square, mine, cosine, sine, got, sums)

    far = list(range(low, sets, low))
    steps = [0] + far
    half = max(1, (count - 1) // 2)
    beside = [exchange(block, "set", step) for step in far]
    across = [exchange(block, "seq", k) for k in order[:half]]
    both = jnp.concatenate([block] + beside, axis=0)
    together = [exchange(both, "seq", k) for k in reversed(order[half:])]
    prompts = [prompt] + [exchange(prompt, "set", step) for step in far]
    stretches = [[block] + beside]
    for arrived in across:
        stretches.append([arrived] + [exchange(arrived, "set", step) for step in far])
    stretches += [[arrived] for arrived in together]

    def share(values, spans):
        plan, pieces = [], []
        for lines, (size, _) in zip(values, spans):
            whole = len(lines) == 1
            plan.append({step: (len(pieces) + (0 if whole else n), n * size if whole else 0) for n, step in enumerate(steps)})
            pieces += lines
        if low == 2:
            other = exchange(jnp.concatenate([line for lines in values for line in lines], axis=0), "set", 1)
            first = 0
            for stretch, (size, _) in zip(plan, spans):
                for step in steps:
                    stretch[step ^ 1] = (len(pieces), first)
                    first += size
            pieces.append(other)
        return dict(plan=plan, pieces=pieces, spans=spans)

    ends = span_offset, cont_lengths
    near = share([stretches[0], prompts], [(rows, False), (prompt.shape[0], True)])
    state = attend(*ends, query, sets, state=state, **near)
    rest = stretches[1:]
    attended, block = attend(*ends, query, sets, state=state, last=block, **share(rest, [(rows, False)] * len(rest)))
    return block, attended[None]


def solution(mesh):
    placed = (
        P("parts", "seq"),
        P("seq"),
        P("seq", "set"),
        P(("parts", "seq"), None),
        P("parts"),
        P(("parts", "set", "seq"), None, None),
        P(("parts", "set", "seq"), None, None),
        P(("parts", "set", "seq")),
    )
    return jax.shard_map(
        on_device,
        mesh=mesh,
        in_specs=placed,
        out_specs=(P(("parts", "seq"), "set"), P(("parts", "set", "seq"), None, None)),
        check_vma=False,
    )
```
